32 devices in a mesh: edge: 16 (over z, y, x), rep: 2 (over core).
Axes of the slice: x: 2, y: 2, z: 4, core: 2. Of those that a mesh axis runs over, the one named last changes fastest.
Arguments:
- node_feat: float32 [2, 8192, 14], P('rep', 'edge'), may hold values from -6 to 6
- node_types: int32 [2, 8192], P('rep', 'edge'), may hold values from 0 to 8
- boundary: int32 [2, 8192], P('rep', 'edge'), may hold values from 0 to 1
- target: float32 [2, 8192, 2], P('rep', 'edge'), may hold values from -6 to 6
- edge_feat: float32 [2, 131072, 3], P('rep', 'edge'), may hold values from -6 to 6
- senders: int32 [2, 131072], P('rep', 'edge'), may hold values from 0 to 8191, as said below
- receivers: int32 [2, 131072], P('rep', 'edge'), may hold values from 0 to 8191, as said below
- edge_counts: int32 [2, 16], P('rep', 'edge'), may hold values from 4096 to 8192, as said below
- mats: float32 [24, 128, 128], replicated, may hold values from -0.5 to 0.5
- vecs: float32 [60, 128], replicated
- mats_momentum: float32 [24, 128, 128], replicated, may hold values from -0.25 to 0.25
- vecs_momentum: float32 [60, 128], replicated, may hold values from -0.25 to 0.25
- factors: float32 [24, 128, 8], replicated, may hold values from -6 to 6
- errors: float32 [2, 24, 128, 128], P('rep'), may hold values from -0.25 to 0.25
Outputs:
- loss_sum: float32 [], replicated
- loss_count: float32 [], replicated
- stats: float32 [4, 2], replicated
- new_mats: float32 [24, 128, 128], replicated
- new_mats_momentum: float32 [24, 128, 128], replicated
- new_factors: float32 [24, 128, 8], replicated
- new_errors: float32 [2, 24, 128, 128], P('rep')
- new_vecs: float32 [60, 128], replicated
- new_vecs_momentum: float32 [60, 128], replicated
The draws below stay inside these ranges and needn't reach their ends.
Inputs may be any that keep to these rules, and one draw needn't show every extreme that they name: `edge_counts`: multiples of 128; the live slots of a device come first; in each scene some device has all 8192 slots live. `receivers`: every edge slot of device d of a scene has its receiver among the particles d * 512 to (d + 1) * 512 - 1. `senders`: each sender lies within 512 particles of its edge's receiver.
All inputs are finite; a program needn't handle non-finite values.
Results may differ from the reference program's by a relative error of at most 0.0003.
Values sent between devices are 32-bit elements; how exact they have to be, the bound alone decides.
A program may use at most 256 MiB of HBM per device.

```python
from functools import partial
import jax
import jax.numpy as jnp
from jax import lax

LAT = 128
NFEAT = 14
NTYPES = 9
EFEAT = 3
STEPS = 2
RANK = 8
NODE_DEV = 512
EDGE_BLOCKS = 64
EDGE_CAP = 8192
NODES = 8192
EDGES = 131072
REPS = 2
MATS = 24
VROWS = 60


def edge_pairs(key):
    owner = jnp.arange(EDGES)[None, :] // EDGE_CAP
    local = jax.random.randint(jax.random.fold_in(key, 11), (REPS, EDGES), 0, NODE_DEV)
    recv = owner * NODE_DEV + local
    offset = jax.random.randint(jax.random.fold_in(key, 12), (REPS, EDGES), -NODE_DEV, NODE_DEV + 1)
    send = jnp.clip(recv + offset, 0, NODES - 1)
    return (send.astype(jnp.int32), recv.astype(jnp.int32))


def draw_senders(key, part):
    send, recv = edge_pairs(key)
    return send


def draw_receivers(key, part):
    send, recv = edge_pairs(key)
    return recv


def draw_edge_counts(key, part):
    key = jax.random.fold_in(key, 1)
    devices = EDGES // EDGE_CAP
    blocks = jax.random.randint(jax.random.fold_in(key, 5), (REPS, devices), max(EDGE_BLOCKS // 2, 1), EDGE_BLOCKS + 1)
    full = jax.random.randint(jax.random.fold_in(key, 6), (REPS, 1), 0, devices)
    blocks = jnp.where(jnp.arange(devices)[None, :] == full, EDGE_BLOCKS, blocks)
    return (blocks * 128).astype(jnp.int32)


def draw_boundary(key, part):
    key = jax.random.fold_in(key, 2)
    drawn = jax.random.randint(key, (REPS, NODES), 0, 1000)
    limit = 700 - 600 * jnp.arange(NODES) // NODES
    return (drawn < limit[None, :]).astype(jnp.int32)


def draw_vecs(key, part):
    key = jax.random.fold_in(key, 3)
    noise = jax.random.normal(key, (VROWS, LAT), jnp.float32)
    row = jnp.arange(VROWS)[:, None]
    lead = NFEAT + NTYPES
    first = lead + EFEAT
    inside = (row >= first) & (row < VROWS - 4)
    gains = inside & ((row - first) % 5 == 3)
    scale = jnp.where(row < lead, lead ** (-0.5), jnp.where(row < first, EFEAT ** (-0.5), jnp.where(row < VROWS - 2, 0.3, LAT ** (-0.5))))
    scale = jnp.where(gains, 0.1, scale)
    return (jnp.where(gains, 1.0, 0.0) + scale * noise).astype(jnp.float32)


def place_ends(result, rng, low, top_value):
    place = [jax.random.randint(jax.random.fold_in(rng, axis), (), 0, length) for axis, length in enumerate(result.shape)]
    widest = result.shape.index(max(result.shape))
    neighbour = place[:widest] + [(place[widest] + 1) % result.shape[widest]] + place[widest + 1:]
    return result.at[tuple(place)].set(low).at[tuple(neighbour)].set(top_value)


def block_scale(key, dims, pieces, smallest, top_value):
    def one(dim, shards_of):
        steps = jax.random.uniform(jax.random.fold_in(jax.random.fold_in(key, 6), dim), (shards_of,), jnp.float32, smallest / len(pieces), top_value / len(pieces))
        return jnp.repeat(jnp.exp(steps), dims[dim] // shards_of).reshape((-1,) + (1,) * (len(dims) - dim - 1))

    level = one(*pieces[0])
    for cut in pieces[1:]:
        level = level * one(*cut)
    return level


def bell_draw(own_key, shape, deviation, reach, pieces=(), held_as=jnp.bfloat16):
    values = deviation * jax.random.normal(own_key, shape, jnp.float32)
    if pieces:
        values = values * block_scale(own_key, shape, pieces, -0.22, 0.18)
    return jnp.clip(values, -reach, reach).astype(held_as)


def setup_inputs(seed: int = 0) -> dict:
    key_of = jax.random.split(jax.random.key(seed), 15)
    return {
        "node_feat": bell_draw(key_of[0], (REPS, NODES, NFEAT), 1.0, 6.0, ((0, 2), (1, 16)), jnp.float32),
        "node_types": place_ends(jax.random.randint(key_of[1], (REPS, NODES), 0, NTYPES), jax.random.fold_in(key_of[1], 1), 0, NTYPES - 1).astype(jnp.int32),
        "boundary": draw_boundary(jax.random.fold_in(key_of[14], 71), 0),
        "target": bell_draw(key_of[3], (REPS, NODES, 2), 1.0, 6.0, ((0, 2), (1, 16)), jnp.float32),
        "edge_feat": bell_draw(key_of[4], (REPS, EDGES, EFEAT), 1.0, 6.0, ((0, 2), (1, 16)), jnp.float32),
        "senders": draw_senders(jax.random.fold_in(key_of[14], 71), 0),
        "receivers": draw_receivers(jax.random.fold_in(key_of[14], 71), 0),
        "edge_counts": draw_edge_counts(jax.random.fold_in(key_of[14], 71), 0),
        "mats": bell_draw(key_of[8], (MATS, LAT, LAT), LAT ** -0.5, 0.5, (), jnp.float32),
        "vecs": draw_vecs(jax.random.fold_in(key_of[14], 71), 0),
        "mats_momentum": bell_draw(key_of[10], (MATS, LAT, LAT), (2.0 / (NODES * REPS) ** 0.5), 0.25, (), jnp.float32),
        "vecs_momentum": bell_draw(key_of[11], (VROWS, LAT), (2.0 / (NODES * REPS) ** 0.5), 0.25, (), jnp.float32),
        "factors": bell_draw(key_of[12], (MATS, LAT, RANK), 1.0, 6.0, (), jnp.float32),
        "errors": bell_draw(key_of[13], (REPS, MATS, LAT, LAT), (2.0 / (NODES * REPS) ** 0.5), 0.25, ((0, 2),), jnp.float32),
    }


HIGH = lax.Precision.HIGHEST

@jax.custom_vjp
def low(v):
    return lax.optimization_barrier(v.astype(jnp.bfloat16)).astype(jnp.float32)

@jax.custom_vjp
def low_back(v):
    return v

def low_keep(v):
    return (low(v), None)

def low_pass(kept, grad):
    return (grad,)

def back_keep(v):
    return (v, None)

def back_low(kept, grad):
    return (low(grad),)
low.defvjp(low_keep, low_pass)
low_back.defvjp(back_keep, back_low)

def product(a, b):
    return jnp.dot(a, b, precision=HIGH)

def layer_norm(v, gain, offset):
    cent = v - lax.optimization_barrier(jnp.mean(v, -1, keepdims=True))
    var = lax.optimization_barrier(jnp.mean(cent * cent, -1, keepdims=True))
    return cent * lax.rsqrt(var + 1e-05) * gain + offset

def mlp_tail(first, mats, vecs, second, third, which):
    base = NFEAT + NTYPES + EFEAT + 5 * which
    hidden = jax.nn.silu(first + vecs[base])
    hidden = jax.nn.silu(product(hidden, mats[second]) + vecs[base + 1])
    hidden = product(hidden, mats[third]) + vecs[base + 2]
    return layer_norm(hidden, vecs[base + 3], vecs[base + 4])

def encode_nodes(mats, vecs, feat, types):
    onehot = (types[:, None] == jnp.arange(NTYPES)[None, :]).astype(jnp.float32)
    first = product(feat, vecs[:NFEAT]) + product(onehot, vecs[NFEAT:NFEAT + NTYPES])
    return mlp_tail(first, mats, vecs, 0, 1, 0)

def encode_edges(mats, vecs, efeat):
    lead = NFEAT + NTYPES
    return mlp_tail(product(efeat, vecs[lead:lead + EFEAT]), mats, vecs, 2, 3, 1)

def edge_update(step, mats, vecs, edge, sent, recvd):
    base = 6 + 9 * step
    first = product(edge, mats[base]) + product(sent, mats[base + 1]) + product(recvd, mats[base + 2])
    return mlp_tail(first, mats, vecs, base + 3, base + 4, 2 + 2 * step)

def node_update(step, mats, vecs, node, agg):
    base = 6 + 9 * step
    first = product(node, mats[base + 5]) + product(agg, mats[base + 6])
    return mlp_tail(first, mats, vecs, base + 7, base + 8, 3 + 2 * step)

def decode(mats, vecs, node):
    base = NFEAT + NTYPES + EFEAT + 5 * (2 + 2 * STEPS)
    hidden = jax.nn.silu(product(node, mats[4]) + vecs[base])
    hidden = jax.nn.silu(product(hidden, mats[5]) + vecs[base + 1])
    return product(hidden, vecs[base + 2:base + 4].T)

def scene_loss(mats, vecs, feat, types, efeat, send, recv, live, keep, goal):
    node = encode_nodes(mats, vecs, feat, types)
    edge = encode_edges(mats, vecs, efeat)
    for step in range(STEPS):
        message = jax.checkpoint(partial(edge_update, step))(mats, vecs, edge, node[send], node[recv]) * live
        agg = jax.ops.segment_sum(message, recv, num_segments=NODES)
        node = node + node_update(step, mats, vecs, node, agg)
        edge = edge + message
    diff = decode(mats, vecs, node) - goal
    return jnp.sum(diff * diff * keep)

def orthonormal(left):
    columns = []
    for col in range(left.shape[-1]):
        vector = left[:, :, col]
        for prior in columns:
            vector = vector - lax.optimization_barrier(jnp.sum(prior * vector, 1, keepdims=True)) * prior
        vector = vector * lax.rsqrt(lax.optimization_barrier(jnp.sum(vector * vector, 1, keepdims=True)) + 1e-12)
        columns.append(vector)
    return jnp.stack(columns, -1)

def reference(node_feat, node_types, boundary, target, edge_feat, senders, receivers, edge_counts, mats, vecs, mats_momentum, vecs_momentum, factors, errors):
    keep_all = (1 - boundary).astype(jnp.float32)[:, :, None]
    count = jnp.sum(keep_all)
    slots = jnp.arange(EDGES)
    loss_total = jnp.zeros((), jnp.float32)
    vec_grad = jnp.zeros_like(vecs)
    mat_grads = []
    for scene in range(REPS):
        live = (slots % EDGE_CAP < edge_counts[scene][slots // EDGE_CAP]).astype(jnp.float32)[:, None]
        fixed = (node_feat[scene], node_types[scene], edge_feat[scene], senders[scene], receivers[scene], live, keep_all[scene], target[scene])
        value, pull = jax.vjp(lambda m_, v_: scene_loss(m_, v_, *fixed), mats, vecs)
        grad_m, grad_v = pull(jnp.ones((), jnp.float32) / count)
        loss_total = loss_total + value
        vec_grad = vec_grad + grad_v
        mat_grads.append(grad_m + errors[scene])
    velocity = node_feat[:, :, 8:10]
    stats = jnp.stack([lax.optimization_barrier(jnp.sum(velocity * keep_all, (0, 1))), lax.optimization_barrier(jnp.sum(velocity * velocity * keep_all, (0, 1))), lax.optimization_barrier(jnp.sum(target * keep_all, (0, 1))), lax.optimization_barrier(jnp.sum(target * target * keep_all, (0, 1)))]) / count
    left = sum((jnp.einsum('kij,kjr->kir', a, factors, precision=HIGH) for a in mat_grads))
    left = orthonormal(left)
    right = sum((jnp.einsum('kij,kir->kjr', a, left, precision=HIGH) for a in mat_grads))
    approx = jnp.einsum('kir,kjr->kij', left, right, precision=HIGH)
    new_errors = jnp.stack([a - approx for a in mat_grads])
    mats_mom = 0.9 * mats_momentum + approx
    vecs_mom = 0.9 * vecs_momentum + vec_grad
    return (loss_total, count, stats, mats - 4.0 * mats_mom, mats_mom, right, new_errors, vecs - 4.0 * vecs_mom, vecs_mom)
```

```python
from functools import partial

import jax
import jax.numpy as jnp
from jax import lax
from jax.experimental import pallas as pl
from jax.experimental.pallas import tpu as pltpu
from jax.sharding import PartitionSpec as P

NFEAT = 14
NTYPES = 9
EFEAT = 3
LEAD = NFEAT + NTYPES
ROWS0 = LEAD + EFEAT
LAT = 128
BLOCK = 1024
F32 = jnp.float32
BF16 = jnp.bfloat16
NN = (((1,), (0,)), ((), ()))
NT = (((1,), (1,)), ((), ()))
TN = (((0,), (0,)), ((), ()))


def mm(a, b, dims=NN):
    return lax.dot_general(a, b, dims, preferred_element_type=F32)


def split(w):
    hi = w.astype(BF16)
    return hi, (w - hi.astype(F32)).astype(BF16)


def mm2(a, pair, dims=NN):
    return mm(a, pair[0], dims) + mm(a, pair[1], dims)


def mm3(a, b, dims=NN):
    ah, al = split(a)
    bh, bl = split(b)
    return mm(ah, bh, dims) + (mm(ah, bl, dims) + mm(al, bh, dims))


def silu_half(half):
    up = 1.0 + jnp.tanh(half)
    value = half * up
    sig = 0.5 * up
    return value, sig + value - value * sig


def rows_of(vecs_ref, which):
    base = ROWS0 + 5 * which
    return [vecs_ref[base + i : base + i + 1, :] for i in range(5)]


def mean_last(v):
    return jnp.mean(v, -1, keepdims=True)


def fold_rows(v):
    total = v[0:8]
    for i in range(8, v.shape[0], 8):
        total = total + v[i : i + 8]
    return total


def node_tail(first, second, third, vec):
    b1, b2, b3, g, o = vec
    s1, d1 = silu_half(0.5 * (first + b1))
    s2, d2 = silu_half(0.5 * (mm3(s1, second) + b2))
    z = mm3(s2, third) + b3
    c = z - mean_last(z)
    inv = lax.rsqrt(mean_last(c * c) + 1e-05)
    xhat = c * inv
    return xhat * g + o, (s1, d1, s2, d2, xhat, jnp.broadcast_to(inv, xhat.shape))


def node_tail_back(d, kept, second, third, vec):
    s1, d1, s2, d2, xhat, inv = kept
    g = vec[3]
    dy = d * g
    dz3 = inv * (dy - mean_last(dy) - xhat * mean_last(dy * xhat))
    dz2 = mm3(dz3, third, NT) * d2
    dz1 = mm3(dz2, second, NT) * d1
    sums = [fold_rows(v) for v in (dz1, dz2, dz3, d * xhat, d)]
    rows = [jnp.sum(v, 0, keepdims=True) for v in sums]
    return dz1, mm3(s1, dz2, TN), mm3(s2, dz3, TN), rows


def center(w):
    return w - mean_last(w)


def edge_tail(half, second, third, b2, b3, g, o, ones):
    s1, d1 = silu_half(half)
    s1 = s1.astype(BF16)
    s2, d2 = silu_half(mm2(s1, second) + b2)
    s2 = s2.astype(BF16)
    c = mm2(s2, third) + b3
    inv = lax.rsqrt(mm((c * c).astype(BF16), ones) + 1e-05)
    xhat = c * inv
    kept = (s1, d1, s2, d2, xhat.astype(BF16), inv)
    return xhat * g + o, kept


def edge_tail_back(d, kept, second, third, g, ones, grads, sums):
    s1, d1, s2, d2, xhat, inv = kept
    d1, d2, xhat, inv = (v[...].astype(F32) for v in (d1, d2, xhat, inv))
    dx = d * xhat
    dyx = (dx * g).astype(BF16)
    dc = inv * (d * g - xhat * mm(dyx, ones))
    dcb = dc.astype(BF16)
    dz2 = mm2(dcb, third, NT) * d2
    dz2b = dz2.astype(BF16)
    dz1 = mm2(dz2b, second, NT) * d1
    grads[0][...] += mm(s1[...], dz2b, TN)
    grads[1][...] += mm(s2[...], dcb, TN)
    for i, v in enumerate((dz1, dz2, dc, dx, d)):
        sums[i] += fold_rows(v)
    return dz1


def store_kept(refs, kept):
    for ref, v in zip(refs, kept):
        ref[...] = v


def put_pair(ref, at, w):
    hi, lo = split(w)
    ref[at] = hi
    ref[at + 1] = lo


def pair(ref, at):
    return ref[at], ref[at + 1]


def columns_of(code):
    parts = [
        jnp.transpose(jnp.broadcast_to(code[q : q + 1, :], (LAT, LAT))) for q in range(code.shape[0])
    ]
    return jnp.concatenate(parts, 0)


def pick_mask(column, count):
    lanes = lax.broadcasted_iota(jnp.int32, (column.shape[0], LAT), 1)
    parts = [
        jnp.where(column == lanes + LAT * j, 1.0, 0.0).astype(BF16) for j in range(count // LAT)
    ]
    return parts[0] if len(parts) == 1 else jnp.concatenate(parts, 1)


def add_mask(row, count):
    down = lax.broadcasted_iota(jnp.int32, (count, LAT), 0)
    parts = [
        jnp.where(row[q : q + 1, :] == down, 1.0, 0.0).astype(BF16) for q in range(row.shape[0])
    ]
    return jnp.concatenate(parts, 1)


def halves(v, upper):
    return jnp.concatenate([jnp.where(upper, 0.0, v), jnp.where(upper, v, 0.0)], 1)


def choose(wide, upper):
    return jnp.where(upper, wide[:, LAT:], wide[:, :LAT])


def send_of(code):
    return code >> 12


def recv_of(code):
    return code & 1023


def send_upper(code):
    return (code & 2048) != 0


def recv_upper(code):
    return (code & 1024) != 0


def fold_table(table):
    half = table.shape[0] // 2
    return jnp.concatenate([table[:half], table[half:]], 1)


def unfold(v):
    return jnp.concatenate([v[:, :LAT], v[:, LAT:]], 0)


def add_into(ref, code, column, values, recv_only=False):
    if not recv_only:
        ref[1][...] += mm(
            add_mask(send_of(code), ref[1].shape[0]),
            halves(values, send_upper(column)).astype(BF16),
        )
    mask = add_mask(recv_of(code), ref[0].shape[0])
    values = halves(values, recv_upper(column))
    if recv_only:
        ref[0][...] += mm2(mask, split(values))
    else:
        ref[0][...] += mm(mask, values.astype(BF16))


def encode_edges_kernel(x_ref, lo_ref, hi_ref, vecs_ref, e_ref, *rest):
    kept, w_ref = rest[:6], rest[6]
    b1, b2, b3, g, o = rows_of(vecs_ref, 1)

    @pl.when(pl.program_id(0) == 0)
    def _():
        put_pair(w_ref, 0, 0.5 * lo_ref[2])
        put_pair(w_ref, 2, center(hi_ref[0]))

    ones = jnp.full((LAT, LAT), 1.0 / LAT, BF16)
    xh, xl = split(x_ref[...])
    wh, wl = split(0.5 * vecs_ref[LEAD:ROWS0, :])
    half = mm(xh, wh) + (mm(xh, wl) + mm(xl, wh)) + 0.5 * b1
    out, saved = edge_tail(half, pair(w_ref, 0), pair(w_ref, 2), 0.5 * b2, center(b3), g, o, ones)
    e_ref[...] = out.astype(BF16)
    store_kept(kept, saved)


def edge_step(code_ref, e_ref, kept, w_ref, send_table, recv_table, vec, total):
    b1, b2, b3, g, o = vec
    ones = jnp.full((LAT, LAT), 1.0 / LAT, BF16)
    code = code_ref[...]
    column = columns_of(code)
    e = e_ref[...]
    half = mm2(e, pair(w_ref, 0)) + 0.5 * b1
    wide = mm2(pick_mask(send_of(column), send_table.shape[1]), pair(send_table, 0))
    half = half + choose(wide, send_upper(column))
    wide = mm2(pick_mask(recv_of(column), recv_table.shape[1]), pair(recv_table, 0))
    half = half + choose(wide, recv_upper(column))
    out, saved = edge_tail(half, pair(w_ref, 2), pair(w_ref, 4), 0.5 * b2, center(b3), g, o, ones)
    store_kept(kept, saved)
    add_into((total,), code, column, out, recv_only=True)
    return e, out


def put_edge_weights(w_ref, a, second, third):
    put_pair(w_ref, 0, 0.5 * a)
    put_pair(w_ref, 2, 0.5 * second)
    put_pair(w_ref, 4, center(third))


def forward_first_kernel(
    own, code_ref, e_ref, feat_ref, enc_ref, ma, mb, mc, na, vecs_ref, e_out, *rest
):
    kept, rest = rest[:6], rest[6:]
    wide_ref, enc_kept, agg_ref, upd_kept, h_ref, hb_ref, hc_ref = rest[:7]
    w_ref, send_table, recv_table, total = rest[7:]
    step = pl.program_id(0)

    @pl.when(step == 0)
    def _():
        put_edge_weights(w_ref, ma[0], mb[0], mb[1])
        types = lax.broadcasted_iota(jnp.int32, (NTYPES, feat_ref.shape[1]), 0).astype(F32)
        onehot = jnp.where(feat_ref[NFEAT : NFEAT + 1, :] == types, 1.0, 0.0)
        first = mm3(feat_ref[0:NFEAT, :], vecs_ref[0:NFEAT, :], TN)
        first = first + mm2(onehot.astype(BF16), split(vecs_ref[NFEAT:LEAD, :]), TN)
        out, saved = node_tail(first, enc_ref[0], enc_ref[1], rows_of(vecs_ref, 0))
        wide_ref[...] = out
        for i, v in enumerate(saved):
            enc_kept[i] = v
        put_pair(send_table, 0, fold_table(0.5 * mm3(out, ma[1])))
        put_pair(recv_table, 0, fold_table(0.5 * mm3(out[own : 2 * own], ma[2])))
        total[...] = jnp.zeros_like(total)

    e, out = edge_step(
        code_ref, e_ref, kept, w_ref, send_table, recv_table, rows_of(vecs_ref, 2), total
    )
    e_out[...] = (e.astype(F32) + out).astype(BF16)

    @pl.when(step == pl.num_programs(0) - 1)
    def _():
        h = wide_ref[own : 2 * own, :]
        agg = unfold(total[...])
        agg_ref[...] = agg
        first = mm3(h, mb[2]) + mm3(agg, mc[0])
        delta, saved = node_tail(first, mc[1], mc[2], rows_of(vecs_ref, 3))
        for i, v in enumerate(saved):
            upd_kept[i] = v
        h = h + delta
        h_ref[...] = h
        hb_ref[...] = 0.5 * mm3(h, na[1])
        hc_ref[...] = 0.5 * mm3(h, na[2])


def forward_second_kernel(
    own, code_ref, e_ref, left, mid, right, hc_ref, h_ref, ma, mb, mc, dec, vecs_ref, goal_ref,
    keep_ref, feat_ref, *rest
):
    kept, rest = rest[:6], rest[6:]
    dh_ref, dagg_ref, gm_ref, gv_ref, sums_ref = rest[:5]
    w_ref, send_table, recv_table, total = rest[5:]
    step = pl.program_id(0)

    @pl.when(step == 0)
    def _():
        put_edge_weights(w_ref, ma[0], mb[0], mb[1])
        table = jnp.concatenate([left[...], mid[...], right[...]], 0)
        put_pair(send_table, 0, fold_table(table))
        put_pair(recv_table, 0, fold_table(hc_ref[...]))
        total[...] = jnp.zeros_like(total)

    edge_step(code_ref, e_ref, kept, w_ref, send_table, recv_table, rows_of(vecs_ref, 4), total)

    @pl.when(step == pl.num_programs(0) - 1)
    def _():
        h = h_ref[...]
        agg = unfold(total[...])
        vec = rows_of(vecs_ref, 5)
        first = mm3(h, mb[2]) + mm3(agg, mc[0])
        delta, saved = node_tail(first, mc[1], mc[2], vec)
        out = h + delta
        base = ROWS0 + 30
        s1, d1 = silu_half(0.5 * (mm3(out, dec[1]) + vecs_ref[base : base + 1, :]))
        s2, d2 = silu_half(0.5 * (mm3(s1, dec[2]) + vecs_ref[base + 1 : base + 2, :]))
        last = vecs_ref[base + 2 : base + 4, :]
        keep = keep_ref[...]
        goal = goal_ref[...]
        diff = mm3(last, s2, NT) - goal
        kept_diff = diff * keep
        dpred = 2.0 * kept_diff
        dz2 = mm3(dpred, last, TN) * d2
        dz1 = mm3(dz2, dec[2], NT) * d1
        d = mm3(dz1, dec[1], NT)
        dz, g_second, g_third, rows = node_tail_back(d, saved, mc[1], mc[2], vec)
        dh_ref[...] = d + mm3(dz, mb[2], NT)
        dagg_ref[...] = mm3(dz, mc[0], NT)
        gm_ref[0] = mm3(out, dz1, TN)
        gm_ref[1] = mm3(s1, dz2, TN)
        gm_ref[2] = mm3(h, dz, TN)
        gm_ref[3] = mm3(agg, dz, TN)
        gm_ref[4] = g_second
        gm_ref[5] = g_third
        rows = rows + [
            jnp.sum(fold_rows(dz1), 0, keepdims=True),
            jnp.sum(fold_rows(dz2), 0, keepdims=True),
            mm3(dpred, s2),
        ]
        at = 0
        for v in rows:
            gv_ref[at : at + v.shape[0], :] = v
            at += v.shape[0]
        gv_ref[at:, :] = jnp.zeros((gv_ref.shape[0] - at, LAT), F32)
        velocity = feat_ref[8:10, :]
        pieces = [
            kept_diff * diff,
            velocity * keep,
            velocity * velocity * keep,
            goal * keep,
            goal * goal * keep,
            jnp.broadcast_to(keep, velocity.shape),
        ]
        for i, v in enumerate(pieces):
            part = v[:, 0:LAT]
            for j in range(LAT, own, LAT):
                part = part + v[:, j : j + LAT]
            sums_ref[2 * i : 2 * i + 2, :] = part
        sums_ref[12:16, :] = jnp.zeros((4, LAT), F32)


def backward_step(code_ref, kept, e_ref, dagg, de, w_ref, vec, gm, sums, totals):
    ones = jnp.full((LAT, LAT), 1.0 / LAT, BF16)
    code = code_ref[...]
    column = columns_of(code)
    wide = mm2(pick_mask(recv_of(column), dagg.shape[1]), pair(dagg, 0))
    d = choose(wide, recv_upper(column))
    if de is not None:
        d = d + de
    dz1 = edge_tail_back(
        d, kept, pair(w_ref, 2), pair(w_ref, 4), vec[3], ones, (gm.at[1], gm.at[2]), sums
    )
    dz1b = dz1.astype(BF16)
    gm[0] += mm(e_ref[...], dz1b, TN)
    add_into(totals, code, column, dz1)
    back = mm2(dz1b, pair(w_ref, 0), NT)
    return back if de is None else de + back


def finish_sums(sums):
    rows = [jnp.sum(sums[i], 0, keepdims=True) for i in range(5)]
    rows[2] = center(rows[2])
    return rows


def put_back_weights(w_ref, at, a, second, third):
    put_pair(w_ref, at, a)
    put_pair(w_ref, at + 2, second)
    put_pair(w_ref, at + 4, center(third))


def backward_second_kernel(own, code_ref, *rest):
    kept, rest = rest[:6], rest[6:]
    e_ref, dagg_ref, ma, mb, vecs_ref, de_out, gm, gv_ref, spread, s_recv = rest[:10]
    w_ref, dagg, sums, recv_total, send_total = rest[10:]
    step = pl.program_id(0)

    @pl.when(step == 0)
    def _():
        put_back_weights(w_ref, 0, ma[0], mb[0], mb[1])
        put_pair(dagg, 0, fold_table(dagg_ref[...]))
        gm[...] = jnp.zeros_like(gm)
        sums[...] = jnp.zeros_like(sums)
        recv_total[...] = jnp.zeros_like(recv_total)
        send_total[...] = jnp.zeros_like(send_total)

    de = backward_step(
        code_ref, kept, e_ref, dagg, None, w_ref, rows_of(vecs_ref, 4), gm, sums,
        (recv_total, send_total),
    )
    de_out[...] = de.astype(BF16)

    @pl.when(step == pl.num_programs(0) - 1)
    def _():
        gm[2] = center(gm[2])
        for i, v in enumerate(finish_sums(sums)):
            gv_ref[i : i + 1, :] = v
        gv_ref[5:8, :] = jnp.zeros((3, LAT), F32)
        spread[...] = unfold(send_total[...])
        s_recv[...] = unfold(recv_total[...])


def backward_first_kernel(own, code_ref, *rest):
    kept, rest = rest[:6], rest[6:]
    e_ref, rest = rest[0], rest[1:]
    enc_kept, rest = rest[:6], rest[6:]
    x_ref, de_ref, dh_ref, mid, from_left, from_right, s_recv, h_ref, rest = *rest[:8], rest[8:]
    wide_ref, node_kept, upd_kept, agg_ref, feat_ref, rest = *rest[:5], rest[5:]
    enc_lo, enc_hi, ma, mb, mc, na, vecs_ref, rest = *rest[:7], rest[7:]
    gm, gn, gv_ref = rest[:3]
    w_ref, dagg, sums, enc_sums, we_ref, dh0, recv_total, send_total = rest[3:]
    step = pl.program_id(0)

    @pl.when(step == 0)
    def _():
        put_back_weights(w_ref, 0, ma[0], mb[0], mb[1])
        put_pair(w_ref, 6, enc_lo[2])
        put_pair(w_ref, 8, center(enc_hi[0]))
        for ref in (gm, sums, enc_sums, we_ref, recv_total, send_total):
            ref[...] = jnp.zeros_like(ref)
        sent = mid[...] + from_left[...] + from_right[...]
        got = s_recv[...]
        h = h_ref[...]
        gn[0] = mm3(h, sent, TN)
        gn[1] = mm3(h, got, TN)
        d = dh_ref[...] + mm3(sent, na[1], NT) + mm3(got, na[2], NT)
        vec = rows_of(vecs_ref, 3)
        saved = [upd_kept[i] for i in range(6)]
        dz, g_second, g_third, rows = node_tail_back(d, saved, mc[1], mc[2], vec)
        gn[2] = mm3(wide_ref[own : 2 * own, :], dz, TN)
        gn[3] = mm3(agg_ref[...], dz, TN)
        gn[4] = g_second
        gn[5] = g_third
        for i, v in enumerate(rows):
            gv_ref[i : i + 1, :] = v
        dh0[...] = d + mm3(dz, mb[2], NT)
        put_pair(dagg, 0, fold_table(mm3(dz, mc[0], NT)))

    de = backward_step(
        code_ref, kept, e_ref, dagg, de_ref[...].astype(F32), w_ref, rows_of(vecs_ref, 2), gm, sums,
        (recv_total, send_total),
    )
    ones = jnp.full((LAT, LAT), 1.0 / LAT, BF16)
    dz1 = edge_tail_back(
        de, enc_kept, pair(w_ref, 6), pair(w_ref, 8), rows_of(vecs_ref, 1)[3], ones,
        (gm.at[3], gm.at[4]), enc_sums,
    )
    we_ref[...] += mm(x_ref[...].astype(BF16), dz1.astype(BF16), TN)

    @pl.when(step == pl.num_programs(0) - 1)
    def _():
        gm[2] = center(gm[2])
        gm[4] = center(gm[4])
        at = 5
        for v in finish_sums(sums) + finish_sums(enc_sums):
            gv_ref[at : at + 1, :] = v
            at += 1
        gv_ref[at : at + EFEAT, :] = we_ref[...]
        at += EFEAT
        sent = unfold(send_total[...])
        got = unfold(recv_total[...])
        h = wide_ref[...]
        gn[6] = mm3(h, sent, TN)
        gn[7] = mm3(h[own : 2 * own], got, TN)
        d = mm3(sent, ma[1], NT)
        inner = d[own : 2 * own] + dh0[...] + mm3(got, ma[2], NT)
        d = jnp.concatenate([d[:own], inner, d[2 * own :]], 0)
        saved = [node_kept[i] for i in range(6)]
        vec = rows_of(vecs_ref, 0)
        dz, g_second, g_third, rows = node_tail_back(d, saved, enc_lo[0], enc_lo[1], vec)
        gn[8] = g_second
        gn[9] = g_third
        types = lax.broadcasted_iota(jnp.int32, (NTYPES, feat_ref.shape[1]), 0).astype(F32)
        onehot = jnp.where(feat_ref[NFEAT : NFEAT + 1, :] == types, 1.0, 0.0)
        for v in rows:
            gv_ref[at : at + 1, :] = v
            at += 1
        gv_ref[at : at + NFEAT, :] = mm3(feat_ref[0:NFEAT, :], dz)
        at += NFEAT
        gv_ref[at : at + NTYPES, :] = mm2(onehot.astype(BF16), split(dz))
        at += NTYPES
        gv_ref[at:, :] = jnp.zeros((gv_ref.shape[0] - at, LAT), F32)


def whole(shape):
    return pl.BlockSpec(shape, lambda i: (0,) * len(shape))


def third(at):
    return pl.BlockSpec((3, LAT, LAT), lambda i: (at, 0, 0))


def edges(width):
    return pl.BlockSpec((BLOCK, width), lambda i: (i, 0))


CODE = pl.BlockSpec((BLOCK // LAT, LAT), lambda i: (i, 0))
KEPT = 6
KINDS = (BF16, F32, BF16, F32, BF16, F32)


def call(kernel, count, ins, outs, scratch):
    return pl.pallas_call(
        kernel,
        grid=(count // BLOCK,),
        in_specs=[spec for _, spec in ins],
        out_specs=[spec for _, _, spec in outs],
        out_shape=[jax.ShapeDtypeStruct(shape, kind) for shape, kind, _ in outs],
        scratch_shapes=scratch,
        compiler_params=pltpu.CompilerParams(
            dimension_semantics=("arbitrary",), vmem_limit_bytes=56 << 20
        ),
    )(*[array for array, _ in ins])


def full(shape):
    return (shape, F32, whole(shape))


def shifted(up, down):
    count = lax.axis_size("edge")
    ends = count - 1
    from_left = lax.ppermute(up, "edge", [(i, i + 1) for i in range(ends)])
    from_right = lax.ppermute(down, "edge", [(i + 1, i) for i in range(ends)])
    return from_left, from_right


SMALL = {"n1": 0, "e1": 16, "n0": 24, "sums": 72}
SMALL_ROWS = 88
PLACES = (
    (4, 5, 20, 21, 22, 23),
    (15, 18, 19),
    (6, 9, 10, 2, 3),
    (16, 17, 11, 12, 13, 14, 7, 8, 0, 1),
)


def sides_of(count):
    return {16: (2, 2, 4), 64: (4, 4, 4)}.get(count, (count, 1, 1))


class Reducer:
    def __init__(self, count, rows):
        sides = sides_of(count)
        strides = (1, sides[0], sides[0] * sides[1])
        dims = list(zip(sides, strides))
        self.orders = (dims, [dims[1], dims[0], dims[2]])
        self.rows = rows
        self.count = count
        self.copies = 2 * sum(k - 1 for k in sides)

    def scratch(self):
        shapes = []
        for order in self.orders:
            length = self.rows // 2
            for k, _ in order:
                length //= k
                shapes.append(pltpu.VMEM((max(k - 1, 1), length, LAT), F32))
        sems = [pltpu.SemaphoreType.DMA((2 * self.copies,))] * 2
        return shapes + sems

    def bind(self, acc, full, scratch):
        self.acc, self.full = acc, full
        self.slots = (scratch[:3], scratch[3:6])
        self.send, self.recv = scratch[6:]
        self.me = lax.axis_index("edge")
        self.begin = [0, self.rows // 2]
        self.length = [self.rows // 2] * 2
        self.flying = [[], []]
        self.used = 0

    def at(self, order, t):
        k, stride = order
        mine = (self.me // stride) % k
        other = (mine + t) % k
        return mine, other, self.me + (other - mine) * stride

    def peers(self):
        return [self.at(d, t)[2] for d in self.orders[0] for t in range(1, d[0])]

    def copy(self, source, target, device):
        out = pltpu.make_async_remote_copy(
            src_ref=source,
            dst_ref=target,
            send_sem=self.send.at[self.used],
            recv_sem=self.recv.at[self.used],
            device_id={"edge": device},
            device_id_type=pl.DeviceIdType.MESH,
        )
        self.used += 1
        out.start()
        return out

    def window(self, begin, length):
        return pl.ds(pl.multiple_of(begin, 8), length)

    def scatter(self, half, stage):
        side = self.orders[half][stage]
        k = side[0]
        length = self.length[half] // k
        for t in range(1, k):
            _, other, device = self.at(side, t)
            source = self.acc.at[self.window(self.begin[half] + other * length, length)]
            self.flying[half].append(self.copy(source, self.slots[half][stage].at[t - 1], device))
        self.begin[half] = self.begin[half] + ((self.me // side[1]) % k) * length
        self.length[half] = length

    def add(self, half, stage):
        for one in self.flying[half]:
            one.wait()
        self.flying[half] = []
        rows = self.window(self.begin[half], self.length[half])
        k = self.orders[half][stage][0]
        value = self.acc[rows, :]
        for t in range(1, k):
            value = value + self.slots[half][stage][t - 1]
        self.acc[rows, :] = value
        if stage == 2:
            self.full[rows, :] = value

    def gather(self, half, stage):
        side = self.orders[half][stage]
        k = side[0]
        rows = self.window(self.begin[half], self.length[half])
        for t in range(1, k):
            part = self.full.at[rows]
            self.flying[half].append(self.copy(part, part, self.at(side, t)[2]))

    def arrive(self, half, stage):
        for one in self.flying[half]:
            one.wait()
        self.flying[half] = []
        k, stride = self.orders[half][stage]
        self.begin[half] = self.begin[half] - ((self.me // stride) % k) * self.length[half]
        self.length[half] = self.length[half] * k

    def run(self):
        for stage in range(3):
            for half in range(2):
                if stage:
                    self.add(half, stage - 1)
                self.scatter(half, stage)
        for stage in (2, 1, 0):
            for half in range(2):
                if stage == 2:
                    self.add(half, 2)
                else:
                    self.arrive(half, stage + 1)
                self.gather(half, stage)
        for half in range(2):
            self.arrive(half, 0)


def reduce_kernel(reducer, mats, *refs):
    pieces, refs = refs[:4], refs[4:]
    rows_in, refs = refs[:4], refs[4:]
    errors, factors, refs = refs[0], refs[1], refs[2:]
    total_ref, left_ref, right_ref, small_ref, refs = *refs[:4], refs[4:]
    acc, full, mine, theirs, right_mine, right_theirs, pair_send, pair_recv = refs[:8]
    reducer.bind(acc, full, refs[8:])
    sibling = {"rep": 1 - lax.axis_index("rep")}
    barrier = pltpu.get_barrier_semaphore()
    peers = [{"edge": one} for one in reducer.peers()] + [sibling]
    for peer in peers:
        pl.semaphore_signal(barrier, inc=1, device_id=peer, device_id_type=pl.DeviceIdType.MESH)
    pl.semaphore_wait(barrier, len(peers))

    for ref, places in zip(pieces, PLACES):
        for i, place in enumerate(places):
            acc[place * LAT : (place + 1) * LAT, :] = ref[i]
    base = mats * LAT
    for ref, at in zip(rows_in, SMALL.values()):
        acc[base + at : base + at + ref.shape[0], :] = ref[...]
    acc[base + SMALL_ROWS :, :] = jnp.zeros((acc.shape[0] - base - SMALL_ROWS, LAT), F32)
    rank = factors.shape[1]

    def of(k):
        return pl.ds(pl.multiple_of(k * LAT, LAT), LAT)

    def ranked(k, offset=0):
        return pl.ds(pl.multiple_of(offset + k * rank, 8), rank)

    reducer.run()

    def project(k, unused):
        mine[ranked(k), :] = mm3(factors[k], full[of(k), :], NT)
        mine[ranked(k, mats * rank), :] = mm3(factors[k], errors[k], NT)
        return unused

    lax.fori_loop(0, mats, project, 0)
    end = 2 * mats * rank
    mine[end:, :] = full[base : base + SMALL_ROWS, :]

    def swap(source, target, at):
        one = pltpu.make_async_remote_copy(
            src_ref=source,
            dst_ref=target,
            send_sem=pair_send.at[at],
            recv_sem=pair_recv.at[at],
            device_id=sibling,
            device_id_type=pl.DeviceIdType.MESH,
        )
        one.start()
        one.wait()

    swap(mine, theirs, 0)
    small = mine[end:, :] + theirs[end:, :]
    small_ref[...] = small
    at = SMALL["sums"] + 10
    scale = 1.0 / jnp.sum(small[at : at + 1, :], 1, keepdims=True)
    half = mats * rank
    both = (mine[0:half, :] + theirs[0:half, :]) * scale
    both = both + (mine[half:end, :] + theirs[half:end, :])
    both = both.reshape(mats, rank, LAT)
    columns = [both[:, i, :] for i in range(rank)]
    for i in range(rank):
        v = columns[i]
        v = v * lax.rsqrt(jnp.sum(v * v, 1, keepdims=True) + 1e-12)
        columns[i] = v
        for j in range(i + 1, rank):
            columns[j] = columns[j] - jnp.sum(v * columns[j], 1, keepdims=True) * v
    for i in range(rank):
        left_ref[:, i, :] = columns[i]

    def transform(k, unused):
        total = full[of(k), :] * scale + errors[k]
        total_ref[k] = total
        right_mine[ranked(k), :] = mm3(left_ref[k], total)
        return unused

    lax.fori_loop(0, mats, transform, 0)
    swap(right_mine, right_theirs, 1)
    right_ref[...] = (right_mine[...] + right_theirs[...]).reshape(mats, rank, LAT)


def reduce_gradients(pieces, rows, errors, factors):
    mats, _, rank = factors.shape
    count = lax.axis_size("edge")
    unit = 16 * count
    height = -(-(mats * LAT + SMALL_ROWS) // unit) * unit
    reducer = Reducer(count, height)
    flat = lambda n: pltpu.VMEM((n, LAT), F32)
    message = 2 * mats * rank + SMALL_ROWS
    vmem = pl.BlockSpec(memory_space=pltpu.VMEM)
    shape = lambda *dims: jax.ShapeDtypeStruct(dims, F32)
    return pl.pallas_call(
        partial(reduce_kernel, reducer, mats),
        in_specs=[vmem] * 10,
        out_specs=[vmem] * 4,
        out_shape=[
            shape(mats, LAT, LAT), shape(mats, rank, LAT), shape(mats, rank, LAT),
            shape(SMALL_ROWS, LAT),
        ],
        scratch_shapes=[
            flat(height), flat(height), flat(message), flat(message), flat(mats * rank),
            flat(mats * rank), pltpu.SemaphoreType.DMA((2,)), pltpu.SemaphoreType.DMA((2,)),
        ]
        + reducer.scratch(),
        compiler_params=pltpu.CompilerParams(
            collective_id=0, has_side_effects=True, vmem_limit_bytes=56 << 20
        ),
    )(*pieces, *rows, errors, jnp.swapaxes(factors, 1, 2))


def finish_kernel(total, left, right, mats, momentum, new_mats, new_momentum, new_errors):
    for k in range(total.shape[0]):
        approx = mm3(left[k], right[k], TN)
        moved = 0.9 * momentum[k] + approx
        new_momentum[k] = moved
        new_mats[k] = mats[k] - 4.0 * moved
        new_errors[k] = total[k] - approx


def finish(total, left, right, mats, momentum):
    group = 4
    big = pl.BlockSpec((group, LAT, LAT), lambda i: (i, 0, 0))
    thin = pl.BlockSpec((group,) + left.shape[1:], lambda i: (i, 0, 0))
    return pl.pallas_call(
        finish_kernel,
        grid=(total.shape[0] // group,),
        in_specs=[big, thin, thin, big, big],
        out_specs=[big] * 3,
        out_shape=[jax.ShapeDtypeStruct(total.shape, F32)] * 3,
    )(total, left, right, mats, momentum)


def shards(
    node_feat, node_types, boundary, target, edge_feat, senders, receivers, edge_counts, mats, vecs,
    mats_momentum, vecs_momentum, factors, errors,
):
    own = node_feat.shape[1]
    wide = 3 * own
    count = senders.shape[1]
    place = lax.axis_index("edge")
    slots = jnp.arange(count, dtype=jnp.int32)
    live = slots < edge_counts[0, 0]
    send = senders[0] - (place - 1) * own
    recv = receivers[0] - place * own
    upper_s = send >= wide // 2
    upper_r = recv >= own // 2
    send = jnp.where(upper_s, send - wide // 2, send)
    recv = jnp.where(upper_r, recv - own // 2, recv)
    code = (send << 12) + jnp.where(upper_s, 2048, 0) + jnp.where(upper_r, 1024, 0) + recv
    code = jnp.where(live, code, (1023 << 12) + 1023).reshape(count // LAT, LAT)

    feat = jnp.concatenate(
        [node_feat[0].T, node_types.astype(F32), jnp.zeros((1, own), F32)], 0
    )
    from_left, from_right = shifted(feat, feat)
    feat_wide = jnp.concatenate([from_left, feat, from_right], 1)
    keep = (1 - boundary).astype(F32)
    goal = target[0].T
    x = edge_feat[0]

    kept_outs = [((count, LAT), kind, edges(LAT)) for kind in KINDS]
    vec_in = (vecs, whole(vecs.shape))
    mat = lambda at: (mats, third(at))
    node = (own, LAT)
    pairs = lambda n: pltpu.VMEM((n, LAT, LAT), BF16)
    tables = [
        pltpu.VMEM((2, wide // 2, 2 * LAT), BF16),
        pltpu.VMEM((2, own // 2, 2 * LAT), BF16),
        pltpu.VMEM((own // 2, 2 * LAT), F32),
    ]

    e0, *enc = call(
        encode_edges_kernel,
        count,
        [(x, edges(EFEAT)), mat(0), mat(1), vec_in],
        [((count, LAT), BF16, edges(LAT))] + kept_outs,
        [pairs(4)],
    )
    e1, *rest = call(
        partial(forward_first_kernel, own),
        count,
        [(code, CODE), (e0, edges(LAT)), (feat_wide, whole(feat_wide.shape)), mat(0)]
        + [mat(2), mat(3), mat(4), mat(5), vec_in],
        [((count, LAT), BF16, edges(LAT))]
        + kept_outs
        + [full((wide, LAT)), full((KEPT, wide, LAT)), full(node), full((KEPT,) + node)]
        + [full(node), full(node), full(node)],
        [pairs(6)] + tables,
    )
    kept0, rest = rest[:KEPT], rest[KEPT:]
    h0w, node_kept, agg0, upd_kept, h1, hb, hc = rest
    left, right = shifted(hb, hb)
    nodes = lambda v: (v, whole(v.shape))
    *kept1, dh, dagg, gm_n1, gv_n1, sums = call(
        partial(forward_second_kernel, own),
        count,
        [(code, CODE), (e1, edges(LAT)), nodes(left), nodes(hb), nodes(right), nodes(hc), nodes(h1)]
        + [mat(5), mat(6), mat(7), mat(1), vec_in, nodes(goal), nodes(keep), nodes(feat)],
        kept_outs
        + [full(node), full(node), full((6, LAT, LAT)), full((16, LAT)), full((16, LAT))],
        [pairs(6)] + tables,
    )
    totals = [
        pltpu.VMEM((own // 2, 2 * LAT), F32),
        pltpu.VMEM((wide // 2, 2 * LAT), F32),
    ]
    dagg_table = pltpu.VMEM((2, own // 2, 2 * LAT), BF16)
    row_sums = pltpu.VMEM((5, 8, LAT), F32)
    de, gm_e1, gv_e1, spread, s_recv = call(
        partial(backward_second_kernel, own),
        count,
        [(code, CODE)] + [(v, edges(LAT)) for v in kept1] + [(e1, edges(LAT)), nodes(dagg)]
        + [mat(5), mat(6), vec_in],
        [((count, LAT), BF16, edges(LAT)), full((3, LAT, LAT)), full((8, LAT)), full((wide, LAT))]
        + [full(node)],
        [pairs(6), dagg_table, row_sums] + totals,
    )
    from_left, from_right = shifted(spread[2 * own :], spread[:own])
    gm_e0, gm_n0, gv_0 = call(
        partial(backward_first_kernel, own),
        count,
        [(code, CODE)] + [(v, edges(LAT)) for v in kept0] + [(e0, edges(LAT))]
        + [(v, edges(LAT)) for v in enc] + [(x, edges(EFEAT)), (de, edges(LAT)), nodes(dh)]
        + [nodes(spread[own : 2 * own]), nodes(from_left), nodes(from_right), nodes(s_recv)]
        + [nodes(h1), nodes(h0w), nodes(node_kept), nodes(upd_kept), nodes(agg0), nodes(feat_wide)]
        + [mat(0), mat(1), mat(2), mat(3), mat(4), mat(5), vec_in],
        [full((5, LAT, LAT)), full((10, LAT, LAT)), full((48, LAT))],
        [pairs(10), dagg_table, row_sums, row_sums, pltpu.VMEM((EFEAT, LAT), F32)]
        + [pltpu.VMEM(node, F32)] + totals,
    )
    total, left, right, small = reduce_gradients(
        (gm_n1, gm_e1, gm_e0, gm_n0), (gv_n1, gv_e1, gv_0, sums), errors[0], factors
    )
    new_mats, mats_mom, new_errors = finish(total, left, right, mats, mats_momentum)
    sums = jnp.sum(small[SMALL["sums"] :][:12].reshape(6, 2, LAT), -1)
    kept_count = sums[5, 0]
    stats = sums[1:5] / kept_count
    n1, e1, n0 = (small[SMALL[name] :] for name in ("n1", "e1", "n0"))
    vec_grad = jnp.concatenate(
        [n0[23:46], n0[15:18], n0[18:23], n0[10:15], n0[5:10], n0[0:5], e1[0:5], n1[0:9]]
    )
    vecs_mom = 0.9 * vecs_momentum + vec_grad / kept_count
    return (
        sums[0, 0] + sums[0, 1],
        kept_count,
        stats,
        new_mats,
        mats_mom,
        jnp.swapaxes(right, 1, 2),
        new_errors[None],
        vecs - 4.0 * vecs_mom,
        vecs_mom,
    )


def solution(mesh):
    placed = (
        P("rep", "edge", None),
        P("rep", "edge"),
        P("rep", "edge"),
        P("rep", "edge", None),
        P("rep", "edge", None),
        P("rep", "edge"),
        P("rep", "edge"),
        P("rep", "edge"),
        P(),
        P(),
        P(),
        P(),
        P(),
        P("rep", None, None, None),
    )
    return jax.shard_map(
        shards,
        mesh=mesh,
        in_specs=placed,
        out_specs=(P(), P(), P(), P(), P(), P(), P("rep", None, None, None), P(), P()),
        check_vma=False,
    )
```

```python
from functools import partial

import jax
import jax.numpy as jnp
from jax import lax
from jax.experimental import pallas as pl
from jax.experimental.pallas import tpu as pltpu
from jax.sharding import PartitionSpec as P

NFEAT = 14
NTYPES = 9
EFEAT = 3
LEAD = NFEAT + NTYPES
ROWS0 = LEAD + EFEAT
LAT = 128
BLOCK = 1024
SUB = 512
SHIFT = 12
F32 = jnp.float32
BF16 = jnp.bfloat16
MESH = pl.DeviceIdType.MESH
NN = (((1,), (0,)), ((), ()))
NT = (((1,), (1,)), ((), ()))
TN = (((0,), (0,)), ((), ()))


def mm(a, b, dims=NN):
    return lax.dot_general(a, b, dims, preferred_element_type=F32)


def split(w):
    hi = w.astype(BF16)
    return hi, (w - hi.astype(F32)).astype(BF16)


def twice(a):
    return jnp.concatenate([a, a], 1)


def stacked(w):
    return jnp.concatenate(split(w), 0)


def side_by_side(v):
    return jnp.concatenate(split(v), 1)


def joined(wide):
    return wide[:, :LAT] + wide[:, LAT:]


def mm3(a, b, dims=NN):
    ah, al = split(a)
    bh, bl = split(b)
    return mm(ah, bh, dims) + (mm(ah, bl, dims) + mm(al, bh, dims))


def silu_half(half):
    up = 1.0 + jnp.tanh(half)
    value = half * up
    sig = 0.5 * up
    return value, sig + value - value * sig


def mean_last(v):
    return jnp.mean(v, -1, keepdims=True)


def center(w):
    return w - mean_last(w)


def fold_rows(v):
    total = v[0:8]
    for i in range(8, v.shape[0], 8):
        total = total + v[i : i + 8]
    return total


def row_sum(v):
    return jnp.sum(fold_rows(v), 0, keepdims=True)


def unfold(v):
    return jnp.concatenate([v[:, :LAT], v[:, LAT:]], 0)


def together(parts):
    parts = list(parts)
    while parts:
        for part in list(parts):
            try:
                next(part)
            except StopIteration:
                parts.remove(part)


def node_tail(first, second, third, vec):
    b1, b2, b3, g, o = vec
    half1 = 0.5 * (first + b1)
    half2 = 0.5 * (mm3(silu_half(half1)[0], second) + b2)
    z = mm3(silu_half(half2)[0], third) + b3
    c = z - mean_last(z)
    inv = lax.rsqrt(mean_last(c * c) + 1e-05)
    xhat = c * inv
    return xhat * g + o, (half1, half2, xhat, jnp.broadcast_to(inv, xhat.shape))


def node_tail_back(d, kept, second, third, vec):
    half1, half2, xhat, inv = kept
    s1, d1 = silu_half(half1)
    s2, d2 = silu_half(half2)
    dy = d * vec[3]
    dz3 = inv * (dy - mean_last(dy) - xhat * mean_last(dy * xhat))
    dz2 = mm3(dz3, third, NT) * d2
    dz1 = mm3(dz2, second, NT) * d1
    rows = [row_sum(v) for v in (dz1, dz2, dz3, d * xhat, d)]
    return dz1, mm3(s1, dz2, TN), mm3(s2, dz3, TN), rows


def edge_tail(rows, half, kept, second, third, vec, ones):
    _, b2, b3, g, o = vec
    kept[0][rows, :] = half.astype(BF16)
    s1 = silu_half(half)[0].astype(BF16)
    half = mm(twice(s1), second) + 0.5 * b2
    yield
    kept[1][rows, :] = half.astype(BF16)
    s2 = silu_half(half)[0].astype(BF16)
    c = mm(twice(s2), third) + center(b3)
    yield
    inv = lax.rsqrt(mm((c * c).astype(BF16), ones) + 1e-05)
    xhat = c * inv
    kept[2][rows, :] = xhat.astype(BF16)
    kept[3][rows, :] = inv.astype(BF16)
    return xhat * g + o


def edge_tail_back(rows, d, kept, second, third, g, ones, grads, sums):
    xhat = kept[2][rows, :].astype(F32)
    inv = kept[3][rows, :].astype(F32)
    dx = d * xhat
    dc = inv * (d * g - xhat * mm((dx * g).astype(BF16), ones))
    dcb = dc.astype(BF16)
    for at, v in ((2, dc), (3, dx), (4, d)):
        sums[at] += fold_rows(v)
    yield
    s2, d2 = silu_half(kept[1][rows, :].astype(F32))
    dz2 = mm(twice(dcb), third) * d2
    grads[1][...] += mm(s2.astype(BF16), dcb, TN)
    sums[1] += fold_rows(dz2)
    dz2b = dz2.astype(BF16)
    yield
    s1, d1 = silu_half(kept[0][rows, :].astype(F32))
    dz1 = mm(twice(dz2b), second) * d1
    grads[0][...] += mm(s1.astype(BF16), dz2b, TN)
    sums[0] += fold_rows(dz1)
    yield
    return dz1


def finish_sums(sums):
    rows = [jnp.sum(sums[i], 0, keepdims=True) for i in range(5)]
    rows[2] = center(rows[2])
    return rows


def columns_of(code):
    parts = [
        jnp.transpose(jnp.broadcast_to(code[q : q + 1, :], (LAT, LAT))) for q in range(code.shape[0])
    ]
    return jnp.concatenate(parts, 0)


def pick_mask(column, count):
    lanes = lax.broadcasted_iota(jnp.int32, (column.shape[0], LAT), 1)
    return [jnp.where(column == lanes + LAT * j, 1.0, 0.0).astype(BF16) for j in range(count // LAT)]


def add_mask(row, count):
    down = lax.broadcasted_iota(jnp.int32, (count, LAT), 0)
    parts = [
        jnp.where(row[q : q + 1, :] == down, 1.0, 0.0).astype(BF16) for q in range(row.shape[0])
    ]
    return jnp.concatenate(parts, 1)


def halves(v, upper):
    return jnp.concatenate([jnp.where(upper, 0.0, v), jnp.where(upper, v, 0.0)], 1).astype(BF16)


def send_of(code):
    return code >> SHIFT


def recv_of(code):
    return code & ((1 << SHIFT) - 1)


def folded(index, half):
    return jnp.where(index >= half, index - half, index)


def sides_of(count):
    return {16: (2, 2, 4), 64: (4, 4, 4)}.get(count, (count, 1, 1))


class Reducer:
    def __init__(self, count, rows):
        sides = sides_of(count)
        strides = (1, sides[0], sides[0] * sides[1])
        dims = list(zip(sides, strides))
        self.orders = (dims, [dims[1], dims[0], dims[2]])
        unit = 16 * count
        self.rows = -(-rows // unit) * unit

    def scratch(self):
        shapes = {"acc": pltpu.VMEM((self.rows, LAT), F32), "full": pltpu.VMEM((self.rows, LAT), F32)}
        copies = 0
        for half, order in enumerate(self.orders):
            length = self.rows // 2
            for stage, (k, _) in enumerate(order):
                length //= k
                shapes[f"slot{half}{stage}"] = pltpu.VMEM((max(k - 1, 1), length, LAT), F32)
                copies += k - 1
        shapes["send"] = pltpu.SemaphoreType.DMA((2 * copies,))
        shapes["recv"] = pltpu.SemaphoreType.DMA((2 * copies,))
        return shapes

    def bind(self, refs):
        self.refs = refs
        self.acc, self.full = refs["acc"], refs["full"]
        me = lax.axis_index("edge")
        self.begin = []
        self.length = []
        self.sems = {}
        used = 0
        for half, order in enumerate(self.orders):
            begin = [half * (self.rows // 2)]
            length = [self.rows // 2]
            for k, stride in order:
                length.append(length[-1] // k)
                begin.append(begin[-1] + ((me // stride) % k) * length[-1])
            self.begin.append(begin)
            self.length.append(length)
            for stage, (k, stride) in enumerate(order):
                for t in range(1, k):
                    for phase in range(2):
                        mine = (me // stride) % k
                        other = (mine + t) % k
                        self.sems[half, stage, phase, t] = (used, other, me + (other - mine) * stride)
                        used += 1

    def peers(self):
        order = self.orders[0]
        return [
            self.sems[0, stage, 0, t][2] for stage in range(3) for t in range(1, order[stage][0])
        ]

    def window(self, begin, length):
        return pl.ds(pl.multiple_of(begin, 8), length)

    def copies(self, half, stage, phase):
        k = self.orders[half][stage][0]
        out = []
        for t in range(1, k):
            at, other, device = self.sems[half, stage, phase, t]
            length = self.length[half][stage + 1]
            if phase == 0:
                rows = self.window(self.begin[half][stage] + other * length, length)
                source, target = self.acc.at[rows], self.refs[f"slot{half}{stage}"].at[t - 1]
            else:
                rows = self.window(self.begin[half][stage + 1], length)
                source = target = self.full.at[rows]
            out.append(
                pltpu.make_async_remote_copy(
                    src_ref=source,
                    dst_ref=target,
                    send_sem=self.refs["send"].at[at],
                    recv_sem=self.refs["recv"].at[at],
                    device_id={"edge": device},
                    device_id_type=MESH,
                )
            )
        return out

    def start(self, half, stage, phase):
        for one in self.copies(half, stage, phase):
            one.start()

    def wait(self, half, stage, phase):
        for one in self.copies(half, stage, phase):
            one.wait()
        if phase:
            return
        rows = self.window(self.begin[half][stage + 1], self.length[half][stage + 1])
        value = self.acc[rows, :]
        for t in range(1, self.orders[half][stage][0]):
            value = value + self.refs[f"slot{half}{stage}"][t - 1]
        if stage == 2:
            self.full[rows, :] = value
        else:
            self.acc[rows, :] = value

    SEQUENCE = ((0, 0), (1, 0), (2, 0), (2, 1), (1, 1), (0, 1))
    STEPS = len(SEQUENCE) + 1

    def step(self, index):
        for half in range(2):
            if index:
                self.wait(half, *self.SEQUENCE[index - 1])
            if index < len(self.SEQUENCE):
                self.start(half, *self.SEQUENCE[index])


PLACES = (
    (4, 5, 20, 21, 22, 23),
    (15, 18, 19, 16, 17, 11, 12, 13, 14),
    (6, 9, 10, 2, 3, 7, 8, 0, 1),
)
ROWS1 = 32
ROWS2 = 8
ROWS3 = 48


class Refs(dict):
    def __getattr__(self, name):
        return self[name]


def train_kernel(reducers, names, mats_count, rank, *refs):
    r = Refs(zip(names, refs))
    groups = []
    for i, reducer in enumerate(reducers):
        mark = f"sum{i}_"
        reducer.bind({k[len(mark) :]: v for k, v in r.items() if k.startswith(mark)})
        groups.append(reducer)
    first, second, third = groups
    own = r.feat.shape[1]
    count = r.code.shape[0] * LAT
    me = lax.axis_index("edge")
    last = lax.axis_size("edge") - 1
    has_left, has_right = me > 0, me < last
    sibling = {"rep": 1 - lax.axis_index("rep")}
    mats, vecs = r.mats, r.vecs
    ones = jnp.full((LAT, LAT), 1.0 / LAT, BF16)
    middle = pl.ds(own, own)

    def rows_of(which):
        base = ROWS0 + 5 * which
        return [vecs[base + i : base + i + 1, :] for i in range(5)]

    @pl.when(me == 0)
    def _():
        r.feat_wide[0] = jnp.zeros(r.feat.shape, F32)
        r.hb[0:own, :] = jnp.zeros((own, LAT), F32)
        r.rims[0] = jnp.zeros((own, LAT), F32)

    @pl.when(me == last)
    def _():
        r.feat_wide[2] = jnp.zeros(r.feat.shape, F32)
        r.hb[2 * own :, :] = jnp.zeros((own, LAT), F32)
        r.rims[1] = jnp.zeros((own, LAT), F32)

    barrier = pltpu.get_barrier_semaphore()

    around = [lax.rem(me + shift, last + 1) for shift in (1, last)]
    others = [{"edge": one} for one in first.peers() + around] + [sibling]
    for peer in others:
        pl.semaphore_signal(barrier, inc=1, device_id=peer, device_id_type=MESH)
    pl.semaphore_wait(barrier, len(others))

    def neighbours(at, up, up_target, down, down_target):
        def one(index, source, target, shift):
            return pltpu.make_async_remote_copy(
                src_ref=source,
                dst_ref=target,
                send_sem=r.halo_send.at[at + index],
                recv_sem=r.halo_recv.at[at + index],
                device_id={"edge": me + shift},
                device_id_type=MESH,
            )

        return one(0, up, up_target, 1), one(1, down, down_target, -1)

    def start(pair):
        @pl.when(has_right)
        def _():
            pair[0].start()

        @pl.when(has_left)
        def _():
            pair[1].start()

    def wait(pair):
        @pl.when(has_right)
        def _():
            pair[0].wait_send()
            pair[1].wait_recv()

        @pl.when(has_left)
        def _():
            pair[1].wait_send()
            pair[0].wait_recv()

    feats = neighbours(0, r.feat, r.feat_wide.at[0], r.feat, r.feat_wide.at[2])
    start(feats)

    def loop(body, during=None):
        def step(i, unused):
            if during is not None:
                for index in range(Reducer.STEPS):

                    @pl.when(i == index)
                    def _():
                        during.step(index)

            base = pl.multiple_of(i * (BLOCK // LAT), BLOCK // LAT)
            code = r.code[pl.ds(base, BLOCK // LAT), :]
            per = count // LAT
            planes = [r.x[pl.ds(base + p * per, BLOCK // LAT), :] for p in range(EFEAT)]
            parts = []
            for at in range(0, BLOCK, SUB):
                rows = pl.ds(pl.multiple_of(i * BLOCK + at, SUB), SUB)
                cut = slice(at // LAT, (at + SUB) // LAT)
                parts.append(body(rows, code[cut], [plane[cut] for plane in planes]))
            together(parts)
            return unused

        lax.fori_loop(0, count // BLOCK, step, 0)

    def features(planes):
        lines = [
            jnp.concatenate([plane[q : q + 1, :] for q in range(plane.shape[0])], 1)
            for plane in planes
        ]
        return jnp.concatenate(lines, 0)

    kept = [[r[f"{name}{i}"] for i in range(4)] for name in ("enc", "one", "two")]

    r.w[0] = stacked(0.5 * mats[2])
    r.w[1] = stacked(center(mats[3]))
    vec = rows_of(1)

    def encode(rows, code, planes):
        half = mm3(features(planes), 0.5 * vecs[LEAD:ROWS0, :], TN) + 0.5 * vec[0]
        yield
        out = yield from edge_tail(rows, half, kept[0], r.w[0], r.w[1], vec, ones)
        r.e0[rows, :] = out.astype(BF16)

    loop(encode)

    r.feat_wide[1] = r.feat[...]
    wait(feats)
    def particle_inputs():
        lines = jnp.concatenate([r.feat_wide[i] for i in range(3)], 1)
        types = lax.broadcasted_iota(jnp.int32, (NTYPES, 3 * own), 0).astype(F32)
        return lines[0:NFEAT], jnp.where(lines[NFEAT : NFEAT + 1] == types, 1.0, 0.0)

    lines, onehot = particle_inputs()
    pre = mm3(lines, vecs[0:NFEAT, :], TN) + mm3(onehot, vecs[NFEAT:LEAD, :], TN)
    out, saved = node_tail(pre, mats[0], mats[1], rows_of(0))
    r.h0[...] = out
    for j, v in enumerate(saved):
        r.node_kept[j] = v
    r.table[0 : 3 * own, :] = side_by_side(0.5 * mm3(out, mats[7]))
    r.table[3 * own :, :] = side_by_side(0.5 * mm3(out[own : 2 * own], mats[8]))

    def forward(step, e_in, e_out):
        base = 6 + 9 * step
        vec = rows_of(2 + 2 * step)
        r.w[0] = stacked(0.5 * mats[base])
        r.w[1] = stacked(0.5 * mats[base + 3])
        r.w[2] = stacked(center(mats[base + 4]))
        r.agg_wide[...] = jnp.zeros_like(r.agg_wide)

        def body(rows, code, planes):
            column = columns_of(code)
            e = e_in[rows, :]
            mask = pick_mask(send_of(column), 3 * own) + pick_mask(recv_of(column), own)
            half = joined(mm(jnp.concatenate(mask, 1), r.table[...]))
            half = half + mm(twice(e), r.w[0]) + 0.5 * vec[0]
            yield
            out = yield from edge_tail(rows, half, kept[1 + step], r.w[1], r.w[2], vec, ones)
            if e_out is not None:
                e_out[rows, :] = (e.astype(F32) + out).astype(BF16)
            r.agg_wide[...] += mm(add_mask(recv_of(code), own), side_by_side(out))

        loop(body)

    forward(0, r.e0, r.e1)
    h = r.h0[middle, :]
    agg = joined(r.agg_wide[...])
    r.agg0[...] = agg
    delta, saved = node_tail(mm3(h, mats[11]) + mm3(agg, mats[12]), mats[13], mats[14], rows_of(3))
    for j, v in enumerate(saved):
        r.step_kept[j] = v
    h = h + delta
    r.h1[...] = h
    r.hb[middle, :] = 0.5 * mm3(h, mats[16])
    mine = r.hb.at[middle]
    latents = neighbours(2, mine, r.hb.at[pl.ds(0, own)], mine, r.hb.at[pl.ds(2 * own, own)])
    start(latents)
    r.table[3 * own :, :] = side_by_side(0.5 * mm3(h, mats[17]))
    r.table[middle, :] = side_by_side(r.hb[middle, :])
    wait(latents)
    for i in (0, 2):
        r.table[i * own : (i + 1) * own, :] = side_by_side(r.hb[i * own : (i + 1) * own, :])

    forward(1, r.e1, None)

    def slot(group, places, which):
        at = places.index(which) * LAT
        return group.acc.at[pl.ds(at, LAT)]

    def put(group, places, which, value):
        slot(group, places, which)[...] = value

    def put_rows(group, places, at, rows):
        base = len(places) * LAT + at
        for v in rows:
            group.acc[base : base + v.shape[0], :] = v
            base += v.shape[0]
        return base

    put1, put2, put3 = (partial(put, group, places) for group, places in zip(groups, PLACES))
    agg = joined(r.agg_wide[...])
    h = r.h1[...]
    vec = rows_of(5)
    delta, saved = node_tail(mm3(h, mats[20]) + mm3(agg, mats[21]), mats[22], mats[23], vec)
    out = h + delta
    base = ROWS0 + 30
    s1, d1 = silu_half(0.5 * (mm3(out, mats[4]) + vecs[base : base + 1, :]))
    s2, d2 = silu_half(0.5 * (mm3(s1, mats[5]) + vecs[base + 1 : base + 2, :]))
    ends = vecs[base + 2 : base + 4, :]
    keep = r.keep[...]
    goal = r.goal[...]
    diff = mm3(ends, s2, NT) - goal
    kept_diff = diff * keep
    dpred = 2.0 * kept_diff
    dz2 = mm3(dpred, ends, TN) * d2
    dz1 = mm3(dz2, mats[5], NT) * d1
    d = mm3(dz1, mats[4], NT)
    dz, g_second, g_third, rows = node_tail_back(d, saved, mats[22], mats[23], vec)
    r.dh[...] = d + mm3(dz, mats[20], NT)
    r.dagg[...] = side_by_side(mm3(dz, mats[21], NT))
    put1(4, mm3(out, dz1, TN))
    put1(5, mm3(s1, dz2, TN))
    put1(20, mm3(h, dz, TN))
    put1(21, mm3(agg, dz, TN))
    put1(22, g_second)
    put1(23, g_third)
    rows = rows + [row_sum(dz1), row_sum(dz2), mm3(dpred, s2)]
    rows.append(jnp.zeros((7, LAT), F32))
    velocity = r.feat[8:10, :]
    for v in (
        kept_diff * diff,
        velocity * keep,
        velocity * velocity * keep,
        goal * keep,
        goal * goal * keep,
        jnp.broadcast_to(keep, velocity.shape),
    ):
        part = v[:, 0:LAT]
        for j in range(LAT, own, LAT):
            part = part + v[:, j : j + LAT]
        rows.append(part)
    end = put_rows(first, PLACES[0], 0, rows)
    first.acc[end:, :] = jnp.zeros((first.rows - end, LAT), F32)

    def zero(*targets):
        for target in targets:
            target[...] = jnp.zeros_like(target)

    def backward(step, group, places, e_ref, more, during):
        base = 6 + 9 * step
        grads = [slot(group, places, which) for which in (base, base + 3, base + 4)]
        for i, w in enumerate((mats[base], mats[base + 3], center(mats[base + 4]))):
            r.w[i] = stacked(jnp.transpose(w))
        zero(*grads, r.sums, r.recv_total, r.send_total)
        vec = rows_of(2 + 2 * step)

        def body(rows, code, planes):
            column = columns_of(code)
            recv = recv_of(column)
            d = joined(mm(jnp.concatenate(pick_mask(recv, own), 1), r.dagg[...]))
            if more is not None:
                de = r.de[rows, :].astype(F32)
                d = d + de
            yield
            dz1 = yield from edge_tail_back(
                rows, d, kept[1 + step], r.w[1], r.w[2], vec[3], ones, grads[1:], r.sums
            )
            dz1b = dz1.astype(BF16)
            grads[0][...] += mm(e_ref[rows, :], dz1b, TN)
            half = own // 2
            r.recv_total[...] += mm(
                add_mask(folded(recv_of(code), half), half), halves(dz1, recv >= half)
            )
            half = 3 * half
            r.send_total[...] += mm(
                add_mask(folded(send_of(code), half), half), halves(dz1, column >= (half << SHIFT))
            )
            back = mm(twice(dz1b), r.w[0])
            if more is None:
                r.de[rows, :] = back.astype(BF16)
            else:
                yield from more(rows, planes, de + back)

        loop(body, during)
        grads[2][...] = center(grads[2][...])

    backward(1, second, PLACES[1], r.e1, None, first)
    end = put_rows(second, PLACES[1], 0, finish_sums(r.sums))
    second.acc[end:, :] = jnp.zeros((second.rows - end, LAT), F32)
    r.spread[...] = unfold(r.send_total[...])
    rims = neighbours(
        4, r.spread.at[pl.ds(2 * own, own)], r.rims.at[0], r.spread.at[pl.ds(0, own)], r.rims.at[1]
    )
    start(rims)
    got = unfold(r.recv_total[...])
    h = r.h1[...]
    put2(17, mm3(h, got, TN))
    d = r.dh[...] + mm3(got, mats[17], NT)
    wait(rims)
    sent = r.spread[middle, :] + r.rims[0] + r.rims[1]
    put2(16, mm3(h, sent, TN))
    d = d + mm3(sent, mats[16], NT)
    saved = [r.step_kept[j] for j in range(4)]
    dz, g_second, g_third, rows = node_tail_back(d, saved, mats[13], mats[14], rows_of(3))
    put2(11, mm3(r.h0[middle, :], dz, TN))
    put2(12, mm3(r.agg0[...], dz, TN))
    put2(13, g_second)
    put2(14, g_third)
    put_rows(third, PLACES[2], 0, rows)
    r.dh[...] = d + mm3(dz, mats[11], NT)
    r.dagg[...] = side_by_side(mm3(dz, mats[12], NT))

    enc_grads = [slot(third, PLACES[2], which) for which in (2, 3)]
    zero(*enc_grads, r.enc_sums, r.we)
    r.w[3] = stacked(jnp.transpose(mats[2]))
    r.w[4] = stacked(jnp.transpose(center(mats[3])))

    def encoder_back(rows, planes, d):
        dz1 = yield from edge_tail_back(
            rows, d, kept[0], r.w[3], r.w[4], rows_of(1)[3], ones, enc_grads, r.enc_sums
        )
        r.we[...] += mm(features(planes).astype(BF16), dz1.astype(BF16))

    backward(0, third, PLACES[2], r.e0, encoder_back, second)
    enc_grads[1][...] = center(enc_grads[1][...])
    rows = finish_sums(r.sums) + finish_sums(r.enc_sums) + [r.we[...]]
    sent = unfold(r.send_total[...])
    got = unfold(r.recv_total[...])
    h = r.h0[...]
    put3(7, mm3(h, sent, TN))
    put3(8, mm3(h[own : 2 * own], got, TN))
    d = mm3(sent, mats[7], NT)
    inner = d[own : 2 * own] + r.dh[...] + mm3(got, mats[8], NT)
    d = jnp.concatenate([d[:own], inner, d[2 * own :]], 0)
    saved = [r.node_kept[j] for j in range(4)]
    dz, g_second, g_third, more = node_tail_back(d, saved, mats[0], mats[1], rows_of(0))
    put3(0, g_second)
    put3(1, g_third)
    lines, onehot = particle_inputs()
    rows = rows + more + [mm3(lines, dz), mm3(onehot, dz)]
    end = put_rows(third, PLACES[2], 5, rows)
    third.acc[end:, :] = jnp.zeros((third.rows - end, LAT), F32)

    def swap(at, source, target):
        return pltpu.make_async_remote_copy(
            src_ref=source,
            dst_ref=target,
            send_sem=r.pair_send.at[at],
            recv_sem=r.pair_recv.at[at],
            device_id=sibling,
            device_id_type=MESH,
        )

    def gradient(which):
        for group, places in zip(groups, PLACES):
            if which in places:
                return group.full[places.index(which) * LAT : (places.index(which) + 1) * LAT, :]
        return None

    def ranked(which):
        return slice(which * rank, (which + 1) * rank)

    third.step(0)
    r.small_mine[0:ROWS1, :] = first.full[6 * LAT : 6 * LAT + ROWS1, :]
    r.small_mine[ROWS1:, :] = second.full[9 * LAT : 9 * LAT + ROWS2, :]
    small = swap(0, r.small_mine, r.small_theirs)
    small.start()
    early = PLACES[0] + PLACES[1]
    for which in range(mats_count):
        r.projected[ranked(which), :] = mm3(r.factors[which], r.errors[which], NT)
    third.step(1)
    small.wait()
    small = r.small_mine[...] + r.small_theirs[...]
    r.small[0 : ROWS1 + ROWS2, :] = small
    at = 16 + 10
    scale = 1.0 / jnp.sum(small[at : at + 1, :], 1, keepdims=True)
    for which in early:
        total = gradient(which) * scale + r.errors[which]
        r.total[which] = total
    third.step(2)
    for which in early:
        r.projected[ranked(which), :] += scale * mm3(r.factors[which], gradient(which), NT)
    for index in range(3, Reducer.STEPS):
        third.step(index)
    for which in PLACES[2]:
        part = gradient(which)
        r.total[which] = part * scale + r.errors[which]
        r.projected[ranked(which), :] += scale * mm3(r.factors[which], part, NT)
    end = mats_count * rank
    r.projected[end:, :] = third.full[9 * LAT : 9 * LAT + ROWS3, :]
    both = swap(1, r.projected, r.projected_theirs)
    both.start()
    both.wait()
    r.small[ROWS1 + ROWS2 :, :] = r.projected[end:, :] + r.projected_theirs[end:, :]
    both = (r.projected[0:end, :] + r.projected_theirs[0:end, :]).reshape(mats_count, rank, LAT)
    columns = [both[:, i, :] for i in range(rank)]
    for i in range(rank):
        v = columns[i]
        v = v * lax.rsqrt(jnp.sum(v * v, 1, keepdims=True) + 1e-12)
        columns[i] = v
        for j in range(i + 1, rank):
            columns[j] = columns[j] - jnp.sum(v * columns[j], 1, keepdims=True) * v
    for i in range(rank):
        r.left[:, i, :] = columns[i]
    for which in range(mats_count):
        r.right_mine[ranked(which), :] = mm3(r.left[which], r.total[which])
    both = swap(2, r.right_mine, r.right_theirs)
    both.start()
    both.wait()
    r.right[...] = (r.right_mine[...] + r.right_theirs[...]).reshape(mats_count, rank, LAT)


def train(inputs, count_edge):
    own = inputs["feat"].shape[1]
    count = inputs["code"].shape[0] * LAT
    mats_count, rank, _ = inputs["factors"].shape
    reducers = [
        Reducer(count_edge, len(places) * LAT + rows)
        for places, rows in zip(PLACES, (ROWS1, ROWS2, ROWS3))
    ]
    flat = lambda *dims: pltpu.VMEM(dims, F32)
    half = lambda *dims: pltpu.VMEM(dims, BF16)
    small = ROWS1 + ROWS2 + ROWS3
    outs = {
        "total": (mats_count, LAT, LAT),
        "left": (mats_count, rank, LAT),
        "right": (mats_count, rank, LAT),
        "small": (small, LAT),
    }
    scratch = {
        "feat_wide": flat(3, *inputs["feat"].shape),
        "w": half(5, 2 * LAT, LAT),
        "h0": flat(3 * own, LAT),
        "node_kept": flat(4, 3 * own, LAT),
        "step_kept": flat(4, own, LAT),
        "table": half(4 * own, 2 * LAT),
        "dagg": half(own, 2 * LAT),
        "agg_wide": flat(own, 2 * LAT),
        "agg0": flat(own, LAT),
        "h1": flat(own, LAT),
        "hb": flat(3 * own, LAT),
        "dh": flat(own, LAT),
        "spread": flat(3 * own, LAT),
        "rims": flat(2, own, LAT),
        "recv_total": flat(own // 2, 2 * LAT),
        "send_total": flat(3 * own // 2, 2 * LAT),
        "sums": flat(5, 8, LAT),
        "enc_sums": flat(5, 8, LAT),
        "we": flat(EFEAT, LAT),
        "e0": half(count, LAT),
        "e1": half(count, LAT),
        "de": half(count, LAT),
        "small_mine": flat(ROWS1 + ROWS2, LAT),
        "small_theirs": flat(ROWS1 + ROWS2, LAT),
        "projected": flat(mats_count * rank + ROWS3, LAT),
        "projected_theirs": flat(mats_count * rank + ROWS3, LAT),
        "right_mine": flat(mats_count * rank, LAT),
        "right_theirs": flat(mats_count * rank, LAT),
        "halo_send": pltpu.SemaphoreType.DMA((6,)),
        "halo_recv": pltpu.SemaphoreType.DMA((6,)),
        "pair_send": pltpu.SemaphoreType.DMA((3,)),
        "pair_recv": pltpu.SemaphoreType.DMA((3,)),
    }
    for name in ("enc", "one", "two"):
        for i in range(4):
            scratch[f"{name}{i}"] = half(count, LAT)
    for i, reducer in enumerate(reducers):
        for name, shape in reducer.scratch().items():
            scratch[f"sum{i}_{name}"] = shape
    vmem = pl.BlockSpec(memory_space=pltpu.VMEM)
    names = list(inputs) + list(outs) + list(scratch)
    return pl.pallas_call(
        partial(train_kernel, reducers, names, mats_count, rank),
        in_specs=[vmem] * len(inputs),
        out_specs=[vmem] * len(outs),
        out_shape=[jax.ShapeDtypeStruct(shape, F32) for shape in outs.values()],
        scratch_shapes=list(scratch.values()),
        compiler_params=pltpu.CompilerParams(
            collective_id=0, has_side_effects=True, vmem_limit_bytes=VMEM_LIMIT
        ),
    )(*inputs.values())


VMEM_LIMIT = 62 << 20


def finish_kernel(total, left, right, small, mats, momentum, vecs, vecs_momentum, *outs):
    new_mats, new_momentum, new_errors, new_vecs, new_vecs_momentum, loss, kept_count, stats = outs
    for k in range(total.shape[0]):
        approx = mm3(left[k], right[k], TN)
        moved = 0.9 * momentum[k] + approx
        new_momentum[k] = moved
        new_mats[k] = mats[k] - 4.0 * moved
        new_errors[k] = total[k] - approx

    @pl.when(pl.program_id(0) == 0)
    def _():
        sums = jnp.sum(small[16:28, :], 1, keepdims=True)
        kept = sums[10:11]
        scale = 1.0 / kept
        loss[...] = sums[0:1] + sums[1:2]
        kept_count[...] = kept
        stats[...] = sums[2:10] * scale
        late = ROWS1 + ROWS2
        cuts = (
            (late + 23, 23), (late + 15, 3), (late + 18, 5), (late + 10, 5), (late + 5, 5),
            (late, 5), (ROWS1, 5), (0, 9),
        )
        grads = jnp.concatenate([small[at : at + length, :] for at, length in cuts], 0)
        moved = 0.9 * vecs_momentum[...] + grads * scale
        new_vecs_momentum[...] = moved
        new_vecs[...] = vecs[...] - 4.0 * moved


def finish(total, left, right, small, mats, momentum, vecs, vecs_momentum):
    group = 6
    big = pl.BlockSpec((group, LAT, LAT), lambda i: (i, 0, 0))
    thin = pl.BlockSpec((group,) + left.shape[1:], lambda i: (i, 0, 0))
    whole = lambda shape: pl.BlockSpec(shape, lambda i: (0,) * len(shape))
    shape = lambda *dims: jax.ShapeDtypeStruct(dims, F32)
    return pl.pallas_call(
        finish_kernel,
        grid=(total.shape[0] // group,),
        in_specs=[big, thin, thin, whole(small.shape), big, big]
        + [whole(vecs.shape), whole(vecs.shape)],
        out_specs=[big] * 3 + [whole(vecs.shape)] * 2 + [whole((1, 1))] * 2 + [whole((8, 1))],
        out_shape=[shape(*total.shape)] * 3
        + [shape(*vecs.shape)] * 2
        + [shape(1, 1), shape(1, 1), shape(8, 1)],
    )(total, left, right, small, mats, momentum, vecs, vecs_momentum)


def shards(
    node_feat, node_types, boundary, target, edge_feat, senders, receivers, edge_counts, mats, vecs,
    mats_momentum, vecs_momentum, factors, errors,
):
    own = node_feat.shape[1]
    count = senders.shape[1]
    place = lax.axis_index("edge")
    lines = (count // LAT, LAT)
    slots = jnp.arange(count, dtype=jnp.int32).reshape(lines)
    send = senders.reshape(lines) - (place - 1) * own
    recv = receivers.reshape(lines) - place * own
    live = slots < edge_counts[0, 0]
    code = jnp.where(live, (send << SHIFT) + recv, (2047 << SHIFT) + 1023)
    feat = jnp.concatenate(
        [node_feat[0].T, node_types.astype(F32), jnp.zeros((1, own), F32)], 0
    )
    inputs = {
        "code": code,
        "x": edge_feat[0].T.reshape(EFEAT * lines[0], LAT),
        "feat": feat,
        "keep": (1 - boundary).astype(F32),
        "goal": target[0].T,
        "mats": mats,
        "vecs": vecs,
        "factors": jnp.swapaxes(factors, 1, 2),
        "errors": errors[0],
    }
    total, left, right, small = train(inputs, lax.axis_size("edge"))
    new_mats, mats_mom, new_errors, new_vecs, vecs_mom, loss, kept, stats = finish(
        total, left, right, small, mats, mats_momentum, vecs, vecs_momentum
    )
    return (
        loss.reshape(()),
        kept.reshape(()),
        stats.reshape(4, 2),
        new_mats,
        mats_mom,
        jnp.swapaxes(right, 1, 2),
        new_errors[None],
        new_vecs,
        vecs_mom,
    )


def solution(mesh):
    placed = (
        P("rep", "edge", None),
        P("rep", "edge"),
        P("rep", "edge"),
        P("rep", "edge", None),
        P("rep", "edge", None),
        P("rep", "edge"),
        P("rep", "edge"),
        P("rep", "edge"),
        P(),
        P(),
        P(),
        P(),
        P(),
        P("rep", None, None, None),
    )
    return jax.shard_map(
        shards,
        mesh=mesh,
        in_specs=placed,
        out_specs=(P(), P(), P(), P(), P(), P(), P("rep", None, None, None), P(), P()),
        check_vma=False,
    )
```

```python
from functools import partial

import jax
import jax.numpy as jnp
from jax import lax
from jax.experimental import pallas as pl
from jax.experimental.pallas import tpu as pltpu
from jax.sharding import PartitionSpec as P

NFEAT = 14
NTYPES = 9
EFEAT = 3
LEAD = NFEAT + NTYPES
ROWS0 = LEAD + EFEAT
LAT = 128
BLOCK = 2048
SUB = 512
SHIFT = 12
F32 = jnp.float32
BF16 = jnp.bfloat16
MESH = pl.DeviceIdType.MESH
NN = (((1,), (0,)), ((), ()))
NT = (((1,), (1,)), ((), ()))
TN = (((0,), (0,)), ((), ()))


def mm(a, b, dims=NN):
    return lax.dot_general(a, b, dims, preferred_element_type=F32)


def split(w):
    hi = w.astype(BF16)
    return hi, (w - hi.astype(F32)).astype(BF16)


def twice(a):
    return jnp.concatenate([a, a], 1)


def stacked(w):
    return jnp.concatenate(split(w), 0)


def side_by_side(v):
    return jnp.concatenate(split(v), 1)


def joined(wide):
    return wide[:, :LAT] + wide[:, LAT:]


def mm3(a, b, dims=NN):
    ah, al = split(a)
    bh, bl = split(b)
    return mm(ah, bh, dims) + (mm(ah, bl, dims) + mm(al, bh, dims))


def silu_half(half):
    up = 1.0 + jnp.tanh(half)
    value = half * up
    sig = 0.5 * up
    return value, sig + value - value * sig


def mean_last(v):
    return jnp.mean(v, -1, keepdims=True)


def center(w):
    return w - mean_last(w)


def fold_rows(v):
    total = v[0:8]
    for i in range(8, v.shape[0], 8):
        total = total + v[i : i + 8]
    return total


def row_sum(v):
    return jnp.sum(fold_rows(v), 0, keepdims=True)


def unfold(v):
    return jnp.concatenate([v[:, :LAT], v[:, LAT:]], 0)


def together(parts):
    parts = list(parts)
    while parts:
        for part in list(parts):
            try:
                next(part)
            except StopIteration:
                parts.remove(part)


def node_tail(first, second, third, vec):
    b1, b2, b3, g, o = vec
    half1 = 0.5 * (first + b1)
    half2 = 0.5 * (mm3(silu_half(half1)[0], second) + b2)
    z = mm3(silu_half(half2)[0], third) + b3
    c = z - mean_last(z)
    inv = lax.rsqrt(mean_last(c * c) + 1e-05)
    xhat = c * inv
    return xhat * g + o, (half1, half2, xhat, jnp.broadcast_to(inv, xhat.shape))


def node_tail_back(d, kept, second, third, vec):
    half1, half2, xhat, inv = kept
    s1, d1 = silu_half(half1)
    s2, d2 = silu_half(half2)
    dy = d * vec[3]
    dz3 = inv * (dy - mean_last(dy) - xhat * mean_last(dy * xhat))
    dz2 = mm3(dz3, third, NT) * d2
    dz1 = mm3(dz2, second, NT) * d1
    rows = [row_sum(v) for v in (dz1, dz2, dz3, d * xhat, d)]
    return dz1, mm3(s1, dz2, TN), mm3(s2, dz3, TN), rows


def edge_tail(rows, half, kept, second, third, vec, ones):
    _, b2, b3, g, o = vec
    kept[0][rows, :] = half.astype(BF16)
    s1 = silu_half(half)[0].astype(BF16)
    half = mm(twice(s1), second) + 0.5 * b2
    yield
    kept[1][rows, :] = half.astype(BF16)
    s2 = silu_half(half)[0].astype(BF16)
    c = mm(twice(s2), third) + center(b3)
    yield
    inv = lax.rsqrt(mm((c * c).astype(BF16), ones) + 1e-05)
    xhat = c * inv
    kept[2][rows, :] = xhat.astype(BF16)
    kept[3][rows, :] = inv.astype(BF16)
    return xhat * g + o


def edge_tail_back(rows, d, kept, second, third, g, ones, grads, sums):
    xhat = kept[2][rows, :].astype(F32)
    inv = kept[3][rows, :].astype(F32)
    dx = d * xhat
    dc = inv * (d * g - xhat * mm((dx * g).astype(BF16), ones))
    dcb = dc.astype(BF16)
    for at, v in ((2, dc), (3, dx), (4, d)):
        sums[at] += fold_rows(v)
    yield
    s2, d2 = silu_half(kept[1][rows, :].astype(F32))
    dz2 = mm(twice(dcb), third) * d2
    grads[1][...] += mm(s2.astype(BF16), dcb, TN)
    sums[1] += fold_rows(dz2)
    dz2b = dz2.astype(BF16)
    yield
    s1, d1 = silu_half(kept[0][rows, :].astype(F32))
    dz1 = mm(twice(dz2b), second) * d1
    grads[0][...] += mm(s1.astype(BF16), dz2b, TN)
    sums[0] += fold_rows(dz1)
    yield
    return dz1


def finish_sums(sums):
    rows = [jnp.sum(sums[i], 0, keepdims=True) for i in range(5)]
    rows[2] = center(rows[2])
    return rows


def columns_of(code):
    parts = [
        jnp.transpose(jnp.broadcast_to(code[q : q + 1, :], (LAT, LAT))) for q in range(code.shape[0])
    ]
    return jnp.concatenate(parts, 0)


def pick_mask(column, count):
    lanes = lax.broadcasted_iota(jnp.int32, (column.shape[0], LAT), 1)
    return [jnp.where(column == lanes + LAT * j, 1.0, 0.0).astype(BF16) for j in range(count // LAT)]


def add_mask(row, count):
    down = lax.broadcasted_iota(jnp.int32, (count, LAT), 0)
    parts = [
        jnp.where(row[q : q + 1, :] == down, 1.0, 0.0).astype(BF16) for q in range(row.shape[0])
    ]
    return jnp.concatenate(parts, 1)


def halves(v, upper):
    return jnp.concatenate([jnp.where(upper, 0.0, v), jnp.where(upper, v, 0.0)], 1).astype(BF16)


def send_of(code):
    return code >> SHIFT


def recv_of(code):
    return code & ((1 << SHIFT) - 1)


def folded(index, half):
    return jnp.where(index >= half, index - half, index)


def orders_of(count):
    if count == 16:
        near, far = (4, 1), (4, 4)
        return [[near, far], [far, near]]
    if count == 64:
        a, b, c = (4, 1), (4, 4), (4, 16)
        return [[a, b, c], [b, c, a]]
    return [[(count, 1)], [(count, 1)]]


class Reducer:
    def __init__(self, count, rows):
        self.orders = orders_of(count)
        unit = 8 * count
        units = max(-(-rows // unit), 2)
        self.rows = units * unit
        near = min(max(round(units * 2 / 3), 1), units - 1) * unit
        self.parts = ((0, near), (near, self.rows - near))
        stages = len(self.orders[0])
        self.sequence = [(i, 0) for i in range(stages)] + [(i, 1) for i in reversed(range(stages))]
        self.steps = len(self.sequence) + 1

    def scratch(self):
        shapes = {"acc": pltpu.VMEM((self.rows, LAT), F32), "full": pltpu.VMEM((self.rows, LAT), F32)}
        copies = 0
        for half, order in enumerate(self.orders):
            length = self.parts[half][1]
            for stage, (k, _) in enumerate(order):
                length //= k
                shapes[f"slot{half}{stage}"] = pltpu.VMEM((max(k - 1, 1), length, LAT), F32)
                copies += k - 1
        shapes["send"] = pltpu.SemaphoreType.DMA((2 * copies,))
        shapes["recv"] = pltpu.SemaphoreType.DMA((2 * copies,))
        return shapes

    def bind(self, refs):
        self.refs = refs
        self.acc, self.full = refs["acc"], refs["full"]
        me = lax.axis_index("edge")
        self.begin = []
        self.length = []
        self.sems = {}
        used = 0
        for half, order in enumerate(self.orders):
            begin = [self.parts[half][0]]
            length = [self.parts[half][1]]
            for k, stride in order:
                length.append(length[-1] // k)
                begin.append(begin[-1] + ((me // stride) % k) * length[-1])
            self.begin.append(begin)
            self.length.append(length)
            for stage, (k, stride) in enumerate(order):
                for t in range(1, k):
                    for phase in range(2):
                        mine = (me // stride) % k
                        other = (mine + t) % k
                        self.sems[half, stage, phase, t] = (used, other, me + (other - mine) * stride)
                        used += 1

    def peers(self):
        order = self.orders[0]
        return [
            self.sems[0, stage, 0, t][2]
            for stage in range(len(order))
            for t in range(1, order[stage][0])
        ]

    def window(self, begin, length):
        return pl.ds(pl.multiple_of(begin, 8), length)

    def copies(self, half, stage, phase):
        k = self.orders[half][stage][0]
        out = []
        for t in range(1, k):
            at, other, device = self.sems[half, stage, phase, t]
            length = self.length[half][stage + 1]
            if phase == 0:
                rows = self.window(self.begin[half][stage] + other * length, length)
                source, target = self.acc.at[rows], self.refs[f"slot{half}{stage}"].at[t - 1]
            else:
                rows = self.window(self.begin[half][stage + 1], length)
                source = target = self.full.at[rows]
            out.append(
                pltpu.make_async_remote_copy(
                    src_ref=source,
                    dst_ref=target,
                    send_sem=self.refs["send"].at[at],
                    recv_sem=self.refs["recv"].at[at],
                    device_id={"edge": device},
                    device_id_type=MESH,
                )
            )
        return out

    def start(self, half, stage, phase):
        for one in self.copies(half, stage, phase):
            one.start()

    def wait(self, half, stage, phase):
        for one in self.copies(half, stage, phase):
            one.wait()
        if phase:
            return
        rows = self.window(self.begin[half][stage + 1], self.length[half][stage + 1])
        value = self.acc[rows, :]
        for t in range(1, self.orders[half][stage][0]):
            value = value + self.refs[f"slot{half}{stage}"][t - 1]
        if stage == len(self.orders[half]) - 1:
            self.full[rows, :] = value
        else:
            self.acc[rows, :] = value

    def step(self, index):
        for half in range(2):
            if index:
                self.wait(half, *self.sequence[index - 1])
            if index < len(self.sequence):
                self.start(half, *self.sequence[index])


PLACES = (
    (4, 5, 20, 21, 22, 23),
    (15, 18, 19, 16, 17, 11, 12, 13, 14),
    (6, 9, 10, 7, 8, 0, 1),
    (2, 3),
)
ROWS = (32, 8, 48, 8)
STARTS = tuple(sum(ROWS[:i]) for i in range(5))


class Refs(dict):
    def __getattr__(self, name):
        return self[name]


def train_kernel(reducers, names, mats_count, rank, *refs):
    r = Refs(zip(names, refs))
    groups = []
    for i, reducer in enumerate(reducers):
        mark = f"sum{i}_"
        reducer.bind({k[len(mark) :]: v for k, v in r.items() if k.startswith(mark)})
        groups.append(reducer)
    first, second, third, fourth = groups
    own = r.feat.shape[1]
    count = r.code.shape[0] * LAT
    me = lax.axis_index("edge")
    last = lax.axis_size("edge") - 1
    has_left, has_right = me > 0, me < last
    sibling = {"rep": 1 - lax.axis_index("rep")}
    mats, vecs = r.mats, r.vecs
    ones = jnp.full((LAT, LAT), 1.0 / LAT, BF16)
    middle = pl.ds(own, own)
    r["spread"] = r.hb
    r["agg_wide"] = r.send_total.at[pl.ds(0, own)]

    def rows_of(which):
        base = ROWS0 + 5 * which
        return [vecs[base + i : base + i + 1, :] for i in range(5)]

    @pl.when(me == 0)
    def _():
        r.feat_wide[0] = jnp.zeros(r.feat.shape, F32)
        r.hb[0:own, :] = jnp.zeros((own, LAT), F32)
        r.rims[0] = jnp.zeros((own, LAT), F32)

    @pl.when(me == last)
    def _():
        r.feat_wide[2] = jnp.zeros(r.feat.shape, F32)
        r.hb[2 * own :, :] = jnp.zeros((own, LAT), F32)
        r.rims[1] = jnp.zeros((own, LAT), F32)

    barrier = pltpu.get_barrier_semaphore()

    around = [lax.rem(me + shift, last + 1) for shift in (1, last)]
    others = [{"edge": one} for one in first.peers() + around] + [sibling]
    for peer in others:
        pl.semaphore_signal(barrier, inc=1, device_id=peer, device_id_type=MESH)
    pl.semaphore_wait(barrier, len(others))

    def neighbours(at, up, up_target, down, down_target):
        def one(index, source, target, shift):
            return pltpu.make_async_remote_copy(
                src_ref=source,
                dst_ref=target,
                send_sem=r.halo_send.at[at + index],
                recv_sem=r.halo_recv.at[at + index],
                device_id={"edge": me + shift},
                device_id_type=MESH,
            )

        return one(0, up, up_target, 1), one(1, down, down_target, -1)

    def start(pair):
        @pl.when(has_right)
        def _():
            pair[0].start()

        @pl.when(has_left)
        def _():
            pair[1].start()

    def wait(pair):
        @pl.when(has_right)
        def _():
            pair[0].wait_send()
            pair[1].wait_recv()

        @pl.when(has_left)
        def _():
            pair[1].wait_send()
            pair[0].wait_recv()

    feats = neighbours(0, r.feat, r.feat_wide.at[0], r.feat, r.feat_wide.at[2])
    start(feats)

    def loop(body, during=None, every=1):
        turns = count // BLOCK

        def step(i, unused):
            if during is not None:
                for index in range(0, turns, every):

                    @pl.when(i == index)
                    def _():
                        during.step(index // every)

            base = pl.multiple_of(i * (BLOCK // LAT), BLOCK // LAT)
            code = r.code[pl.ds(base, BLOCK // LAT), :]
            per = count // LAT
            planes = [r.x[pl.ds(base + p * per, BLOCK // LAT), :] for p in range(EFEAT)]
            parts = []
            for at in range(0, BLOCK, SUB):
                rows = pl.ds(pl.multiple_of(i * BLOCK + at, SUB), SUB)
                cut = slice(at // LAT, (at + SUB) // LAT)
                parts.append(body(rows, code[cut], [plane[cut] for plane in planes]))
            together(parts)
            return unused

        lax.fori_loop(0, count // BLOCK, step, 0)

    def features(planes):
        lines = [
            jnp.concatenate([plane[q : q + 1, :] for q in range(plane.shape[0])], 1)
            for plane in planes
        ]
        return jnp.concatenate(lines, 0)

    kept = [[r[f"{name}{i}"] for i in range(4)] for name in ("enc", "one", "two")]

    r.w[0] = stacked(0.5 * mats[2])
    r.w[1] = stacked(center(mats[3]))
    vec = rows_of(1)

    def encode(rows, code, planes):
        half = mm3(features(planes), 0.5 * vecs[LEAD:ROWS0, :], TN) + 0.5 * vec[0]
        yield
        out = yield from edge_tail(rows, half, kept[0], r.w[0], r.w[1], vec, ones)
        r.e0[rows, :] = out.astype(BF16)

    loop(encode)

    r.feat_wide[1] = r.feat[...]
    wait(feats)
    def particle_inputs():
        lines = jnp.concatenate([r.feat_wide[i] for i in range(3)], 1)
        types = lax.broadcasted_iota(jnp.int32, (NTYPES, 3 * own), 0).astype(F32)
        return lines[0:NFEAT], jnp.where(lines[NFEAT : NFEAT + 1] == types, 1.0, 0.0)

    lines, onehot = particle_inputs()
    pre = mm3(lines, vecs[0:NFEAT, :], TN) + mm3(onehot, vecs[NFEAT:LEAD, :], TN)
    out, saved = node_tail(pre, mats[0], mats[1], rows_of(0))
    r.h0[...] = out
    for j, v in enumerate(saved):
        r.node_kept[j] = v
    r.table[0 : 3 * own, :] = side_by_side(0.5 * mm3(out, mats[7]))
    r.table[3 * own :, :] = side_by_side(0.5 * mm3(out[own : 2 * own], mats[8]))

    def forward(step, e_in, e_out):
        base = 6 + 9 * step
        vec = rows_of(2 + 2 * step)
        r.w[0] = stacked(0.5 * mats[base])
        r.w[1] = stacked(0.5 * mats[base + 3])
        r.w[2] = stacked(center(mats[base + 4]))
        r.agg_wide[...] = jnp.zeros_like(r.agg_wide)

        def body(rows, code, planes):
            column = columns_of(code)
            e = e_in[rows, :]
            mask = pick_mask(send_of(column), 3 * own) + pick_mask(recv_of(column), own)
            half = joined(mm(jnp.concatenate(mask, 1), r.table[...]))
            half = half + mm(twice(e), r.w[0]) + 0.5 * vec[0]
            yield
            out = yield from edge_tail(rows, half, kept[1 + step], r.w[1], r.w[2], vec, ones)
            if e_out is not None:
                e_out[rows, :] = (e.astype(F32) + out).astype(BF16)
            r.agg_wide[...] += mm(add_mask(recv_of(code), own), side_by_side(out))

        loop(body)

    forward(0, r.e0, r.e1)
    h = r.h0[middle, :]
    agg = joined(r.agg_wide[...])
    r.agg0[...] = agg
    delta, saved = node_tail(mm3(h, mats[11]) + mm3(agg, mats[12]), mats[13], mats[14], rows_of(3))
    for j, v in enumerate(saved):
        r.step_kept[j] = v
    h = h + delta
    r.h1[...] = h
    r.hb[middle, :] = 0.5 * mm3(h, mats[16])
    mine = r.hb.at[middle]
    latents = neighbours(2, mine, r.hb.at[pl.ds(0, own)], mine, r.hb.at[pl.ds(2 * own, own)])
    start(latents)
    r.table[3 * own :, :] = side_by_side(0.5 * mm3(h, mats[17]))
    r.table[middle, :] = side_by_side(r.hb[middle, :])
    wait(latents)
    for i in (0, 2):
        r.table[i * own : (i + 1) * own, :] = side_by_side(r.hb[i * own : (i + 1) * own, :])

    forward(1, r.e1, None)

    def slot(group, places, which):
        at = places.index(which) * LAT
        return group.acc.at[pl.ds(at, LAT)]

    def put(group, places, which, value):
        slot(group, places, which)[...] = value

    def put_rows(group, places, at, rows):
        base = len(places) * LAT + at
        for v in rows:
            group.acc[base : base + v.shape[0], :] = v
            base += v.shape[0]
        return base

    def finish_step(group, at):
        for index in range(at, group.steps):
            group.step(index)

    put1, put2, put3, _ = (partial(put, group, places) for group, places in zip(groups, PLACES))
    agg = joined(r.agg_wide[...])
    h = r.h1[...]
    vec = rows_of(5)
    delta, saved = node_tail(mm3(h, mats[20]) + mm3(agg, mats[21]), mats[22], mats[23], vec)
    out = h + delta
    base = ROWS0 + 30
    s1, d1 = silu_half(0.5 * (mm3(out, mats[4]) + vecs[base : base + 1, :]))
    s2, d2 = silu_half(0.5 * (mm3(s1, mats[5]) + vecs[base + 1 : base + 2, :]))
    ends = vecs[base + 2 : base + 4, :]
    keep = r.keep[...]
    goal = r.goal[...]
    diff = mm3(ends, s2, NT) - goal
    kept_diff = diff * keep
    dpred = 2.0 * kept_diff
    dz2 = mm3(dpred, ends, TN) * d2
    dz1 = mm3(dz2, mats[5], NT) * d1
    d = mm3(dz1, mats[4], NT)
    dz, g_second, g_third, rows = node_tail_back(d, saved, mats[22], mats[23], vec)
    r.dh[...] = d + mm3(dz, mats[20], NT)
    r.dagg[...] = side_by_side(mm3(dz, mats[21], NT))
    put1(4, mm3(out, dz1, TN))
    put1(5, mm3(s1, dz2, TN))
    put1(20, mm3(h, dz, TN))
    put1(21, mm3(agg, dz, TN))
    put1(22, g_second)
    put1(23, g_third)
    rows = rows + [row_sum(dz1), row_sum(dz2), mm3(dpred, s2)]
    rows.append(jnp.zeros((7, LAT), F32))
    velocity = r.feat[8:10, :]
    for v in (
        kept_diff * diff,
        velocity * keep,
        velocity * velocity * keep,
        goal * keep,
        goal * goal * keep,
        jnp.broadcast_to(keep, velocity.shape),
    ):
        part = v[:, 0:LAT]
        for j in range(LAT, own, LAT):
            part = part + v[:, j : j + LAT]
        rows.append(part)
    end = put_rows(first, PLACES[0], 0, rows)
    first.acc[end:, :] = jnp.zeros((first.rows - end, LAT), F32)

    def zero(*targets):
        for target in targets:
            target[...] = jnp.zeros_like(target)

    def backward(step, group, places, e_ref, residual, during):
        base = 6 + 9 * step
        grads = [slot(group, places, which) for which in (base, base + 3, base + 4)]
        for i, w in enumerate((mats[base], mats[base + 3], center(mats[base + 4]))):
            r.w[i] = stacked(jnp.transpose(w))
        zero(*grads, r.sums, r.recv_total, r.send_total)
        vec = rows_of(2 + 2 * step)

        def body(rows, code, planes):
            column = columns_of(code)
            recv = recv_of(column)
            d = joined(mm(jnp.concatenate(pick_mask(recv, own), 1), r.dagg[...]))
            if residual:
                de = r.de[rows, :].astype(F32)
                d = d + de
            yield
            dz1 = yield from edge_tail_back(
                rows, d, kept[1 + step], r.w[1], r.w[2], vec[3], ones, grads[1:], r.sums
            )
            dz1b = dz1.astype(BF16)
            grads[0][...] += mm(e_ref[rows, :], dz1b, TN)
            half = own // 2
            r.recv_total[...] += mm(
                add_mask(folded(recv_of(code), half), half), halves(dz1, recv >= half)
            )
            half = 3 * half
            r.send_total[...] += mm(
                add_mask(folded(send_of(code), half), half), halves(dz1, column >= (half << SHIFT))
            )
            back = mm(twice(dz1b), r.w[0])
            if residual:
                back = de + back
            r.de[rows, :] = back.astype(BF16)

        loop(body, during)
        grads[2][...] = center(grads[2][...])

    backward(1, second, PLACES[1], r.e1, False, first)
    end = put_rows(second, PLACES[1], 0, finish_sums(r.sums))
    second.acc[end:, :] = jnp.zeros((second.rows - end, LAT), F32)
    r.spread[...] = unfold(r.send_total[...])
    rims = neighbours(
        4, r.spread.at[pl.ds(2 * own, own)], r.rims.at[0], r.spread.at[pl.ds(0, own)], r.rims.at[1]
    )
    start(rims)
    done = count // BLOCK
    finish_step(first, done)
    got = unfold(r.recv_total[...])
    h = r.h1[...]
    put2(17, mm3(h, got, TN))
    d = r.dh[...] + mm3(got, mats[17], NT)
    wait(rims)
    sent = r.spread[middle, :] + r.rims[0] + r.rims[1]
    put2(16, mm3(h, sent, TN))
    d = d + mm3(sent, mats[16], NT)
    saved = [r.step_kept[j] for j in range(4)]
    dz, g_second, g_third, rows = node_tail_back(d, saved, mats[13], mats[14], rows_of(3))
    put2(11, mm3(r.h0[middle, :], dz, TN))
    put2(12, mm3(r.agg0[...], dz, TN))
    put2(13, g_second)
    put2(14, g_third)
    put_rows(third, PLACES[2], 0, rows)
    r.dh[...] = d + mm3(dz, mats[11], NT)
    r.dagg[...] = side_by_side(mm3(dz, mats[12], NT))

    backward(0, third, PLACES[2], r.e0, True, second)
    sent = unfold(r.send_total[...])
    got = unfold(r.recv_total[...])
    h = r.h0[...]
    put3(7, mm3(h, sent, TN))
    put3(8, mm3(h[own : 2 * own], got, TN))
    d = mm3(sent, mats[7], NT)
    inner = d[own : 2 * own] + r.dh[...] + mm3(got, mats[8], NT)
    d = jnp.concatenate([d[:own], inner, d[2 * own :]], 0)
    saved = [r.node_kept[j] for j in range(4)]
    dz, g_second, g_third, more = node_tail_back(d, saved, mats[0], mats[1], rows_of(0))
    put3(0, g_second)
    put3(1, g_third)
    lines, onehot = particle_inputs()
    rows = finish_sums(r.sums) + more + [mm3(lines, dz), mm3(onehot, dz)]
    end = put_rows(third, PLACES[2], 5, rows)
    third.acc[end:, :] = jnp.zeros((third.rows - end, LAT), F32)
    third.step(0)
    finish_step(second, done)

    enc_grads = [slot(fourth, PLACES[3], which) for which in PLACES[3]]
    zero(*enc_grads, r.sums, r.we)
    r.w[0] = stacked(jnp.transpose(mats[2]))
    r.w[1] = stacked(jnp.transpose(center(mats[3])))
    gain = rows_of(1)[3]

    def encoder_back(rows, code, planes):
        d = r.de[rows, :].astype(F32)
        dz1 = yield from edge_tail_back(
            rows, d, kept[0], r.w[0], r.w[1], gain, ones, enc_grads, r.sums
        )
        r.we[...] += mm(features(planes).astype(BF16), dz1.astype(BF16))

    loop(encoder_back)
    enc_grads[1][...] = center(enc_grads[1][...])
    end = put_rows(fourth, PLACES[3], 0, finish_sums(r.sums) + [r.we[...]])
    fourth.acc[end:, :] = jnp.zeros((fourth.rows - end, LAT), F32)

    def swap(at, source, target):
        return pltpu.make_async_remote_copy(
            src_ref=source,
            dst_ref=target,
            send_sem=r.pair_send.at[at],
            recv_sem=r.pair_recv.at[at],
            device_id=sibling,
            device_id_type=MESH,
        )

    def gradient(which):
        for group, places in zip(groups, PLACES):
            if which in places:
                return group.full[places.index(which) * LAT : (places.index(which) + 1) * LAT, :]
        return None

    def ranked(which):
        return slice(which * rank, (which + 1) * rank)

    third.step(1)
    fourth.step(0)
    for group, places, at, size in zip(groups[:2], PLACES, STARTS, ROWS):
        base = len(places) * LAT
        r.small_mine[at : at + size, :] = group.full[base : base + size, :]
    small = swap(0, r.small_mine, r.small_theirs)
    small.start()
    for which in range(mats_count):
        r.projected[ranked(which), :] = mm3(r.factors[which], r.errors[which], NT)
    small.wait()
    small = r.small_mine[...] + r.small_theirs[...]
    r.small[0 : STARTS[2], :] = small
    at = 16 + 10
    scale = 1.0 / jnp.sum(small[at : at + 1, :], 1, keepdims=True)

    def take(chosen):
        for which in chosen:
            part = gradient(which)
            r.total[which] = part * scale + r.errors[which]
            r.projected[ranked(which), :] += scale * mm3(r.factors[which], part, NT)

    third.step(2)
    fourth.step(1)
    take(PLACES[0])
    for index in range(3, third.steps):
        third.step(index)
        fourth.step(index - 1)
        if index == 3:
            take(PLACES[1])
    take(PLACES[2])
    finish_step(fourth, third.steps - 1)
    take(PLACES[3])
    end = mats_count * rank
    for group, places, at, size in zip(groups[2:], PLACES[2:], STARTS[2:], ROWS[2:]):
        base = len(places) * LAT
        at = end + at - STARTS[2]
        r.projected[at : at + size, :] = group.full[base : base + size, :]
    both = swap(1, r.projected, r.projected_theirs)
    both.start()
    both.wait()
    r.small[STARTS[2] :, :] = r.projected[end:, :] + r.projected_theirs[end:, :]
    both = (r.projected[0:end, :] + r.projected_theirs[0:end, :]).reshape(mats_count, rank, LAT)
    columns = [both[:, i, :] for i in range(rank)]
    for i in range(rank):
        v = columns[i]
        v = v * lax.rsqrt(jnp.sum(v * v, 1, keepdims=True) + 1e-12)
        columns[i] = v
        for j in range(i + 1, rank):
            columns[j] = columns[j] - jnp.sum(v * columns[j], 1, keepdims=True) * v
    for i in range(rank):
        r.left[:, i, :] = columns[i]
    for which in range(mats_count):
        r.right_mine[ranked(which), :] = mm3(r.left[which], r.total[which])
    both = swap(2, r.right_mine, r.right_theirs)
    both.start()
    both.wait()
    r.right[...] = (r.right_mine[...] + r.right_theirs[...]).reshape(mats_count, rank, LAT)


def train(inputs, count_edge):
    own = inputs["feat"].shape[1]
    count = inputs["code"].shape[0] * LAT
    mats_count, rank, _ = inputs["factors"].shape
    reducers = [
        Reducer(count_edge, len(places) * LAT + rows)
        for places, rows in zip(PLACES, ROWS)
    ]
    flat = lambda *dims: pltpu.VMEM(dims, F32)
    half = lambda *dims: pltpu.VMEM(dims, BF16)
    small, late = STARTS[4], STARTS[4] - STARTS[2]
    outs = {
        "total": (mats_count, LAT, LAT),
        "left": (mats_count, rank, LAT),
        "right": (mats_count, rank, LAT),
        "small": (small, LAT),
    }
    scratch = {
        "feat_wide": flat(3, *inputs["feat"].shape),
        "w": half(3, 2 * LAT, LAT),
        "h0": flat(3 * own, LAT),
        "node_kept": flat(4, 3 * own, LAT),
        "step_kept": flat(4, own, LAT),
        "table": half(4 * own, 2 * LAT),
        "dagg": half(own, 2 * LAT),
        "agg0": flat(own, LAT),
        "h1": flat(own, LAT),
        "hb": flat(3 * own, LAT),
        "dh": flat(own, LAT),
        "rims": flat(2, own, LAT),
        "recv_total": flat(own // 2, 2 * LAT),
        "send_total": flat(3 * own // 2, 2 * LAT),
        "sums": flat(5, 8, LAT),
        "we": flat(EFEAT, LAT),
        "e0": half(count, LAT),
        "e1": half(count, LAT),
        "de": half(count, LAT),
        "small_mine": flat(STARTS[2], LAT),
        "small_theirs": flat(STARTS[2], LAT),
        "projected": flat(mats_count * rank + late, LAT),
        "projected_theirs": flat(mats_count * rank + late, LAT),
        "right_mine": flat(mats_count * rank, LAT),
        "right_theirs": flat(mats_count * rank, LAT),
        "halo_send": pltpu.SemaphoreType.DMA((6,)),
        "halo_recv": pltpu.SemaphoreType.DMA((6,)),
        "pair_send": pltpu.SemaphoreType.DMA((3,)),
        "pair_recv": pltpu.SemaphoreType.DMA((3,)),
    }
    for name in ("enc", "one", "two"):
        for i in range(4):
            scratch[f"{name}{i}"] = half(count, LAT)
    for i, reducer in enumerate(reducers):
        for name, shape in reducer.scratch().items():
            scratch[f"sum{i}_{name}"] = shape
    vmem = pl.BlockSpec(memory_space=pltpu.VMEM)
    names = list(inputs) + list(outs) + list(scratch)
    return pl.pallas_call(
        partial(train_kernel, reducers, names, mats_count, rank),
        in_specs=[vmem] * len(inputs),
        out_specs=[vmem] * len(outs),
        out_shape=[jax.ShapeDtypeStruct(shape, F32) for shape in outs.values()],
        scratch_shapes=list(scratch.values()),
        compiler_params=pltpu.CompilerParams(
            collective_id=0, has_side_effects=True, vmem_limit_bytes=VMEM_LIMIT
        ),
    )(*inputs.values())


VMEM_LIMIT = 62 << 20


def finish_kernel(total, left, right, small, mats, momentum, vecs, vecs_momentum, *outs):
    new_mats, new_momentum, new_errors, new_vecs, new_vecs_momentum, loss, kept_count, stats = outs
    for k in range(total.shape[0]):
        approx = mm3(left[k], right[k], TN)
        moved = 0.9 * momentum[k] + approx
        new_momentum[k] = moved
        new_mats[k] = mats[k] - 4.0 * moved
        new_errors[k] = total[k] - approx

    @pl.when(pl.program_id(0) == 0)
    def _():
        sums = jnp.sum(small[16:28, :], 1, keepdims=True)
        kept = sums[10:11]
        scale = 1.0 / kept
        loss[...] = sums[0:1] + sums[1:2]
        kept_count[...] = kept
        stats[...] = sums[2:10] * scale
        n1, e1, n0, enc, _ = STARTS
        cuts = (
            (n0 + 15, 23), (enc + 5, 3), (n0 + 10, 5), (enc, 5), (n0 + 5, 5), (n0, 5), (e1, 5),
            (n1, 9),
        )
        grads = jnp.concatenate([small[at : at + length, :] for at, length in cuts], 0)
        moved = 0.9 * vecs_momentum[...] + grads * scale
        new_vecs_momentum[...] = moved
        new_vecs[...] = vecs[...] - 4.0 * moved


def finish(total, left, right, small, mats, momentum, vecs, vecs_momentum):
    group = 6
    big = pl.BlockSpec((group, LAT, LAT), lambda i: (i, 0, 0))
    thin = pl.BlockSpec((group,) + left.shape[1:], lambda i: (i, 0, 0))
    whole = lambda shape: pl.BlockSpec(shape, lambda i: (0,) * len(shape))
    shape = lambda *dims: jax.ShapeDtypeStruct(dims, F32)
    return pl.pallas_call(
        finish_kernel,
        grid=(total.shape[0] // group,),
        in_specs=[big, thin, thin, whole(small.shape), big, big]
        + [whole(vecs.shape), whole(vecs.shape)],
        out_specs=[big] * 3 + [whole(vecs.shape)] * 2 + [whole((1, 1))] * 2 + [whole((8, 1))],
        out_shape=[shape(*total.shape)] * 3
        + [shape(*vecs.shape)] * 2
        + [shape(1, 1), shape(1, 1), shape(8, 1)],
    )(total, left, right, small, mats, momentum, vecs, vecs_momentum)


def shards(
    node_feat, node_types, boundary, target, edge_feat, senders, receivers, edge_counts, mats, vecs,
    mats_momentum, vecs_momentum, factors, errors,
):
    own = node_feat.shape[1]
    count = senders.shape[1]
    place = lax.axis_index("edge")
    lines = (count // LAT, LAT)
    slots = jnp.arange(count, dtype=jnp.int32).reshape(lines)
    send = senders.reshape(lines) - (place - 1) * own
    recv = receivers.reshape(lines) - place * own
    live = slots < edge_counts[0, 0]
    code = jnp.where(live, (send << SHIFT) + recv, (2047 << SHIFT) + 1023)
    feat = jnp.concatenate(
        [node_feat[0].T, node_types.astype(F32), jnp.zeros((1, own), F32)], 0
    )
    inputs = {
        "code": code,
        "x": edge_feat[0].T.reshape(EFEAT * lines[0], LAT),
        "feat": feat,
        "keep": (1 - boundary).astype(F32),
        "goal": target[0].T,
        "mats": mats,
        "vecs": vecs,
        "factors": jnp.swapaxes(factors, 1, 2),
        "errors": errors[0],
    }
    total, left, right, small = train(inputs, lax.axis_size("edge"))
    new_mats, mats_mom, new_errors, new_vecs, vecs_mom, loss, kept, stats = finish(
        total, left, right, small, mats, mats_momentum, vecs, vecs_momentum
    )
    return (
        loss.reshape(()),
        kept.reshape(()),
        stats.reshape(4, 2),
        new_mats,
        mats_mom,
        jnp.swapaxes(right, 1, 2),
        new_errors[None],
        new_vecs,
        vecs_mom,
    )


def solution(mesh):
    placed = (
        P("rep", "edge", None),
        P("rep", "edge"),
        P("rep", "edge"),
        P("rep", "edge", None),
        P("rep", "edge", None),
        P("rep", "edge"),
        P("rep", "edge"),
        P("rep", "edge"),
        P(),
        P(),
        P(),
        P(),
        P(),
        P("rep", None, None, None),
    )
    return jax.shard_map(
        shards,
        mesh=mesh,
        in_specs=placed,
        out_specs=(P(), P(), P(), P(), P(), P(), P("rep", None, None, None), P(), P()),
        check_vma=False,
    )
```

```python
from functools import partial

import jax
import jax.numpy as jnp
from jax import lax
from jax.experimental import pallas as pl
from jax.experimental.pallas import tpu as pltpu
from jax.sharding import PartitionSpec as P

NFEAT = 14
NTYPES = 9
EFEAT = 3
LEAD = NFEAT + NTYPES
ROWS0 = LEAD + EFEAT
LAT = 128
BLOCK = 2048
SUB = 512
SHIFT = 12
F32 = jnp.float32
BF16 = jnp.bfloat16
MESH = pl.DeviceIdType.MESH
NN = (((1,), (0,)), ((), ()))
NT = (((1,), (1,)), ((), ()))
TN = (((0,), (0,)), ((), ()))


def mm(a, b, dims=NN):
    return lax.dot_general(a, b, dims, preferred_element_type=F32)


def split(w):
    hi = w.astype(BF16)
    return hi, (w - hi.astype(F32)).astype(BF16)


def twice(a):
    return jnp.concatenate([a, a], 1)


def stacked(w):
    return jnp.concatenate(split(w), 0)


def side_by_side(v):
    return jnp.concatenate(split(v), 1)


def joined(wide):
    return wide[:, :LAT] + wide[:, LAT:]


def mm3(a, b, dims=NN):
    ah, al = split(a)
    bh, bl = split(b)
    return mm(ah, bh, dims) + (mm(ah, bl, dims) + mm(al, bh, dims))


def silu_half(half):
    up = 1.0 + jnp.tanh(half)
    value = half * up
    sig = 0.5 * up
    return value, sig + value - value * sig


def mean_last(v):
    return jnp.mean(v, -1, keepdims=True)


def center(w):
    return w - mean_last(w)


def fold_rows(v):
    total = v[0:8]
    for i in range(8, v.shape[0], 8):
        total = total + v[i : i + 8]
    return total


def row_sum(v):
    return jnp.sum(fold_rows(v), 0, keepdims=True)


def unfold(v):
    return jnp.concatenate([v[:, :LAT], v[:, LAT:]], 0)


def together(parts):
    parts = list(parts)
    while parts:
        for part in list(parts):
            try:
                next(part)
            except StopIteration:
                parts.remove(part)


def node_tail(first, second, third, vec):
    b1, b2, b3, g, o = vec
    half1 = 0.5 * (first + b1)
    half2 = 0.5 * (mm3(silu_half(half1)[0], second) + b2)
    z = mm3(silu_half(half2)[0], third) + b3
    c = z - mean_last(z)
    inv = lax.rsqrt(mean_last(c * c) + 1e-05)
    xhat = c * inv
    return xhat * g + o, (half1, half2, xhat, jnp.broadcast_to(inv, xhat.shape))


def node_tail_back(d, kept, second, third, vec):
    half1, half2, xhat, inv = kept
    s1, d1 = silu_half(half1)
    s2, d2 = silu_half(half2)
    dy = d * vec[3]
    dz3 = inv * (dy - mean_last(dy) - xhat * mean_last(dy * xhat))
    dz2 = mm3(dz3, third, NT) * d2
    dz1 = mm3(dz2, second, NT) * d1
    rows = [row_sum(v) for v in (dz1, dz2, dz3, d * xhat, d)]
    return dz1, mm3(s1, dz2, TN), mm3(s2, dz3, TN), rows


def edge_tail(rows, half, kept, second, third, vec, ones):
    _, b2, b3, g, o = vec
    kept[0][rows, :] = half.astype(BF16)
    s1 = silu_half(half)[0].astype(BF16)
    half = mm(twice(s1), second) + 0.5 * b2
    yield
    kept[1][rows, :] = half.astype(BF16)
    s2 = silu_half(half)[0].astype(BF16)
    c = mm(twice(s2), third) + center(b3)
    yield
    inv = lax.rsqrt(mm((c * c).astype(BF16), ones) + 1e-05)
    xhat = c * inv
    kept[2][rows, :] = xhat.astype(BF16)
    kept[3][rows, :] = inv.astype(BF16)
    return xhat * g + o


def edge_tail_back(rows, d, kept, second, third, g, ones, sums):
    xhat = kept[2][rows, :].astype(F32)
    inv = kept[3][rows, :].astype(F32)
    dx = d * xhat
    dc = inv * (d * g - xhat * mm((dx * g).astype(BF16), ones))
    dcb = dc.astype(BF16)
    for at, v in ((2, dc), (3, dx), (4, d)):
        sums[at] += fold_rows(v)
    yield
    s2, d2 = silu_half(kept[1][rows, :].astype(F32))
    dz2 = mm(twice(dcb), third) * d2
    sums[1] += fold_rows(dz2)
    dz2b = dz2.astype(BF16)
    yield
    s1, d1 = silu_half(kept[0][rows, :].astype(F32))
    dz1 = mm(twice(dz2b), second) * d1
    sums[0] += fold_rows(dz1)
    return dz1, dz2b, dcb, s1.astype(BF16), s2.astype(BF16)


def finish_sums(sums):
    rows = [jnp.sum(sums[i], 0, keepdims=True) for i in range(5)]
    rows[2] = center(rows[2])
    return rows


def columns_of(code):
    parts = [
        jnp.transpose(jnp.broadcast_to(code[q : q + 1, :], (LAT, LAT))) for q in range(code.shape[0])
    ]
    return jnp.concatenate(parts, 0)


def pick_mask(column, count):
    lanes = lax.broadcasted_iota(jnp.int32, (column.shape[0], LAT), 1)
    return [jnp.where(column == lanes + LAT * j, 1.0, 0.0).astype(BF16) for j in range(count // LAT)]


def add_mask(row, count):
    down = lax.broadcasted_iota(jnp.int32, (count, LAT), 0)
    parts = [
        jnp.where(row[q : q + 1, :] == down, 1.0, 0.0).astype(BF16) for q in range(row.shape[0])
    ]
    return jnp.concatenate(parts, 1)


def halves(v, lower, upper):
    return jnp.concatenate([jnp.where(lower, v, 0.0), jnp.where(upper, v, 0.0)], 1).astype(BF16)


def choose(wide, upper):
    return jnp.where(upper, wide[:, LAT:], wide[:, :LAT])


def send_of(code):
    return code >> SHIFT


def recv_of(code):
    return code & ((1 << SHIFT) - 1)


def folded(index, half):
    return jnp.where(index >= half, index - half, index)


def inner_of(send, own):
    at = send - own
    return jnp.where((at >= 0) & (at < own), folded(at, own // 2), -1)


def outer_of(send, own):
    return jnp.where((send >= own) & (send < 2 * own), -1, folded(send, 2 * own))


def orders_of(count):
    if count == 16:
        near, far = (4, 1), (4, 4)
        return [[near, far], [far, near]]
    if count == 64:
        a, b, c = (4, 1), (4, 4), (4, 16)
        return [[a, b, c], [b, c, a]]
    return [[(count, 1)], [(count, 1)]]


class Reducer:
    def __init__(self, count, rows):
        self.orders = orders_of(count)
        unit = 8 * count
        units = max(-(-rows // unit), 2)
        self.rows = units * unit
        near = min(max(round(units * 2 / 3), 1), units - 1) * unit
        self.parts = ((0, near), (near, self.rows - near))
        stages = len(self.orders[0])
        self.sequence = [(i, 0) for i in range(stages)] + [(i, 1) for i in reversed(range(stages))]
        self.steps = len(self.sequence) + 1

    def scratch(self):
        shapes = {"acc": pltpu.VMEM((self.rows, LAT), F32), "full": pltpu.VMEM((self.rows, LAT), F32)}
        copies = 0
        for half, order in enumerate(self.orders):
            length = self.parts[half][1]
            for stage, (k, _) in enumerate(order):
                length //= k
                shapes[f"slot{half}{stage}"] = pltpu.VMEM((max(k - 1, 1), length, LAT), F32)
                copies += k - 1
        shapes["send"] = pltpu.SemaphoreType.DMA((2 * copies,))
        shapes["recv"] = pltpu.SemaphoreType.DMA((2 * copies,))
        return shapes

    def bind(self, refs):
        self.refs = refs
        self.acc, self.full = refs["acc"], refs["full"]
        me = lax.axis_index("edge")
        self.begin = []
        self.length = []
        self.sems = {}
        used = 0
        for half, order in enumerate(self.orders):
            begin = [self.parts[half][0]]
            length = [self.parts[half][1]]
            for k, stride in order:
                length.append(length[-1] // k)
                begin.append(begin[-1] + ((me // stride) % k) * length[-1])
            self.begin.append(begin)
            self.length.append(length)
            for stage, (k, stride) in enumerate(order):
                for t in range(1, k):
                    for phase in range(2):
                        mine = (me // stride) % k
                        other = (mine + t) % k
                        self.sems[half, stage, phase, t] = (used, other, me + (other - mine) * stride)
                        used += 1

    def peers(self):
        order = self.orders[0]
        return [
            self.sems[0, stage, 0, t][2]
            for stage in range(len(order))
            for t in range(1, order[stage][0])
        ]

    def window(self, begin, length):
        return pl.ds(pl.multiple_of(begin, 8), length)

    def copies(self, half, stage, phase):
        k = self.orders[half][stage][0]
        out = []
        for t in range(1, k):
            at, other, device = self.sems[half, stage, phase, t]
            length = self.length[half][stage + 1]
            if phase == 0:
                rows = self.window(self.begin[half][stage] + other * length, length)
                source, target = self.acc.at[rows], self.refs[f"slot{half}{stage}"].at[t - 1]
            else:
                rows = self.window(self.begin[half][stage + 1], length)
                source = target = self.full.at[rows]
            out.append(
                pltpu.make_async_remote_copy(
                    src_ref=source,
                    dst_ref=target,
                    send_sem=self.refs["send"].at[at],
                    recv_sem=self.refs["recv"].at[at],
                    device_id={"edge": device},
                    device_id_type=MESH,
                )
            )
        return out

    def start(self, half, stage, phase):
        for one in self.copies(half, stage, phase):
            one.start()

    def wait(self, half, stage, phase):
        for one in self.copies(half, stage, phase):
            one.wait()
        if phase:
            return
        rows = self.window(self.begin[half][stage + 1], self.length[half][stage + 1])
        value = self.acc[rows, :]
        for t in range(1, self.orders[half][stage][0]):
            value = value + self.refs[f"slot{half}{stage}"][t - 1]
        if stage == len(self.orders[half]) - 1:
            self.full[rows, :] = value
        else:
            self.acc[rows, :] = value

    def step(self, index):
        for half in range(2):
            if index:
                self.wait(half, *self.sequence[index - 1])
            if index < len(self.sequence):
                self.start(half, *self.sequence[index])


PLACES = (
    (4, 5, 20, 21, 22, 23),
    (15, 18, 19, 16, 17, 11, 12, 13, 14),
    (6, 9, 10, 7, 8, 0, 1),
    (2, 3),
)
ROWS = (32, 8, 48, 8)
STARTS = tuple(sum(ROWS[:i]) for i in range(5))


class Refs(dict):
    def __getattr__(self, name):
        return self[name]


def train_kernel(reducers, names, mats_count, rank, *refs):
    r = Refs(zip(names, refs))
    groups = []
    for i, reducer in enumerate(reducers):
        mark = f"sum{i}_"
        reducer.bind({k[len(mark) :]: v for k, v in r.items() if k.startswith(mark)})
        groups.append(reducer)
    first, second, third, fourth = groups
    own = r.goal.shape[1]
    count = r.code.shape[0] * LAT
    lines = own // LAT
    me = lax.axis_index("edge")
    last = lax.axis_size("edge") - 1
    has_left, has_right = me > 0, me < last
    sibling = {"rep": 1 - lax.axis_index("rep")}
    barrier = pltpu.get_barrier_semaphore()
    around = [lax.rem(me + shift, last + 1) for shift in (1, last)]
    others = [{"edge": one} for one in first.peers() + around] + [sibling]
    for peer in others:
        pl.semaphore_signal(barrier, inc=1, device_id=peer, device_id_type=MESH)
    fetches = [
        pltpu.make_async_copy(source, target, r.fetch_sem.at[at])
        for at, (source, target) in enumerate(
            (
                (r.mats_in.at[pl.ds(2, 2)], r.mats.at[pl.ds(2, 2)]),
                (r.mats_in.at[pl.ds(0, 2)], r.mats.at[pl.ds(0, 2)]),
                (r.mats_in.at[pl.ds(4, mats_count - 4)], r.mats.at[pl.ds(4, mats_count - 4)]),
                (r.errors_in, r.errors),
            )
        )
    ]
    for one in fetches:
        one.start()
    mats, vecs = r.mats, r.vecs
    ones = jnp.full((LAT, LAT), 1.0 / LAT, BF16)
    middle = pl.ds(own, own)
    r["spread"] = r.hb
    r["agg_wide"] = r.outer_total

    def rows_of(which):
        base = ROWS0 + 5 * which
        return [vecs[base + i : base + i + 1, :] for i in range(5)]

    for q in range(lines):
        lanes = slice(q * LAT, (q + 1) * LAT)
        r.feat_wide[1, 0:NFEAT, lanes] = r.node_lines[pl.ds(q, NFEAT, stride=lines), :]
        r.feat_wide[1, NFEAT : NFEAT + 1, lanes] = r.types[q : q + 1, :].astype(F32)
        r.keep[:, lanes] = (1 - r.boundary[q : q + 1, :]).astype(F32)
    r.feat_wide[1, NFEAT + 1 :, :] = jnp.zeros((1, own), F32)

    @pl.when(me == 0)
    def _():
        r.feat_wide[0] = jnp.zeros(r.feat_wide.shape[1:], F32)
        r.hb[0:own, :] = jnp.zeros((own, LAT), F32)
        r.rims[0] = jnp.zeros((own, LAT), F32)

    @pl.when(me == last)
    def _():
        r.feat_wide[2] = jnp.zeros(r.feat_wide.shape[1:], F32)
        r.hb[2 * own :, :] = jnp.zeros((own, LAT), F32)
        r.rims[1] = jnp.zeros((own, LAT), F32)

    slots = lax.broadcasted_iota(jnp.int32, r.code.shape, 0) * LAT
    slots = slots + lax.broadcasted_iota(jnp.int32, r.code.shape, 1)
    code = ((r.senders[...] - (me - 1) * own) << SHIFT) + (r.receivers[...] - me * own)
    r.code[...] = jnp.where(slots < r.counts[...], code, (2047 << SHIFT) + 1023)

    def neighbours(at, up, up_target, down, down_target):
        def one(index, source, target, shift):
            return pltpu.make_async_remote_copy(
                src_ref=source,
                dst_ref=target,
                send_sem=r.halo_send.at[at + index],
                recv_sem=r.halo_recv.at[at + index],
                device_id={"edge": me + shift},
                device_id_type=MESH,
            )

        return one(0, up, up_target, 1), one(1, down, down_target, -1)

    def start(pair):
        @pl.when(has_right)
        def _():
            pair[0].start()

        @pl.when(has_left)
        def _():
            pair[1].start()

    def wait(pair):
        @pl.when(has_right)
        def _():
            pair[0].wait_send()
            pair[1].wait_recv()

        @pl.when(has_left)
        def _():
            pair[1].wait_send()
            pair[0].wait_recv()

    mine = r.feat_wide.at[1]
    feats = neighbours(0, mine, r.feat_wide.at[0], mine, r.feat_wide.at[2])

    def begin():
        pl.semaphore_wait(barrier, len(others))
        start(feats)

    turns = count // BLOCK

    def steps_of(group):
        return {index: partial(group.step, index) for index in range(turns)}

    def loop(body, hooks=None):
        def step(i, unused):
            for index, hook in (hooks or {}).items():
                pl.when(i == index)(hook)

            base = pl.multiple_of(i * (BLOCK // LAT), BLOCK // LAT)
            code = r.code[pl.ds(base, BLOCK // LAT), :]
            per = count // LAT
            planes = [r.x[pl.ds(base + p * per, BLOCK // LAT), :] for p in range(EFEAT)]
            parts = []
            for at in range(0, BLOCK, SUB):
                rows = pl.ds(pl.multiple_of(i * BLOCK + at, SUB), SUB)
                cut = slice(at // LAT, (at + SUB) // LAT)
                parts.append(body(rows, code[cut], [plane[cut] for plane in planes]))
            together(parts)
            return unused

        lax.fori_loop(0, count // BLOCK, step, 0)

    def features(planes):
        lines = [
            jnp.concatenate([plane[q : q + 1, :] for q in range(plane.shape[0])], 1)
            for plane in planes
        ]
        return jnp.concatenate(lines, 0)

    kept = [[r[f"{name}{i}"] for i in range(4)] for name in ("enc", "one", "two")]

    fetches[0].wait()
    r.w[0] = stacked(0.5 * mats[2])
    r.w[1] = stacked(center(mats[3]))
    vec = rows_of(1)

    def encode(rows, code, planes):
        half = mm3(features(planes), 0.5 * vecs[LEAD:ROWS0, :], TN) + 0.5 * vec[0]
        yield
        out = yield from edge_tail(rows, half, kept[0], r.w[0], r.w[1], vec, ones)
        r.e0[rows, :] = out.astype(BF16)

    loop(encode, {turns // 2: begin})

    fetches[1].wait()
    fetches[2].wait()
    wait(feats)
    def particle_inputs():
        values = jnp.concatenate([r.feat_wide[i] for i in range(3)], 1)
        types = lax.broadcasted_iota(jnp.int32, (NTYPES, 3 * own), 0).astype(F32)
        return values[0:NFEAT], jnp.where(values[NFEAT : NFEAT + 1] == types, 1.0, 0.0)

    plain, onehot = particle_inputs()
    pre = mm3(plain, vecs[0:NFEAT, :], TN) + mm3(onehot, vecs[NFEAT:LEAD, :], TN)
    out, saved = node_tail(pre, mats[0], mats[1], rows_of(0))
    r.h0[...] = out
    for j, v in enumerate(saved):
        r.node_kept[j] = v
    latent = 0.5 * mm3(out, mats[7])

    def put_inner(v):
        r.inner[...] = jnp.concatenate([v[: own // 2], v[own // 2 :]], 1).astype(BF16)

    def put_outer(left, right):
        r.outer[...] = jnp.concatenate([left, right], 1).astype(BF16)

    put_inner(latent[own : 2 * own])
    put_outer(latent[:own], latent[2 * own :])
    r.recv_table[...] = side_by_side(0.5 * mm3(out[own : 2 * own], mats[8]))

    def put_weights(step):
        base = 6 + 9 * step
        r.w[0] = stacked(0.5 * mats[base])
        r.w[1] = stacked(0.5 * mats[base + 3])
        r.w[2] = stacked(center(mats[base + 4]))

    def near_part(column, send, e, b1):
        wide = mm(jnp.concatenate(pick_mask(recv_of(column), own), 1), r.recv_table[...])
        half = joined(wide) + mm(twice(e), r.w[0]) + 0.5 * b1
        wide = mm(jnp.concatenate(pick_mask(inner_of(send, own), own // 2), 1), r.inner[...])
        return half + choose(wide, send >= own + own // 2)

    def far_part(send):
        wide = mm(jnp.concatenate(pick_mask(outer_of(send, own), own), 1), r.outer[...])
        return choose(wide, send >= 2 * own)

    def add_up(rows, half, code, step, vec):
        out = yield from edge_tail(rows, half, kept[1 + step], r.w[1], r.w[2], vec, ones)
        r.agg_wide[...] += mm(add_mask(recv_of(code), own), side_by_side(out))
        return out

    put_weights(0)
    r.agg_wide[...] = jnp.zeros_like(r.agg_wide)
    vec0 = rows_of(2)

    def first_step(rows, code, planes):
        column = columns_of(code)
        send = send_of(column)
        e = r.e0[rows, :]
        half = near_part(column, send, e, vec0[0]) + far_part(send)
        yield
        out = yield from add_up(rows, half, code, 0, vec0)
        r.e1[rows, :] = (e.astype(F32) + out).astype(BF16)

    loop(first_step)
    h = r.h0[middle, :]
    agg = joined(r.agg_wide[...])
    r.agg0[...] = agg
    delta, saved = node_tail(mm3(h, mats[11]) + mm3(agg, mats[12]), mats[13], mats[14], rows_of(3))
    for j, v in enumerate(saved):
        r.step_kept[j] = v
    h = h + delta
    r.h1[...] = h
    r.hb[middle, :] = 0.5 * mm3(h, mats[16])
    mine = r.hb.at[middle]
    latents = neighbours(2, mine, r.hb.at[pl.ds(0, own)], mine, r.hb.at[pl.ds(2 * own, own)])
    start(latents)
    r.recv_table[...] = side_by_side(0.5 * mm3(h, mats[17]))
    put_inner(r.hb[middle, :])

    put_weights(1)
    r.agg_wide[...] = jnp.zeros_like(r.agg_wide)
    vec1 = rows_of(4)

    def near_step(rows, code, planes):
        column = columns_of(code)
        half = near_part(column, send_of(column), r.e1[rows, :], vec1[0])
        yield
        kept[2][2][rows, :], kept[2][3][rows, :] = split(half)

    def second_step(rows, code, planes):
        send = send_of(columns_of(code))
        half = kept[2][2][rows, :].astype(F32) + kept[2][3][rows, :].astype(F32) + far_part(send)
        yield
        yield from add_up(rows, half, code, 1, vec1)

    loop(near_step)
    wait(latents)
    put_outer(r.hb[0:own, :], r.hb[2 * own :, :])
    loop(second_step)

    def slot(group, places, which):
        at = places.index(which) * LAT
        return group.acc.at[pl.ds(at, LAT)]

    def put(group, places, which, value):
        slot(group, places, which)[...] = value

    def put_rows(group, places, at, rows):
        base = len(places) * LAT + at
        for v in rows:
            group.acc[base : base + v.shape[0], :] = v
            base += v.shape[0]
        return base

    def finish_step(group, at):
        for index in range(at, group.steps):
            group.step(index)

    put1, put2, put3, _ = (partial(put, group, places) for group, places in zip(groups, PLACES))
    agg = joined(r.agg_wide[...])
    h = r.h1[...]
    vec = rows_of(5)
    delta, saved = node_tail(mm3(h, mats[20]) + mm3(agg, mats[21]), mats[22], mats[23], vec)
    out = h + delta
    base = ROWS0 + 30
    s1, d1 = silu_half(0.5 * (mm3(out, mats[4]) + vecs[base : base + 1, :]))
    s2, d2 = silu_half(0.5 * (mm3(s1, mats[5]) + vecs[base + 1 : base + 2, :]))
    ends = vecs[base + 2 : base + 4, :]
    keep = r.keep[...]
    goal = r.goal[...]
    diff = mm3(ends, s2, NT) - goal
    kept_diff = diff * keep
    dpred = 2.0 * kept_diff
    dz2 = mm3(dpred, ends, TN) * d2
    dz1 = mm3(dz2, mats[5], NT) * d1
    d = mm3(dz1, mats[4], NT)
    dz, g_second, g_third, rows = node_tail_back(d, saved, mats[22], mats[23], vec)
    r.dh[...] = d + mm3(dz, mats[20], NT)
    r.dagg[...] = side_by_side(mm3(dz, mats[21], NT))
    put1(4, mm3(out, dz1, TN))
    put1(5, mm3(s1, dz2, TN))
    put1(20, mm3(h, dz, TN))
    put1(21, mm3(agg, dz, TN))
    put1(22, g_second)
    put1(23, g_third)
    rows = rows + [row_sum(dz1), row_sum(dz2), mm3(dpred, s2)]
    rows.append(jnp.zeros((7, LAT), F32))
    velocity = r.feat_wide[1, 8:10, :]
    for v in (
        kept_diff * diff,
        velocity * keep,
        velocity * velocity * keep,
        goal * keep,
        goal * goal * keep,
        jnp.broadcast_to(keep, velocity.shape),
    ):
        part = v[:, 0:LAT]
        for j in range(LAT, own, LAT):
            part = part + v[:, j : j + LAT]
        rows.append(part)
    end = put_rows(first, PLACES[0], 0, rows)
    first.acc[end:, :] = jnp.zeros((first.rows - end, LAT), F32)

    def zero(*targets):
        for target in targets:
            target[...] = jnp.zeros_like(target)

    half = own // 2

    def put_back(step):
        base = 6 + 9 * step
        for i, w in enumerate((mats[base], mats[base + 3], center(mats[base + 4]))):
            r.w[i] = stacked(jnp.transpose(w))

    def chain(rows, column, step, gain, residual):
        d = joined(mm(jnp.concatenate(pick_mask(recv_of(column), own), 1), r.dagg[...]))
        if residual is not None:
            d = d + residual
        yield
        return (
            yield from edge_tail_back(
                rows, d, kept[1 + step], r.w[1], r.w[2], gain, ones, r.sums
            )
        )

    def add_outer(code, send, dz1):
        r.outer_total[...] += mm(
            add_mask(outer_of(send_of(code), own), own), halves(dz1, send < own, send >= 2 * own)
        )

    def add_inner(code, column, send, dz1):
        recv = recv_of(column)
        r.recv_total[...] += mm(
            add_mask(folded(recv_of(code), half), half), halves(dz1, recv < half, recv >= half)
        )
        edge = own + half
        r.inner_total[...] += mm(
            add_mask(inner_of(send_of(code), own), half), halves(dz1, send < edge, send >= edge)
        )

    def slots_of(group, places, step):
        base = 6 + 9 * step
        return [slot(group, places, which) for which in (base, base + 3, base + 4)]

    def add_grads(grads, e, dz1b, dz2b, dcb, s1, s2):
        grads[0][...] += mm(e, dz1b, TN)
        grads[1][...] += mm(s1, dz2b, TN)
        grads[2][...] += mm(s2, dcb, TN)

    put_back(1)
    grads1 = slots_of(second, PLACES[1], 1)
    zero(*grads1, r.sums, r.recv_total, r.inner_total, r.outer_total)
    gain1 = vec1[3]

    def chain_step(rows, code, planes):
        column = columns_of(code)
        dz1, *others = yield from chain(rows, column, 1, gain1, None)
        for ref, v in zip((kept[2][3], kept[2][2], kept[2][0], kept[2][1]), others):
            ref[rows, :] = v
        r.de[rows, :] = dz1.astype(BF16)
        add_outer(code, send_of(column), dz1)

    def grads_step(rows, code, planes):
        column = columns_of(code)
        dz1b = r.de[rows, :]
        s1, s2, dcb, dz2b = (ref[rows, :] for ref in kept[2])
        add_grads(grads1, r.e1[rows, :], dz1b, dz2b, dcb, s1, s2)
        add_inner(code, column, send_of(column), dz1b.astype(F32))
        r.de[rows, :] = mm(twice(dz1b), r.w[0]).astype(BF16)
        yield

    loop(chain_step, steps_of(first))
    r.spread[0:own, :] = r.outer_total[:, :LAT]
    r.spread[2 * own :, :] = r.outer_total[:, LAT:]
    rims = neighbours(
        4, r.spread.at[pl.ds(2 * own, own)], r.rims.at[0], r.spread.at[pl.ds(0, own)], r.rims.at[1]
    )
    start(rims)
    loop(grads_step)
    grads1[2][...] = center(grads1[2][...])
    end = put_rows(second, PLACES[1], 0, finish_sums(r.sums))
    second.acc[end:, :] = jnp.zeros((second.rows - end, LAT), F32)
    got = unfold(r.recv_total[...])
    h = r.h1[...]
    put2(17, mm3(h, got, TN))
    d = r.dh[...] + mm3(got, mats[17], NT)
    sent = unfold(r.inner_total[...])
    wait(rims)
    finish_step(first, turns)
    sent = sent + r.rims[0] + r.rims[1]
    put2(16, mm3(h, sent, TN))
    d = d + mm3(sent, mats[16], NT)
    saved = [r.step_kept[j] for j in range(4)]
    dz, g_second, g_third, rows = node_tail_back(d, saved, mats[13], mats[14], rows_of(3))
    put2(11, mm3(r.h0[middle, :], dz, TN))
    put2(12, mm3(r.agg0[...], dz, TN))
    put2(13, g_second)
    put2(14, g_third)
    put_rows(third, PLACES[2], 0, rows)
    r.dh[...] = d + mm3(dz, mats[11], NT)
    r.dagg[...] = side_by_side(mm3(dz, mats[12], NT))

    put_back(0)
    grads0 = slots_of(third, PLACES[2], 0)
    zero(*grads0, r.sums, r.recv_total, r.inner_total, r.outer_total)
    gain0 = vec0[3]

    def whole_step(rows, code, planes):
        column = columns_of(code)
        send = send_of(column)
        de = r.de[rows, :].astype(F32)
        dz1, *others = yield from chain(rows, column, 0, gain0, de)
        dz1b = dz1.astype(BF16)
        yield
        add_grads(grads0, r.e0[rows, :], dz1b, *others)
        add_outer(code, send, dz1)
        add_inner(code, column, send, dz1)
        r.de[rows, :] = (de + mm(twice(dz1b), r.w[0])).astype(BF16)

    loop(whole_step, steps_of(second))
    grads0[2][...] = center(grads0[2][...])
    sent = unfold(r.inner_total[...])
    sent = jnp.concatenate([r.outer_total[:, :LAT], sent, r.outer_total[:, LAT:]], 0)
    got = unfold(r.recv_total[...])
    h = r.h0[...]
    put3(7, mm3(h, sent, TN))
    put3(8, mm3(h[own : 2 * own], got, TN))
    d = mm3(sent, mats[7], NT)
    inner = d[own : 2 * own] + r.dh[...] + mm3(got, mats[8], NT)
    d = jnp.concatenate([d[:own], inner, d[2 * own :]], 0)
    saved = [r.node_kept[j] for j in range(4)]
    dz, g_second, g_third, more = node_tail_back(d, saved, mats[0], mats[1], rows_of(0))
    put3(0, g_second)
    put3(1, g_third)
    plain, onehot = particle_inputs()
    rows = finish_sums(r.sums) + more + [mm3(plain, dz), mm3(onehot, dz)]
    end = put_rows(third, PLACES[2], 5, rows)
    third.acc[end:, :] = jnp.zeros((third.rows - end, LAT), F32)
    third.step(0)
    finish_step(second, turns)

    enc_grads = [slot(fourth, PLACES[3], which) for which in PLACES[3]]
    zero(*enc_grads, r.sums, r.we)
    r.w[0] = stacked(jnp.transpose(mats[2]))
    r.w[1] = stacked(jnp.transpose(center(mats[3])))
    gain = rows_of(1)[3]

    def encoder_back(rows, code, planes):
        d = r.de[rows, :].astype(F32)
        dz1, dz2b, dcb, s1, s2 = yield from edge_tail_back(
            rows, d, kept[0], r.w[0], r.w[1], gain, ones, r.sums
        )
        yield
        enc_grads[0][...] += mm(s1, dz2b, TN)
        enc_grads[1][...] += mm(s2, dcb, TN)
        r.we[...] += mm(features(planes).astype(BF16), dz1.astype(BF16))

    loop(encoder_back)
    enc_grads[1][...] = center(enc_grads[1][...])
    end = put_rows(fourth, PLACES[3], 0, finish_sums(r.sums) + [r.we[...]])
    fourth.acc[end:, :] = jnp.zeros((fourth.rows - end, LAT), F32)

    def swap(at, source, target):
        return pltpu.make_async_remote_copy(
            src_ref=source,
            dst_ref=target,
            send_sem=r.pair_send.at[at],
            recv_sem=r.pair_recv.at[at],
            device_id=sibling,
            device_id_type=MESH,
        )

    def gradient(which):
        for group, places in zip(groups, PLACES):
            if which in places:
                return group.full[places.index(which) * LAT : (places.index(which) + 1) * LAT, :]
        return None

    def ranked(which):
        return slice(which * rank, (which + 1) * rank)

    third.step(1)
    fourth.step(0)
    for group, places, at, size in zip(groups[:2], PLACES, STARTS, ROWS):
        base = len(places) * LAT
        r.small_mine[at : at + size, :] = group.full[base : base + size, :]
    small = swap(0, r.small_mine, r.small_theirs)
    small.start()
    fetches[3].wait()
    for which in range(mats_count):
        r.projected[ranked(which), :] = mm3(r.factors[which], r.errors[which], NT)
    small.wait()
    small = r.small_mine[...] + r.small_theirs[...]
    r.small[0 : STARTS[2], :] = small
    at = 16 + 10
    scale = 1.0 / jnp.sum(small[at : at + 1, :], 1, keepdims=True)

    def take(chosen):
        for which in chosen:
            part = gradient(which)
            r.total[which] = part * scale + r.errors[which]
            r.projected[ranked(which), :] += scale * mm3(r.factors[which], part, NT)

    third.step(2)
    fourth.step(1)
    take(PLACES[0])
    for index in range(3, third.steps):
        third.step(index)
        fourth.step(index - 1)
        if index == 3:
            take(PLACES[1])
    take(PLACES[2])
    finish_step(fourth, third.steps - 1)
    take(PLACES[3])
    end = mats_count * rank
    for group, places, at, size in zip(groups[2:], PLACES[2:], STARTS[2:], ROWS[2:]):
        base = len(places) * LAT
        at = end + at - STARTS[2]
        r.projected[at : at + size, :] = group.full[base : base + size, :]
    both = swap(1, r.projected, r.projected_theirs)
    both.start()
    both.wait()
    r.small[STARTS[2] :, :] = r.projected[end:, :] + r.projected_theirs[end:, :]
    both = (r.projected[0:end, :] + r.projected_theirs[0:end, :]).reshape(mats_count, rank, LAT)
    columns = [both[:, i, :] for i in range(rank)]
    for i in range(rank):
        v = columns[i]
        v = v * lax.rsqrt(jnp.sum(v * v, 1, keepdims=True) + 1e-12)
        columns[i] = v
        for j in range(i + 1, rank):
            columns[j] = columns[j] - jnp.sum(v * columns[j], 1, keepdims=True) * v
    for i in range(rank):
        r.left[:, i, :] = columns[i]
    for which in range(mats_count):
        r.right_mine[ranked(which), :] = mm3(r.left[which], r.total[which])
    both = swap(2, r.right_mine, r.right_theirs)
    both.start()
    both.wait()
    r.right[...] = (r.right_mine[...] + r.right_theirs[...]).reshape(mats_count, rank, LAT)


def train(inputs, count_edge):
    own = inputs["goal"].shape[1]
    lines = inputs["senders"].shape
    count = lines[0] * LAT
    mats_count, rank, _ = inputs["factors"].shape
    reducers = [
        Reducer(count_edge, len(places) * LAT + rows)
        for places, rows in zip(PLACES, ROWS)
    ]
    flat = lambda *dims: pltpu.VMEM(dims, F32)
    half = lambda *dims: pltpu.VMEM(dims, BF16)
    small, late = STARTS[4], STARTS[4] - STARTS[2]
    outs = {
        "total": (mats_count, LAT, LAT),
        "left": (mats_count, rank, LAT),
        "right": (mats_count, rank, LAT),
        "small": (small, LAT),
    }
    scratch = {
        "code": pltpu.VMEM(lines, jnp.int32),
        "mats": flat(*inputs["mats_in"].shape),
        "errors": flat(*inputs["errors_in"].shape),
        "keep": flat(1, own),
        "feat_wide": flat(3, NFEAT + 2, own),
        "w": half(3, 2 * LAT, LAT),
        "h0": flat(3 * own, LAT),
        "node_kept": flat(4, 3 * own, LAT),
        "step_kept": flat(4, own, LAT),
        "inner": half(own // 2, 2 * LAT),
        "outer": half(own, 2 * LAT),
        "recv_table": half(own, 2 * LAT),
        "dagg": half(own, 2 * LAT),
        "agg0": flat(own, LAT),
        "h1": flat(own, LAT),
        "hb": flat(3 * own, LAT),
        "dh": flat(own, LAT),
        "rims": flat(2, own, LAT),
        "recv_total": flat(own // 2, 2 * LAT),
        "inner_total": flat(own // 2, 2 * LAT),
        "outer_total": flat(own, 2 * LAT),
        "sums": flat(5, 8, LAT),
        "we": flat(EFEAT, LAT),
        "e0": half(count, LAT),
        "e1": half(count, LAT),
        "de": half(count, LAT),
        "small_mine": flat(STARTS[2], LAT),
        "small_theirs": flat(STARTS[2], LAT),
        "projected": flat(mats_count * rank + late, LAT),
        "projected_theirs": flat(mats_count * rank + late, LAT),
        "right_mine": flat(mats_count * rank, LAT),
        "right_theirs": flat(mats_count * rank, LAT),
        "fetch_sem": pltpu.SemaphoreType.DMA((4,)),
        "halo_send": pltpu.SemaphoreType.DMA((6,)),
        "halo_recv": pltpu.SemaphoreType.DMA((6,)),
        "pair_send": pltpu.SemaphoreType.DMA((3,)),
        "pair_recv": pltpu.SemaphoreType.DMA((3,)),
    }
    for name in ("enc", "one", "two"):
        for i in range(4):
            scratch[f"{name}{i}"] = half(count, LAT)
    for i, reducer in enumerate(reducers):
        for name, shape in reducer.scratch().items():
            scratch[f"sum{i}_{name}"] = shape
    vmem = pl.BlockSpec(memory_space=pltpu.VMEM)
    names = list(inputs) + list(outs) + list(scratch)
    return pl.pallas_call(
        partial(train_kernel, reducers, names, mats_count, rank),
        in_specs=[pl.BlockSpec(memory_space=pl.ANY) if name.endswith("_in") else vmem for name in inputs],
        out_specs=[vmem] * len(outs),
        out_shape=[jax.ShapeDtypeStruct(shape, F32) for shape in outs.values()],
        scratch_shapes=list(scratch.values()),
        compiler_params=pltpu.CompilerParams(
            collective_id=0, has_side_effects=True, vmem_limit_bytes=VMEM_LIMIT
        ),
    )(*inputs.values())


VMEM_LIMIT = 62 << 20


def finish_kernel(total, left, right, small, mats, momentum, vecs, vecs_momentum, *outs):
    new_mats, new_momentum, new_errors, new_factors, *outs = outs
    new_vecs, new_vecs_momentum, loss, kept_count, stats = outs
    new_factors[...] = right[...]
    for k in range(total.shape[0]):
        approx = mm3(left[k], right[k], TN)
        moved = 0.9 * momentum[k] + approx
        new_momentum[k] = moved
        new_mats[k] = mats[k] - 4.0 * moved
        new_errors[k] = total[k] - approx

    @pl.when(pl.program_id(0) == 0)
    def _():
        sums = jnp.sum(small[16:28, :], 1, keepdims=True)
        kept = sums[10:11]
        scale = 1.0 / kept
        loss[...] = sums[0:1] + sums[1:2]
        kept_count[...] = kept
        lanes = lax.broadcasted_iota(jnp.int32, stats.shape, 1)
        table = jnp.zeros(stats.shape, F32)
        for i in range(4):
            table = jnp.where(lanes == i, sums[2 + 2 * i : 4 + 2 * i], table)
        stats[...] = table * scale
        n1, e1, n0, enc, _ = STARTS
        cuts = (
            (n0 + 15, 23), (enc + 5, 3), (n0 + 10, 5), (enc, 5), (n0 + 5, 5), (n0, 5), (e1, 5),
            (n1, 9),
        )
        grads = jnp.concatenate([small[at : at + length, :] for at, length in cuts], 0)
        moved = 0.9 * vecs_momentum[...] + grads * scale
        new_vecs_momentum[...] = moved
        new_vecs[...] = vecs[...] - 4.0 * moved


def finish(total, left, right, small, mats, momentum, vecs, vecs_momentum):
    group = 6
    big = pl.BlockSpec((group, LAT, LAT), lambda i: (i, 0, 0))
    thin = pl.BlockSpec((group,) + left.shape[1:], lambda i: (i, 0, 0))
    whole = lambda shape: pl.BlockSpec(shape, lambda i: (0,) * len(shape))
    shape = lambda *dims: jax.ShapeDtypeStruct(dims, F32)
    return pl.pallas_call(
        finish_kernel,
        grid=(total.shape[0] // group,),
        in_specs=[big, thin, thin, whole(small.shape), big, big]
        + [whole(vecs.shape), whole(vecs.shape)],
        out_specs=[big] * 3 + [thin] + [whole(vecs.shape)] * 2 + [whole((1, 1))] * 2 + [whole((2, 4))],
        out_shape=[shape(*total.shape)] * 3
        + [shape(*right.shape)]
        + [shape(*vecs.shape)] * 2
        + [shape(1, 1), shape(1, 1), shape(2, 4)],
    )(total, left, right, small, mats, momentum, vecs, vecs_momentum)


def shards(
    node_feat, node_types, boundary, target, edge_feat, senders, receivers, edge_counts, mats, vecs,
    mats_momentum, vecs_momentum, factors, errors,
):
    own = node_feat.shape[1]
    count = senders.shape[1]
    lines = (count // LAT, LAT)
    few = (own // LAT, LAT)
    inputs = {
        "senders": senders.reshape(lines),
        "receivers": receivers.reshape(lines),
        "counts": edge_counts,
        "x": jnp.transpose(edge_feat, (2, 0, 1)).reshape(EFEAT * lines[0], LAT),
        "node_lines": jnp.transpose(node_feat, (2, 0, 1)).reshape(NFEAT * few[0], LAT),
        "types": node_types.reshape(few),
        "boundary": boundary.reshape(few),
        "goal": target[0].T,
        "mats_in": mats,
        "vecs": vecs,
        "factors": jnp.swapaxes(factors, 1, 2),
        "errors_in": errors[0],
    }
    total, left, right, small = train(inputs, lax.axis_size("edge"))
    new_mats, mats_mom, new_errors, new_factors, new_vecs, vecs_mom, loss, kept, stats = finish(
        total, left, right, small, mats, mats_momentum, vecs, vecs_momentum
    )
    return (
        loss.reshape(()),
        kept.reshape(()),
        stats.T,
        new_mats,
        mats_mom,
        jnp.swapaxes(new_factors, 1, 2),
        new_errors[None],
        new_vecs,
        vecs_mom,
    )


def solution(mesh):
    placed = (
        P("rep", "edge", None),
        P("rep", "edge"),
        P("rep", "edge"),
        P("rep", "edge", None),
        P("rep", "edge", None),
        P("rep", "edge"),
        P("rep", "edge"),
        P("rep", "edge"),
        P(),
        P(),
        P(),
        P(),
        P(),
        P("rep", None, None, None),
    )
    return jax.shard_map(
        shards,
        mesh=mesh,
        in_specs=placed,
        out_specs=(P(), P(), P(), P(), P(), P(), P("rep", None, None, None), P(), P()),
        check_vma=False,
    )
```

```python
from functools import partial

import jax
import jax.numpy as jnp
from jax import lax
from jax.experimental import pallas as pl
from jax.experimental.pallas import tpu as pltpu
from jax.sharding import PartitionSpec as P

NFEAT = 14
NTYPES = 9
EFEAT = 3
LEAD = NFEAT + NTYPES
ROWS0 = LEAD + EFEAT
LAT = 128
BLOCK = 2048
SUB = 512
SHIFT = 10
NONE = (1 << SHIFT) - 1
F32 = jnp.float32
BF16 = jnp.bfloat16
MESH = pl.DeviceIdType.MESH
NN = (((1,), (0,)), ((), ()))
NT = (((1,), (1,)), ((), ()))
TN = (((0,), (0,)), ((), ()))


def mm(a, b, dims=NN):
    return lax.dot_general(a, b, dims, preferred_element_type=F32)


def split(w):
    hi = w.astype(BF16)
    return hi, (w - hi.astype(F32)).astype(BF16)


def twice(a):
    return jnp.concatenate([a, a], 1)


def stacked(w):
    return jnp.concatenate(split(w), 0)


def side_by_side(v):
    return jnp.concatenate(split(v), 1)


def joined(wide):
    return wide[:, :LAT] + wide[:, LAT:]


def mm3(a, b, dims=NN):
    ah, al = split(a)
    bh, bl = split(b)
    (axis_a,), (axis_b,) = dims[0]
    if a.shape[axis_a] % LAT:
        return mm(ah, bh, dims) + (mm(ah, bl, dims) + mm(al, bh, dims))
    a = jnp.concatenate([ah, ah, al], axis_a)
    return mm(a, jnp.concatenate([bh, bl, bh], axis_b), dims)


def silu_half(half):
    rest = jnp.tanh(half)
    up = 1.0 + rest
    value = half * up
    return value, up + value * (1.0 - rest)


def mean_last(v):
    return jnp.mean(v, -1, keepdims=True)


def center(w):
    return w - mean_last(w)


def fold_rows(v):
    total = v[0:8]
    for i in range(8, v.shape[0], 8):
        total = total + v[i : i + 8]
    return total


def row_sum(v):
    return jnp.sum(fold_rows(v), 0, keepdims=True)


def fold_table(v):
    half = v.shape[0] // 2
    return jnp.concatenate([v[:half], v[half:]], 1).astype(BF16)


def unfold(v):
    return jnp.concatenate([v[:, :LAT], v[:, LAT:]], 0)


def together(parts):
    parts = list(parts)
    while parts:
        for part in list(parts):
            try:
                next(part)
            except StopIteration:
                parts.remove(part)


def node_tail(first, second, third, vec):
    b1, b2, b3, g, o = vec
    half1 = 0.5 * (first + b1)
    half2 = 0.5 * (mm3(silu_half(half1)[0], second) + b2)
    z = mm3(silu_half(half2)[0], third) + b3
    c = z - mean_last(z)
    inv = lax.rsqrt(mean_last(c * c) + 1e-05)
    xhat = c * inv
    return xhat * g + o, (half1, half2, xhat, jnp.broadcast_to(inv, xhat.shape))


def node_tail_back(d, kept, second, third, vec):
    half1, half2, xhat, inv = kept
    s1, d1 = silu_half(half1)
    s2, d2 = silu_half(half2)
    dy = d * vec[3]
    dz3 = inv * (dy - mean_last(dy) - xhat * mean_last(dy * xhat))
    dz2 = mm3(dz3, 0.5 * third, NT) * d2
    dz1 = mm3(dz2, 0.5 * second, NT) * d1
    rows = [row_sum(v) for v in (dz1, dz2, dz3, d * xhat, d)]
    return dz1, mm3(s1, dz2, TN), mm3(s2, dz3, TN), rows


def edge_tail(rows, half, kept, second, third, vec, ones):
    _, b2, b3, g, o = vec
    kept[0][rows, :] = half.astype(BF16)
    s1 = silu_half(half)[0].astype(BF16)
    half = mm(twice(s1), second) + 0.5 * b2
    yield
    kept[1][rows, :] = half.astype(BF16)
    s2 = silu_half(half)[0].astype(BF16)
    c = mm(twice(s2), third) + center(b3)
    yield
    inv = lax.rsqrt(mm((c * c).astype(BF16), ones) + 1e-05)
    xhat = c * inv
    kept[2][rows, :] = xhat.astype(BF16)
    kept[3][rows, :] = inv.astype(BF16)
    return xhat * g + o


def edge_tail_back(rows, d, kept, second, third, g, ones, sums):
    xhat = kept[2][rows, :].astype(F32)
    inv = kept[3][rows, :].astype(F32)
    dx = d * xhat
    dc = inv * (d * g - xhat * mm((dx * g).astype(BF16), ones))
    dcb = dc.astype(BF16)
    for at, v in ((2, dc), (3, dx), (4, d)):
        sums[at] += fold_rows(v)
    yield
    s2, d2 = silu_half(kept[1][rows, :].astype(F32))
    dz2 = mm(twice(dcb), third) * d2
    sums[1] += fold_rows(dz2)
    dz2b = dz2.astype(BF16)
    yield
    s1, d1 = silu_half(kept[0][rows, :].astype(F32))
    dz1 = mm(twice(dz2b), second) * d1
    sums[0] += fold_rows(dz1)
    return dz1, dz2b, dcb, s1.astype(BF16), s2.astype(BF16)


def finish_sums(sums):
    rows = [jnp.sum(sums[i], 0, keepdims=True) for i in range(5)]
    rows[2] = center(rows[2])
    return rows


def columns_of(code):
    parts = [
        jnp.transpose(jnp.broadcast_to(code[q : q + 1, :], (LAT, LAT))) for q in range(code.shape[0])
    ]
    return jnp.concatenate(parts, 0)


def pick_mask(column, begin, count):
    lanes = lax.broadcasted_iota(jnp.int32, (column.shape[0], LAT), 1)
    parts = [
        jnp.where(column == lanes + at, 1.0, 0.0).astype(BF16)
        for at in range(begin, begin + count, LAT)
    ]
    return jnp.concatenate(parts, 1)


def add_mask(row, count):
    down = lax.broadcasted_iota(jnp.int32, (count, LAT), 0)
    parts = [
        jnp.where(row[q : q + 1, :] == down, 1.0, 0.0).astype(BF16) for q in range(row.shape[0])
    ]
    return jnp.concatenate(parts, 1)


def halves(v, upper):
    return jnp.concatenate([jnp.where(upper, 0.0, v), jnp.where(upper, v, 0.0)], 1).astype(BF16)


def choose(wide, upper):
    return jnp.where(upper, wide[:, LAT:], wide[:, :LAT])


def encode_pairs(send, recv, live, own):
    half = own // 2
    inner = (send >= own) & (send < 2 * own)
    upper = (send >= 2 * own) | (inner & (send >= own + half))
    at = jnp.where(inner, send - own, jnp.where(upper, send - 2 * own, send) + half)
    at = jnp.where(inner & upper, at - half, at)
    code = (at << SHIFT) + recv
    code = jnp.where(upper, code + -(1 << 31), code)
    return jnp.where(live, code, (NONE << SHIFT) + NONE)


def send_of(code):
    return (code >> SHIFT) & NONE


def recv_of(code):
    return code & NONE


def upper_of(code):
    return code < 0


def folded(index, half):
    return jnp.where(index >= half, index - half, index)


def orders_of(count):
    if count == 16:
        near, far = (4, 1), (4, 4)
        return [[near, far], [far, near]]
    if count == 64:
        a, b, c = (4, 1), (4, 4), (4, 16)
        return [[a, b, c], [b, c, a]]
    return [[(count, 1)], [(count, 1)]]


class Reducer:
    def __init__(self, count, rows):
        self.orders = orders_of(count)
        unit = 8 * count
        units = max(-(-rows // unit), 2)
        self.rows = units * unit
        near = min(max(round(units * 2 / 3), 1), units - 1) * unit
        self.parts = ((0, near), (near, self.rows - near))
        stages = len(self.orders[0])
        self.sequence = [(i, 0) for i in range(stages)] + [(i, 1) for i in reversed(range(stages))]
        self.steps = len(self.sequence) + 1

    def scratch(self):
        shapes = {"acc": pltpu.VMEM((self.rows, LAT), F32), "full": pltpu.VMEM((self.rows, LAT), F32)}
        copies = 0
        for half, order in enumerate(self.orders):
            length = self.parts[half][1]
            for stage, (k, _) in enumerate(order):
                length //= k
                shapes[f"slot{half}{stage}"] = pltpu.VMEM((max(k - 1, 1), length, LAT), F32)
                copies += k - 1
        shapes["send"] = pltpu.SemaphoreType.DMA((2 * copies,))
        shapes["recv"] = pltpu.SemaphoreType.DMA((2 * copies,))
        return shapes

    def bind(self, refs):
        self.refs = refs
        self.acc, self.full = refs["acc"], refs["full"]
        me = lax.axis_index("edge")
        self.begin = []
        self.length = []
        self.sems = {}
        used = 0
        for half, order in enumerate(self.orders):
            begin = [self.parts[half][0]]
            length = [self.parts[half][1]]
            for k, stride in order:
                length.append(length[-1] // k)
                begin.append(begin[-1] + ((me // stride) % k) * length[-1])
            self.begin.append(begin)
            self.length.append(length)
            for stage, (k, stride) in enumerate(order):
                for t in range(1, k):
                    for phase in range(2):
                        mine = (me // stride) % k
                        other = (mine + t) % k
                        self.sems[half, stage, phase, t] = (used, other, me + (other - mine) * stride)
                        used += 1

    def peers(self):
        order = self.orders[0]
        return [
            self.sems[0, stage, 0, t][2]
            for stage in range(len(order))
            for t in range(1, order[stage][0])
        ]

    def window(self, begin, length):
        return pl.ds(pl.multiple_of(begin, 8), length)

    def copies(self, half, stage, phase):
        k = self.orders[half][stage][0]
        out = []
        for t in range(1, k):
            at, other, device = self.sems[half, stage, phase, t]
            length = self.length[half][stage + 1]
            if phase == 0:
                rows = self.window(self.begin[half][stage] + other * length, length)
                source, target = self.acc.at[rows], self.refs[f"slot{half}{stage}"].at[t - 1]
            else:
                rows = self.window(self.begin[half][stage + 1], length)
                source = target = self.full.at[rows]
            out.append(
                pltpu.make_async_remote_copy(
                    src_ref=source,
                    dst_ref=target,
                    send_sem=self.refs["send"].at[at],
                    recv_sem=self.refs["recv"].at[at],
                    device_id={"edge": device},
                    device_id_type=MESH,
                )
            )
        return out

    def start(self, half, stage, phase):
        for one in self.copies(half, stage, phase):
            one.start()

    def wait(self, half, stage, phase):
        for one in self.copies(half, stage, phase):
            one.wait()
        if phase:
            return
        rows = self.window(self.begin[half][stage + 1], self.length[half][stage + 1])
        value = self.acc[rows, :]
        for t in range(1, self.orders[half][stage][0]):
            value = value + self.refs[f"slot{half}{stage}"][t - 1]
        if stage == len(self.orders[half]) - 1:
            self.full[rows, :] = value
        else:
            self.acc[rows, :] = value

    def step(self, index):
        for half in range(2):
            if index:
                self.wait(half, *self.sequence[index - 1])
            if index < len(self.sequence):
                self.start(half, *self.sequence[index])


PLACES = (
    (4, 5, 20, 21, 22, 23),
    (15, 18, 19, 16, 17, 11, 12, 13, 14),
    (6, 9, 10, 7, 8, 0, 1),
    (2, 3),
)
ROWS = (32, 8, 48, 8)
STARTS = tuple(sum(ROWS[:i]) for i in range(5))


class Refs(dict):
    def __getattr__(self, name):
        return self[name]


def train_kernel(reducers, names, mats_count, rank, *refs):
    r = Refs(zip(names, refs))
    groups = []
    for i, reducer in enumerate(reducers):
        mark = f"sum{i}_"
        reducer.bind({k[len(mark) :]: v for k, v in r.items() if k.startswith(mark)})
        groups.append(reducer)
    first, second, third, fourth = groups
    own = r.goal.shape[1]
    count = r.code.shape[0] * LAT
    lines = own // LAT
    me = lax.axis_index("edge")
    last = lax.axis_size("edge") - 1
    has_left, has_right = me > 0, me < last
    sibling = {"rep": 1 - lax.axis_index("rep")}
    barrier = pltpu.get_barrier_semaphore()
    around = [lax.rem(me + shift, last + 1) for shift in (1, last)]
    others = [{"edge": one} for one in first.peers() + around] + [sibling]
    for peer in others:
        pl.semaphore_signal(barrier, inc=1, device_id=peer, device_id_type=MESH)
    fetches = [
        pltpu.make_async_copy(source, target, r.fetch_sem.at[at])
        for at, (source, target) in enumerate(
            (
                (r.mats_in.at[pl.ds(2, 2)], r.mats.at[pl.ds(2, 2)]),
                (r.mats_in.at[pl.ds(0, 2)], r.mats.at[pl.ds(0, 2)]),
                (r.mats_in.at[pl.ds(4, mats_count - 4)], r.mats.at[pl.ds(4, mats_count - 4)]),
                (r.errors_in, r.errors),
            )
        )
    ]
    for one in fetches:
        one.start()
    mats, vecs = r.mats, r.vecs
    ones = jnp.full((LAT, LAT), 1.0 / LAT, BF16)
    middle = pl.ds(own, own)
    r["spread"] = r.hb
    r["agg_wide"] = r.recv_total

    def rows_of(which):
        base = ROWS0 + 5 * which
        return [vecs[base + i : base + i + 1, :] for i in range(5)]

    for q in range(lines):
        lanes = slice(q * LAT, (q + 1) * LAT)
        r.feat_wide[1, 0:NFEAT, lanes] = r.node_lines[pl.ds(q, NFEAT, stride=lines), :]
        r.feat_wide[1, NFEAT : NFEAT + 1, lanes] = r.types[q : q + 1, :].astype(F32)
        r.keep[:, lanes] = (1 - r.boundary[q : q + 1, :]).astype(F32)
    r.feat_wide[1, NFEAT + 1 :, :] = jnp.zeros((1, own), F32)

    @pl.when(me == 0)
    def _():
        r.feat_wide[0] = jnp.zeros(r.feat_wide.shape[1:], F32)
        r.hb[0:own, :] = jnp.zeros((own, LAT), F32)
        r.rims[0] = jnp.zeros((own, LAT), F32)

    @pl.when(me == last)
    def _():
        r.feat_wide[2] = jnp.zeros(r.feat_wide.shape[1:], F32)
        r.hb[2 * own :, :] = jnp.zeros((own, LAT), F32)
        r.rims[1] = jnp.zeros((own, LAT), F32)

    slots = lax.broadcasted_iota(jnp.int32, r.code.shape, 0) * LAT
    slots = slots + lax.broadcasted_iota(jnp.int32, r.code.shape, 1)
    send = r.senders[...] - (me - 1) * own
    r.code[...] = encode_pairs(send, r.receivers[...] - me * own, slots < r.counts[...], own)

    def neighbours(at, up, up_target, down, down_target):
        def one(index, source, target, shift):
            return pltpu.make_async_remote_copy(
                src_ref=source,
                dst_ref=target,
                send_sem=r.halo_send.at[at + index],
                recv_sem=r.halo_recv.at[at + index],
                device_id={"edge": me + shift},
                device_id_type=MESH,
            )

        return one(0, up, up_target, 1), one(1, down, down_target, -1)

    def start(pair):
        @pl.when(has_right)
        def _():
            pair[0].start()

        @pl.when(has_left)
        def _():
            pair[1].start()

    def wait(pair):
        @pl.when(has_right)
        def _():
            pair[0].wait_send()
            pair[1].wait_recv()

        @pl.when(has_left)
        def _():
            pair[1].wait_send()
            pair[0].wait_recv()

    mine = r.feat_wide.at[1]
    feats = neighbours(0, mine, r.feat_wide.at[0], mine, r.feat_wide.at[2])

    def begin():
        pl.semaphore_wait(barrier, len(others))
        start(feats)

    turns = count // BLOCK

    def steps_of(group):
        return {index: partial(group.step, index) for index in range(turns)}

    def loop(body, hooks=None):
        def step(i, unused):
            for index, hook in (hooks or {}).items():
                pl.when(i == index)(hook)

            base = pl.multiple_of(i * (BLOCK // LAT), BLOCK // LAT)
            code = r.code[pl.ds(base, BLOCK // LAT), :]
            per = count // LAT
            planes = [r.x[pl.ds(base + p * per, BLOCK // LAT), :] for p in range(EFEAT)]
            parts = []
            for at in range(0, BLOCK, SUB):
                rows = pl.ds(pl.multiple_of(i * BLOCK + at, SUB), SUB)
                cut = slice(at // LAT, (at + SUB) // LAT)
                parts.append(body(rows, code[cut], [plane[cut] for plane in planes]))
            together(parts)
            return unused

        lax.fori_loop(0, count // BLOCK, step, 0)

    def features(planes):
        lines = [
            jnp.concatenate([plane[q : q + 1, :] for q in range(plane.shape[0])], 1)
            for plane in planes
        ]
        return jnp.concatenate(lines, 0)

    kept = [[r[f"{name}{i}"] for i in range(4)] for name in ("enc", "one", "two")]

    fetches[0].wait()
    r.w[0] = stacked(0.5 * mats[2])
    r.w[1] = stacked(center(mats[3]))
    vec = rows_of(1)

    def encode(rows, code, planes):
        half = mm3(features(planes), 0.5 * vecs[LEAD:ROWS0, :], TN) + 0.5 * vec[0]
        yield
        out = yield from edge_tail(rows, half, kept[0], r.w[0], r.w[1], vec, ones)
        r.e0[rows, :] = out.astype(BF16)

    loop(encode, {turns // 2: begin})

    fetches[1].wait()
    fetches[2].wait()
    wait(feats)
    def particle_inputs():
        values = jnp.concatenate([r.feat_wide[i] for i in range(3)], 1)
        types = lax.broadcasted_iota(jnp.int32, (NTYPES, 3 * own), 0).astype(F32)
        return values[0:NFEAT], jnp.where(values[NFEAT : NFEAT + 1] == types, 1.0, 0.0)

    plain, onehot = particle_inputs()
    pre = mm3(plain, vecs[0:NFEAT, :], TN) + mm3(onehot, vecs[NFEAT:LEAD, :], TN)
    out, saved = node_tail(pre, mats[0], mats[1], rows_of(0))
    r.h0[...] = out
    for j, v in enumerate(saved):
        r.node_kept[j] = v
    latent = 0.5 * mm3(out, mats[7])
    half = own // 2

    def put_inner(v):
        r.senders_table[0:half, :] = jnp.concatenate([v[:half], v[half:]], 1).astype(BF16)

    def put_outer(left, right):
        r.senders_table[half:, :] = jnp.concatenate([left, right], 1).astype(BF16)

    put_inner(latent[own : 2 * own])
    put_outer(latent[:own], latent[2 * own :])
    shared = rows_of(2)[0]
    r.recv_table[...] = side_by_side(0.5 * (mm3(out[own : 2 * own], mats[8]) + shared))

    def put_weights(step):
        base = 6 + 9 * step
        r.w[0] = stacked(0.5 * mats[base])
        r.w[1] = stacked(0.5 * mats[base + 3])
        r.w[2] = stacked(center(mats[base + 4]))

    def near_part(column, e):
        wide = mm(pick_mask(recv_of(column), 0, own), r.recv_table[...])
        return joined(wide) + mm(twice(e), r.w[0])

    def sent_part(column, begin, end):
        wide = mm(pick_mask(send_of(column), begin, end - begin), r.senders_table[begin:end, :])
        return choose(wide, upper_of(column))

    def add_up(rows, half1, code, column, step, vec):
        out = yield from edge_tail(rows, half1, kept[1 + step], r.w[1], r.w[2], vec, ones)
        r.agg_wide[...] += mm(
            add_mask(folded(recv_of(code), half), half), halves(out, recv_of(column) >= half)
        )
        return out

    put_weights(0)
    r.agg_wide[...] = jnp.zeros_like(r.agg_wide)
    vec0 = rows_of(2)

    def first_step(rows, code, planes):
        column = columns_of(code)
        e = r.e0[rows, :]
        half1 = near_part(column, e) + sent_part(column, 0, half + own)
        yield
        out = yield from add_up(rows, half1, code, column, 0, vec0)
        r.e1[rows, :] = (e.astype(F32) + out).astype(BF16)

    loop(first_step)
    h = r.h0[middle, :]
    agg = unfold(r.agg_wide[...])
    r.agg0[...] = agg
    delta, saved = node_tail(mm3(h, mats[11]) + mm3(agg, mats[12]), mats[13], mats[14], rows_of(3))
    for j, v in enumerate(saved):
        r.step_kept[j] = v
    h = h + delta
    r.h1[...] = h
    r.hb[middle, :] = 0.5 * mm3(h, mats[16])
    mine = r.hb.at[middle]
    latents = neighbours(2, mine, r.hb.at[pl.ds(0, own)], mine, r.hb.at[pl.ds(2 * own, own)])
    start(latents)
    r.recv_table[...] = side_by_side(0.5 * (mm3(h, mats[17]) + rows_of(4)[0]))
    put_inner(r.hb[middle, :])

    put_weights(1)
    r.agg_wide[...] = jnp.zeros_like(r.agg_wide)
    vec1 = rows_of(4)

    def near_step(rows, code, planes):
        column = columns_of(code)
        half1 = near_part(column, r.e1[rows, :]) + sent_part(column, 0, half)
        yield
        kept[2][2][rows, :], kept[2][3][rows, :] = split(half1)

    def second_step(rows, code, planes):
        column = columns_of(code)
        half1 = kept[2][2][rows, :].astype(F32) + kept[2][3][rows, :].astype(F32)
        half1 = half1 + sent_part(column, half, half + own)
        yield
        yield from add_up(rows, half1, code, column, 1, vec1)

    loop(near_step)
    wait(latents)
    put_outer(r.hb[0:own, :], r.hb[2 * own :, :])
    loop(second_step)

    def slot(group, places, which):
        at = places.index(which) * LAT
        return group.acc.at[pl.ds(at, LAT)]

    def put(group, places, which, value):
        slot(group, places, which)[...] = value

    def put_rows(group, places, at, rows):
        base = len(places) * LAT + at
        for v in rows:
            group.acc[base : base + v.shape[0], :] = v
            base += v.shape[0]
        return base

    def finish_step(group, at):
        for index in range(at, group.steps):
            group.step(index)

    put1, put2, put3, _ = (partial(put, group, places) for group, places in zip(groups, PLACES))
    agg = unfold(r.agg_wide[...])
    h = r.h1[...]
    vec = rows_of(5)
    delta, saved = node_tail(mm3(h, mats[20]) + mm3(agg, mats[21]), mats[22], mats[23], vec)
    out = h + delta
    base = ROWS0 + 30
    s1, d1 = silu_half(0.5 * (mm3(out, mats[4]) + vecs[base : base + 1, :]))
    s2, d2 = silu_half(0.5 * (mm3(s1, mats[5]) + vecs[base + 1 : base + 2, :]))
    ends = vecs[base + 2 : base + 4, :]
    keep = r.keep[...]
    goal = r.goal[...]
    diff = mm3(ends, s2, NT) - goal
    kept_diff = diff * keep
    dpred = 2.0 * kept_diff
    dz2 = mm3(dpred, 0.5 * ends, TN) * d2
    dz1 = mm3(dz2, 0.5 * mats[5], NT) * d1
    d = mm3(dz1, mats[4], NT)
    dz, g_second, g_third, rows = node_tail_back(d, saved, mats[22], mats[23], vec)
    r.dh[...] = d + mm3(dz, mats[20], NT)
    r.dagg[...] = fold_table(mm3(dz, mats[21], NT))
    put1(4, mm3(out, dz1, TN))
    put1(5, mm3(s1, dz2, TN))
    put1(20, mm3(h, dz, TN))
    put1(21, mm3(agg, dz, TN))
    put1(22, g_second)
    put1(23, g_third)
    rows = rows + [row_sum(dz1), row_sum(dz2), mm3(dpred, s2)]
    rows.append(jnp.zeros((7, LAT), F32))
    velocity = r.feat_wide[1, 8:10, :]
    for v in (
        kept_diff * diff,
        velocity * keep,
        velocity * velocity * keep,
        goal * keep,
        goal * goal * keep,
        jnp.broadcast_to(keep, velocity.shape),
    ):
        part = v[:, 0:LAT]
        for j in range(LAT, own, LAT):
            part = part + v[:, j : j + LAT]
        rows.append(part)
    end = put_rows(first, PLACES[0], 0, rows)
    first.acc[end:, :] = jnp.zeros((first.rows - end, LAT), F32)

    def zero(*targets):
        for target in targets:
            target[...] = jnp.zeros_like(target)

    def put_back(step):
        base = 6 + 9 * step
        for i, w in enumerate((mats[base], 0.5 * mats[base + 3], 0.5 * center(mats[base + 4]))):
            r.w[i] = stacked(jnp.transpose(w))

    def chain(rows, column, step, gain, residual):
        recv = recv_of(column)
        d = choose(mm(pick_mask(folded(recv, half), 0, half), r.dagg[...]), recv >= half)
        if residual is not None:
            d = d + residual
        yield
        return (
            yield from edge_tail_back(
                rows, d, kept[1 + step], r.w[1], r.w[2], gain, ones, r.sums
            )
        )

    def add_sent(ref, code, begin, wide):
        ref[...] += mm(add_mask(send_of(code) - begin, ref.shape[0]), wide)

    def add_received(code, column, dz1):
        r.recv_total[...] += mm(
            add_mask(folded(recv_of(code), half), half), halves(dz1, recv_of(column) >= half)
        )

    def slots_of(group, places, step):
        base = 6 + 9 * step
        return [slot(group, places, which) for which in (base, base + 3, base + 4)]

    def add_grads(grads, e, dz1b, dz2b, dcb, s1, s2):
        grads[0][...] += mm(e, dz1b, TN)
        grads[1][...] += mm(s1, dz2b, TN)
        grads[2][...] += mm(s2, dcb, TN)

    put_back(1)
    grads1 = slots_of(second, PLACES[1], 1)
    zero(*grads1, r.sums, r.recv_total, r.inner_total, r.outer_total)
    gain1 = vec1[3]

    def chain_step(rows, code, planes):
        column = columns_of(code)
        dz1, *others = yield from chain(rows, column, 1, gain1, None)
        for ref, v in zip((kept[2][3], kept[2][2], kept[2][0], kept[2][1]), others):
            ref[rows, :] = v
        r.de[rows, :] = dz1.astype(BF16)
        add_sent(r.outer_total, code, half, halves(dz1, upper_of(column)))

    def grads_step(rows, code, planes):
        column = columns_of(code)
        dz1b = r.de[rows, :]
        s1, s2, dcb, dz2b = (ref[rows, :] for ref in kept[2])
        add_grads(grads1, r.e1[rows, :], dz1b, dz2b, dcb, s1, s2)
        dz1 = dz1b.astype(F32)
        add_received(code, column, dz1)
        add_sent(r.inner_total, code, 0, halves(dz1, upper_of(column)))
        r.de[rows, :] = mm(twice(dz1b), r.w[0]).astype(BF16)
        yield

    loop(chain_step, steps_of(first))
    r.spread[0:own, :] = r.outer_total[:, :LAT]
    r.spread[2 * own :, :] = r.outer_total[:, LAT:]
    rims = neighbours(
        4, r.spread.at[pl.ds(2 * own, own)], r.rims.at[0], r.spread.at[pl.ds(0, own)], r.rims.at[1]
    )
    start(rims)
    loop(grads_step)
    grads1[2][...] = center(grads1[2][...])
    end = put_rows(second, PLACES[1], 0, finish_sums(r.sums))
    second.acc[end:, :] = jnp.zeros((second.rows - end, LAT), F32)
    got = unfold(r.recv_total[...])
    h = r.h1[...]
    put2(17, mm3(h, got, TN))
    d = r.dh[...] + mm3(got, mats[17], NT)
    sent = unfold(r.inner_total[...])
    wait(rims)
    finish_step(first, turns)
    sent = sent + r.rims[0] + r.rims[1]
    put2(16, mm3(h, sent, TN))
    d = d + mm3(sent, mats[16], NT)
    saved = [r.step_kept[j] for j in range(4)]
    dz, g_second, g_third, rows = node_tail_back(d, saved, mats[13], mats[14], rows_of(3))
    put2(11, mm3(r.h0[middle, :], dz, TN))
    put2(12, mm3(r.agg0[...], dz, TN))
    put2(13, g_second)
    put2(14, g_third)
    put_rows(third, PLACES[2], 0, rows)
    r.dh[...] = d + mm3(dz, mats[11], NT)
    r.dagg[...] = fold_table(mm3(dz, mats[12], NT))

    put_back(0)
    grads0 = slots_of(third, PLACES[2], 0)
    zero(*grads0, r.sums, r.recv_total, r.inner_total, r.outer_total)
    gain0 = vec0[3]

    def whole_step(rows, code, planes):
        column = columns_of(code)
        de = r.de[rows, :].astype(F32)
        dz1, *others = yield from chain(rows, column, 0, gain0, de)
        dz1b = dz1.astype(BF16)
        yield
        add_grads(grads0, r.e0[rows, :], dz1b, *others)
        wide = halves(dz1, upper_of(column))
        add_sent(r.inner_total, code, 0, wide)
        add_sent(r.outer_total, code, half, wide)
        add_received(code, column, dz1)
        r.de[rows, :] = (de + mm(twice(dz1b), r.w[0])).astype(BF16)

    loop(whole_step, steps_of(second))
    grads0[2][...] = center(grads0[2][...])
    sent = unfold(r.inner_total[...])
    sent = jnp.concatenate([r.outer_total[:, :LAT], sent, r.outer_total[:, LAT:]], 0)
    got = unfold(r.recv_total[...])
    h = r.h0[...]
    put3(7, mm3(h, sent, TN))
    put3(8, mm3(h[own : 2 * own], got, TN))
    d = mm3(sent, mats[7], NT)
    inner = d[own : 2 * own] + r.dh[...] + mm3(got, mats[8], NT)
    d = jnp.concatenate([d[:own], inner, d[2 * own :]], 0)
    saved = [r.node_kept[j] for j in range(4)]
    dz, g_second, g_third, more = node_tail_back(d, saved, mats[0], mats[1], rows_of(0))
    put3(0, g_second)
    put3(1, g_third)
    plain, onehot = particle_inputs()
    rows = finish_sums(r.sums) + more + [mm3(plain, dz), mm3(onehot, dz)]
    end = put_rows(third, PLACES[2], 5, rows)
    third.acc[end:, :] = jnp.zeros((third.rows - end, LAT), F32)
    third.step(0)
    finish_step(second, turns)

    enc_grads = [slot(fourth, PLACES[3], which) for which in PLACES[3]]
    zero(*enc_grads, r.sums, r.we)
    r.w[0] = stacked(jnp.transpose(0.5 * mats[2]))
    r.w[1] = stacked(jnp.transpose(0.5 * center(mats[3])))
    gain = rows_of(1)[3]

    def encoder_back(rows, code, planes):
        d = r.de[rows, :].astype(F32)
        dz1, dz2b, dcb, s1, s2 = yield from edge_tail_back(
            rows, d, kept[0], r.w[0], r.w[1], gain, ones, r.sums
        )
        yield
        enc_grads[0][...] += mm(s1, dz2b, TN)
        enc_grads[1][...] += mm(s2, dcb, TN)
        r.we[...] += mm(features(planes).astype(BF16), dz1.astype(BF16))

    loop(encoder_back, {2: partial(third.step, 1)})
    enc_grads[1][...] = center(enc_grads[1][...])
    end = put_rows(fourth, PLACES[3], 0, finish_sums(r.sums) + [r.we[...]])
    fourth.acc[end:, :] = jnp.zeros((fourth.rows - end, LAT), F32)

    def swap(at, source, target):
        return pltpu.make_async_remote_copy(
            src_ref=source,
            dst_ref=target,
            send_sem=r.pair_send.at[at],
            recv_sem=r.pair_recv.at[at],
            device_id=sibling,
            device_id_type=MESH,
        )

    def gradient(which):
        for group, places in zip(groups, PLACES):
            if which in places:
                return group.full[places.index(which) * LAT : (places.index(which) + 1) * LAT, :]
        return None

    def ranked(which):
        return slice(which * rank, (which + 1) * rank)

    fourth.step(0)
    for group, places, at, size in zip(groups[:2], PLACES, STARTS, ROWS):
        base = len(places) * LAT
        r.small_mine[at : at + size, :] = group.full[base : base + size, :]
    small = swap(0, r.small_mine, r.small_theirs)
    small.start()
    fetches[3].wait()
    for which in range(mats_count):
        r.projected[ranked(which), :] = mm3(r.factors[which], r.errors[which], NT)
    small.wait()
    small = r.small_mine[...] + r.small_theirs[...]
    r.small[0 : STARTS[2], :] = small
    at = 16 + 10
    scale = 1.0 / jnp.sum(small[at : at + 1, :], 1, keepdims=True)

    def take(chosen):
        for which in chosen:
            part = gradient(which)
            r.total[which] = part * scale + r.errors[which]
            r.projected[ranked(which), :] += scale * mm3(r.factors[which], part, NT)

    third.step(2)
    fourth.step(1)
    take(PLACES[0])
    for index in range(3, third.steps):
        third.step(index)
        fourth.step(index - 1)
        if index == 3:
            take(PLACES[1])
    take(PLACES[2])
    finish_step(fourth, third.steps - 1)
    take(PLACES[3])
    end = mats_count * rank
    for group, places, at, size in zip(groups[2:], PLACES[2:], STARTS[2:], ROWS[2:]):
        base = len(places) * LAT
        at = end + at - STARTS[2]
        r.projected[at : at + size, :] = group.full[base : base + size, :]
    both = swap(1, r.projected, r.projected_theirs)
    both.start()
    both.wait()
    r.small[STARTS[2] :, :] = r.projected[end:, :] + r.projected_theirs[end:, :]
    both = (r.projected[0:end, :] + r.projected_theirs[0:end, :]).reshape(mats_count, rank, LAT)
    columns = [both[:, i, :] for i in range(rank)]
    for i in range(rank):
        v = columns[i]
        v = v * lax.rsqrt(jnp.sum(v * v, 1, keepdims=True) + 1e-12)
        columns[i] = v
        for j in range(i + 1, rank):
            columns[j] = columns[j] - jnp.sum(v * columns[j], 1, keepdims=True) * v
    for i in range(rank):
        r.left[:, i, :] = columns[i]
    for which in range(mats_count):
        r.right_mine[ranked(which), :] = mm3(r.left[which], r.total[which])
    both = swap(2, r.right_mine, r.right_theirs)
    both.start()
    both.wait()
    r.right[...] = (r.right_mine[...] + r.right_theirs[...]).reshape(mats_count, rank, LAT)


def train(inputs, count_edge):
    own = inputs["goal"].shape[1]
    lines = inputs["senders"].shape
    count = lines[0] * LAT
    mats_count, rank, _ = inputs["factors"].shape
    reducers = [
        Reducer(count_edge, len(places) * LAT + rows)
        for places, rows in zip(PLACES, ROWS)
    ]
    flat = lambda *dims: pltpu.VMEM(dims, F32)
    half = lambda *dims: pltpu.VMEM(dims, BF16)
    small, late = STARTS[4], STARTS[4] - STARTS[2]
    outs = {
        "total": (mats_count, LAT, LAT),
        "left": (mats_count, rank, LAT),
        "right": (mats_count, rank, LAT),
        "small": (small, LAT),
    }
    scratch = {
        "code": pltpu.VMEM(lines, jnp.int32),
        "mats": flat(*inputs["mats_in"].shape),
        "errors": flat(*inputs["errors_in"].shape),
        "keep": flat(1, own),
        "feat_wide": flat(3, NFEAT + 2, own),
        "w": half(3, 2 * LAT, LAT),
        "h0": flat(3 * own, LAT),
        "node_kept": flat(4, 3 * own, LAT),
        "step_kept": flat(4, own, LAT),
        "senders_table": half(own // 2 + own, 2 * LAT),
        "recv_table": half(own, 2 * LAT),
        "dagg": half(own // 2, 2 * LAT),
        "agg0": flat(own, LAT),
        "h1": flat(own, LAT),
        "hb": flat(3 * own, LAT),
        "dh": flat(own, LAT),
        "rims": flat(2, own, LAT),
        "recv_total": flat(own // 2, 2 * LAT),
        "inner_total": flat(own // 2, 2 * LAT),
        "outer_total": flat(own, 2 * LAT),
        "sums": flat(5, 8, LAT),
        "we": flat(EFEAT, LAT),
        "e0": half(count, LAT),
        "e1": half(count, LAT),
        "de": half(count, LAT),
        "small_mine": flat(STARTS[2], LAT),
        "small_theirs": flat(STARTS[2], LAT),
        "projected": flat(mats_count * rank + late, LAT),
        "projected_theirs": flat(mats_count * rank + late, LAT),
        "right_mine": flat(mats_count * rank, LAT),
        "right_theirs": flat(mats_count * rank, LAT),
        "fetch_sem": pltpu.SemaphoreType.DMA((4,)),
        "halo_send": pltpu.SemaphoreType.DMA((6,)),
        "halo_recv": pltpu.SemaphoreType.DMA((6,)),
        "pair_send": pltpu.SemaphoreType.DMA((3,)),
        "pair_recv": pltpu.SemaphoreType.DMA((3,)),
    }
    for name in ("enc", "one", "two"):
        for i in range(4):
            scratch[f"{name}{i}"] = half(count, LAT)
    for i, reducer in enumerate(reducers):
        for name, shape in reducer.scratch().items():
            scratch[f"sum{i}_{name}"] = shape
    vmem = pl.BlockSpec(memory_space=pltpu.VMEM)
    names = list(inputs) + list(outs) + list(scratch)
    return pl.pallas_call(
        partial(train_kernel, reducers, names, mats_count, rank),
        in_specs=[pl.BlockSpec(memory_space=pl.ANY) if name.endswith("_in") else vmem for name in inputs],
        out_specs=[vmem] * len(outs),
        out_shape=[jax.ShapeDtypeStruct(shape, F32) for shape in outs.values()],
        scratch_shapes=list(scratch.values()),
        compiler_params=pltpu.CompilerParams(
            collective_id=0, has_side_effects=True, vmem_limit_bytes=VMEM_LIMIT
        ),
    )(*inputs.values())


VMEM_LIMIT = 62 << 20


def finish_kernel(total, left, right, small, mats, momentum, vecs, vecs_momentum, *outs):
    new_mats, new_momentum, new_errors, new_factors, *outs = outs
    new_vecs, new_vecs_momentum, loss, kept_count, stats = outs
    new_factors[...] = right[...]
    for k in range(total.shape[0]):
        approx = mm3(left[k], right[k], TN)
        moved = 0.9 * momentum[k] + approx
        new_momentum[k] = moved
        new_mats[k] = mats[k] - 4.0 * moved
        new_errors[k] = total[k] - approx

    @pl.when(pl.program_id(0) == 0)
    def _():
        sums = jnp.sum(small[16:28, :], 1, keepdims=True)
        kept = sums[10:11]
        scale = 1.0 / kept
        loss[...] = sums[0:1] + sums[1:2]
        kept_count[...] = kept
        lanes = lax.broadcasted_iota(jnp.int32, stats.shape, 1)
        table = jnp.zeros(stats.shape, F32)
        for i in range(4):
            table = jnp.where(lanes == i, sums[2 + 2 * i : 4 + 2 * i], table)
        stats[...] = table * scale
        n1, e1, n0, enc, _ = STARTS
        cuts = (
            (n0 + 15, 23), (enc + 5, 3), (n0 + 10, 5), (enc, 5), (n0 + 5, 5), (n0, 5), (e1, 5),
            (n1, 9),
        )
        grads = jnp.concatenate([small[at : at + length, :] for at, length in cuts], 0)
        moved = 0.9 * vecs_momentum[...] + grads * scale
        new_vecs_momentum[...] = moved
        new_vecs[...] = vecs[...] - 4.0 * moved


def finish(total, left, right, small, mats, momentum, vecs, vecs_momentum):
    group = 6
    big = pl.BlockSpec((group, LAT, LAT), lambda i: (i, 0, 0))
    thin = pl.BlockSpec((group,) + left.shape[1:], lambda i: (i, 0, 0))
    whole = lambda shape: pl.BlockSpec(shape, lambda i: (0,) * len(shape))
    shape = lambda *dims: jax.ShapeDtypeStruct(dims, F32)
    return pl.pallas_call(
        finish_kernel,
        grid=(total.shape[0] // group,),
        in_specs=[big, thin, thin, whole(small.shape), big, big]
        + [whole(vecs.shape), whole(vecs.shape)],
        out_specs=[big] * 3 + [thin] + [whole(vecs.shape)] * 2 + [whole((1, 1))] * 2 + [whole((2, 4))],
        out_shape=[shape(*total.shape)] * 3
        + [shape(*right.shape)]
        + [shape(*vecs.shape)] * 2
        + [shape(1, 1), shape(1, 1), shape(2, 4)],
    )(total, left, right, small, mats, momentum, vecs, vecs_momentum)


def shards(
    node_feat, node_types, boundary, target, edge_feat, senders, receivers, edge_counts, mats, vecs,
    mats_momentum, vecs_momentum, factors, errors,
):
    own = node_feat.shape[1]
    count = senders.shape[1]
    lines = (count // LAT, LAT)
    few = (own // LAT, LAT)
    inputs = {
        "senders": senders.reshape(lines),
        "receivers": receivers.reshape(lines),
        "counts": edge_counts,
        "x": jnp.transpose(edge_feat, (2, 0, 1)).reshape(EFEAT * lines[0], LAT),
        "node_lines": jnp.transpose(node_feat, (2, 0, 1)).reshape(NFEAT * few[0], LAT),
        "types": node_types.reshape(few),
        "boundary": boundary.reshape(few),
        "goal": target[0].T,
        "mats_in": mats,
        "vecs": vecs,
        "factors": jnp.swapaxes(factors, 1, 2),
        "errors_in": errors[0],
    }
    total, left, right, small = train(inputs, lax.axis_size("edge"))
    new_mats, mats_mom, new_errors, new_factors, new_vecs, vecs_mom, loss, kept, stats = finish(
        total, left, right, small, mats, mats_momentum, vecs, vecs_momentum
    )
    return (
        loss.reshape(()),
        kept.reshape(()),
        stats.T,
        new_mats,
        mats_mom,
        jnp.swapaxes(new_factors, 1, 2),
        new_errors[None],
        new_vecs,
        vecs_mom,
    )


def solution(mesh):
    placed = (
        P("rep", "edge", None),
        P("rep", "edge"),
        P("rep", "edge"),
        P("rep", "edge", None),
        P("rep", "edge", None),
        P("rep", "edge"),
        P("rep", "edge"),
        P("rep", "edge"),
        P(),
        P(),
        P(),
        P(),
        P(),
        P("rep", None, None, None),
    )
    return jax.shard_map(
        shards,
        mesh=mesh,
        in_specs=placed,
        out_specs=(P(), P(), P(), P(), P(), P(), P("rep", None, None, None), P(), P()),
        check_vma=False,
    )
```

```python
from functools import partial

import jax
import jax.numpy as jnp
from jax import lax
from jax.experimental import pallas as pl
from jax.experimental.pallas import tpu as pltpu
from jax.sharding import PartitionSpec as P

NFEAT = 14
NTYPES = 9
EFEAT = 3
LEAD = NFEAT + NTYPES
ROWS0 = LEAD + EFEAT
LAT = 128
BLOCK = 2048
SUB = 512
SHIFT = 10
NONE = (1 << SHIFT) - 1
F32 = jnp.float32
BF16 = jnp.bfloat16
MESH = pl.DeviceIdType.MESH
NN = (((1,), (0,)), ((), ()))
NT = (((1,), (1,)), ((), ()))
TN = (((0,), (0,)), ((), ()))


def mm(a, b, dims=NN):
    return lax.dot_general(a, b, dims, preferred_element_type=F32)


def split(w):
    hi = w.astype(BF16)
    return hi, (w - hi.astype(F32)).astype(BF16)


def twice(a):
    return jnp.concatenate([a, a], 1)


def stacked(w):
    return jnp.concatenate(split(w), 0)


def side_by_side(v):
    return jnp.concatenate(split(v), 1)


def joined(wide):
    return wide[:, :LAT] + wide[:, LAT:]


def mm3(a, b, dims=NN):
    ah, al = split(a)
    bh, bl = split(b)
    (axis_a,), (axis_b,) = dims[0]
    if a.shape[axis_a] % LAT:
        return mm(ah, bh, dims) + (mm(ah, bl, dims) + mm(al, bh, dims))
    a = jnp.concatenate([ah, ah, al], axis_a)
    return mm(a, jnp.concatenate([bh, bl, bh], axis_b), dims)


def silu_half(half):
    rest = jnp.tanh(half)
    up = 1.0 + rest
    value = half * up
    return value, up + value * (1.0 - rest)


def mean_last(v):
    return jnp.mean(v, -1, keepdims=True)


def center(w):
    return w - mean_last(w)


def fold_rows(v):
    total = v[0:8]
    for i in range(8, v.shape[0], 8):
        total = total + v[i : i + 8]
    return total


def row_sum(v):
    return jnp.sum(fold_rows(v), 0, keepdims=True)


def fold_table(v):
    half = v.shape[0] // 2
    return jnp.concatenate([v[:half], v[half:]], 1).astype(BF16)


def unfold(v):
    return jnp.concatenate([v[:, :LAT], v[:, LAT:]], 0)


def together(parts):
    parts = list(parts)
    while parts:
        for part in list(parts):
            try:
                next(part)
            except StopIteration:
                parts.remove(part)


def node_tail(first, second, third, vec):
    b1, b2, b3, g, o = vec
    half1 = 0.5 * (first + b1)
    half2 = 0.5 * (mm3(silu_half(half1)[0], second) + b2)
    z = mm3(silu_half(half2)[0], third) + b3
    c = z - mean_last(z)
    inv = lax.rsqrt(mean_last(c * c) + 1e-05)
    xhat = c * inv
    return xhat * g + o, (half1, half2, xhat, jnp.broadcast_to(inv, xhat.shape))


def node_tail_back(d, kept, second, third, vec):
    half1, half2, xhat, inv = kept
    s1, d1 = silu_half(half1)
    s2, d2 = silu_half(half2)
    dy = d * vec[3]
    dz3 = inv * (dy - mean_last(dy) - xhat * mean_last(dy * xhat))
    dz2 = mm3(dz3, 0.5 * third, NT) * d2
    dz1 = mm3(dz2, 0.5 * second, NT) * d1
    rows = [row_sum(v) for v in (dz1, dz2, dz3, d * xhat, d)]
    return dz1, mm3(s1, dz2, TN), mm3(s2, dz3, TN), rows


def edge_tail(rows, half, kept, second, third, vec):
    _, b2, b3, g, o = vec
    kept[0][rows, :] = half.astype(BF16)
    s1 = silu_half(half)[0].astype(BF16)
    half = mm(twice(s1), second) + 0.5 * b2
    yield
    kept[1][rows, :] = half.astype(BF16)
    s2 = silu_half(half)[0].astype(BF16)
    c = mm(twice(s2), third) + center(b3)
    yield
    inv = lax.rsqrt(mean_last(c * c) + 1e-05)
    xhat = c * inv
    kept[2][rows, :] = xhat.astype(BF16)
    kept[3][rows, :] = jnp.broadcast_to(inv, c.shape).astype(BF16)
    return xhat * g + o


def edge_tail_back(rows, d, kept, second, third, g, sums):
    xhat = kept[2][rows, :].astype(F32)
    inv = kept[3][rows, :].astype(F32)
    dx = d * xhat
    dc = inv * (d * g - xhat * mean_last(dx * g))
    dcb = dc.astype(BF16)
    for at, v in ((2, dc), (3, dx), (4, d)):
        sums[at] += fold_rows(v)
    yield
    s2, d2 = silu_half(kept[1][rows, :].astype(F32))
    dz2 = mm(twice(dcb), third) * d2
    sums[1] += fold_rows(dz2)
    dz2b = dz2.astype(BF16)
    yield
    s1, d1 = silu_half(kept[0][rows, :].astype(F32))
    dz1 = mm(twice(dz2b), second) * d1
    sums[0] += fold_rows(dz1)
    return dz1, dz2b, dcb, s1.astype(BF16), s2.astype(BF16)


def finish_sums(sums):
    rows = [jnp.sum(sums[i], 0, keepdims=True) for i in range(5)]
    rows[2] = center(rows[2])
    return rows


def columns_of(code):
    parts = [
        jnp.transpose(jnp.broadcast_to(code[q : q + 1, :], (LAT, LAT))) for q in range(code.shape[0])
    ]
    return jnp.concatenate(parts, 0)


def pick_mask(column, begin, count):
    lanes = lax.broadcasted_iota(jnp.int32, (column.shape[0], LAT), 1)
    parts = [
        jnp.where(column == lanes + at, 1.0, 0.0).astype(BF16)
        for at in range(begin, begin + count, LAT)
    ]
    return jnp.concatenate(parts, 1)


def add_mask(row, count):
    down = lax.broadcasted_iota(jnp.int32, (count, LAT), 0)
    parts = [
        jnp.where(row[q : q + 1, :] == down, 1.0, 0.0).astype(BF16) for q in range(row.shape[0])
    ]
    return jnp.concatenate(parts, 1)


def halves(v, upper):
    return jnp.concatenate([jnp.where(upper, 0.0, v), jnp.where(upper, v, 0.0)], 1).astype(BF16)


def choose(wide, upper):
    return jnp.where(upper, wide[:, LAT:], wide[:, :LAT])


def encode_pairs(send, recv, live, own):
    half = own // 2
    inner = (send >= own) & (send < 2 * own)
    upper = (send >= 2 * own) | (inner & (send >= own + half))
    at = jnp.where(inner, send - own, jnp.where(upper, send - 2 * own, send) + half)
    at = jnp.where(inner & upper, at - half, at)
    code = (at << SHIFT) + recv
    code = jnp.where(upper, code + -(1 << 31), code)
    return jnp.where(live, code, (NONE << SHIFT) + NONE)


def send_of(code):
    return (code >> SHIFT) & NONE


def recv_of(code):
    return code & NONE


def upper_of(code):
    return code < 0


def folded(index, half):
    return jnp.where(index >= half, index - half, index)


def orders_of(count):
    if count == 16:
        near, far = (4, 1), (4, 4)
        return [[near, far], [far, near]]
    if count == 64:
        a, b, c = (4, 1), (4, 4), (4, 16)
        return [[a, b, c], [b, c, a]]
    return [[(count, 1)], [(count, 1)]]


class Reducer:
    def __init__(self, count, rows):
        self.orders = orders_of(count)
        unit = 8 * count
        units = max(-(-rows // unit), 2)
        self.rows = units * unit
        near = min(max(round(units * 2 / 3), 1), units - 1) * unit
        self.parts = ((0, near), (near, self.rows - near))
        stages = len(self.orders[0])
        self.sequence = [(i, 0) for i in range(stages)] + [(i, 1) for i in reversed(range(stages))]
        self.steps = len(self.sequence) + 1

    def scratch(self):
        shapes = {"acc": pltpu.VMEM((self.rows, LAT), F32), "full": pltpu.VMEM((self.rows, LAT), F32)}
        copies = 0
        for half, order in enumerate(self.orders):
            length = self.parts[half][1]
            for stage, (k, _) in enumerate(order):
                length //= k
                shapes[f"slot{half}{stage}"] = pltpu.VMEM((max(k - 1, 1), length, LAT), F32)
                copies += k - 1
        shapes["send"] = pltpu.SemaphoreType.DMA((2 * copies,))
        shapes["recv"] = pltpu.SemaphoreType.DMA((2 * copies,))
        return shapes

    def bind(self, refs):
        self.refs = refs
        self.acc, self.full = refs["acc"], refs["full"]
        me = lax.axis_index("edge")
        self.begin = []
        self.length = []
        self.sems = {}
        used = 0
        for half, order in enumerate(self.orders):
            begin = [self.parts[half][0]]
            length = [self.parts[half][1]]
            for k, stride in order:
                length.append(length[-1] // k)
                begin.append(begin[-1] + ((me // stride) % k) * length[-1])
            self.begin.append(begin)
            self.length.append(length)
            for stage, (k, stride) in enumerate(order):
                for t in range(1, k):
                    for phase in range(2):
                        mine = (me // stride) % k
                        other = (mine + t) % k
                        self.sems[half, stage, phase, t] = (used, other, me + (other - mine) * stride)
                        used += 1

    def peers(self):
        order = self.orders[0]
        return [
            self.sems[0, stage, 0, t][2]
            for stage in range(len(order))
            for t in range(1, order[stage][0])
        ]

    def window(self, begin, length):
        return pl.ds(pl.multiple_of(begin, 8), length)

    def copies(self, half, stage, phase):
        k = self.orders[half][stage][0]
        out = []
        for t in range(1, k):
            at, other, device = self.sems[half, stage, phase, t]
            length = self.length[half][stage + 1]
            if phase == 0:
                rows = self.window(self.begin[half][stage] + other * length, length)
                source, target = self.acc.at[rows], self.refs[f"slot{half}{stage}"].at[t - 1]
            else:
                rows = self.window(self.begin[half][stage + 1], length)
                source = target = self.full.at[rows]
            out.append(
                pltpu.make_async_remote_copy(
                    src_ref=source,
                    dst_ref=target,
                    send_sem=self.refs["send"].at[at],
                    recv_sem=self.refs["recv"].at[at],
                    device_id={"edge": device},
                    device_id_type=MESH,
                )
            )
        return out

    def start(self, half, stage, phase):
        for one in self.copies(half, stage, phase):
            one.start()

    def wait(self, half, stage, phase):
        for one in self.copies(half, stage, phase):
            one.wait()
        if phase:
            return
        rows = self.window(self.begin[half][stage + 1], self.length[half][stage + 1])
        value = self.acc[rows, :]
        for t in range(1, self.orders[half][stage][0]):
            value = value + self.refs[f"slot{half}{stage}"][t - 1]
        if stage == len(self.orders[half]) - 1:
            self.full[rows, :] = value
        else:
            self.acc[rows, :] = value

    def step(self, index):
        for half in range(2):
            if index:
                self.wait(half, *self.sequence[index - 1])
            if index < len(self.sequence):
                self.start(half, *self.sequence[index])


PLACES = (
    (4, 5, 20, 21, 22, 23),
    (15, 18, 19, 16, 17, 11, 12, 13, 14),
    (6, 9, 10, 7, 8, 0, 1),
    (2, 3),
)
ROWS = (32, 8, 48, 8)
STARTS = tuple(sum(ROWS[:i]) for i in range(5))


class Refs(dict):
    def __getattr__(self, name):
        return self[name]


def train_kernel(reducers, names, mats_count, rank, *refs):
    r = Refs(zip(names, refs))
    groups = []
    for i, reducer in enumerate(reducers):
        mark = f"sum{i}_"
        reducer.bind({k[len(mark) :]: v for k, v in r.items() if k.startswith(mark)})
        groups.append(reducer)
    first, second, third, fourth = groups
    own = r.goal.shape[1]
    count = r.code.shape[0] * LAT
    lines = own // LAT
    me = lax.axis_index("edge")
    last = lax.axis_size("edge") - 1
    has_left, has_right = me > 0, me < last
    sibling = {"rep": 1 - lax.axis_index("rep")}
    barrier = pltpu.get_barrier_semaphore()
    around = [lax.rem(me + shift, last + 1) for shift in (1, last)]
    others = [{"edge": one} for one in first.peers() + around] + [sibling]
    for peer in others:
        pl.semaphore_signal(barrier, inc=1, device_id=peer, device_id_type=MESH)
    fetches = [
        pltpu.make_async_copy(source, target, r.fetch_sem.at[at])
        for at, (source, target) in enumerate(
            (
                (r.mats_in.at[pl.ds(2, 2)], r.mats.at[pl.ds(2, 2)]),
                (r.mats_in.at[pl.ds(0, 2)], r.mats.at[pl.ds(0, 2)]),
                (r.mats_in.at[pl.ds(4, mats_count - 4)], r.mats.at[pl.ds(4, mats_count - 4)]),
                (r.errors_in, r.errors),
            )
        )
    ]
    for one in fetches:
        one.start()
    mats, vecs = r.mats, r.vecs
    middle = pl.ds(own, own)
    r["spread"] = r.hb
    r["agg_wide"] = r.recv_total

    def rows_of(which):
        base = ROWS0 + 5 * which
        return [vecs[base + i : base + i + 1, :] for i in range(5)]

    for q in range(lines):
        lanes = slice(q * LAT, (q + 1) * LAT)
        r.feat_wide[1, 0:NFEAT, lanes] = r.node_lines[pl.ds(q, NFEAT, stride=lines), :]
        r.feat_wide[1, NFEAT : NFEAT + 1, lanes] = r.types[q : q + 1, :].astype(F32)
        r.keep[:, lanes] = (1 - r.boundary[q : q + 1, :]).astype(F32)
    r.feat_wide[1, NFEAT + 1 :, :] = jnp.zeros((1, own), F32)

    @pl.when(me == 0)
    def _():
        r.feat_wide[0] = jnp.zeros(r.feat_wide.shape[1:], F32)
        r.hb[0:own, :] = jnp.zeros((own, LAT), F32)
        r.rims[0] = jnp.zeros((own, LAT), F32)

    @pl.when(me == last)
    def _():
        r.feat_wide[2] = jnp.zeros(r.feat_wide.shape[1:], F32)
        r.hb[2 * own :, :] = jnp.zeros((own, LAT), F32)
        r.rims[1] = jnp.zeros((own, LAT), F32)

    slots = lax.broadcasted_iota(jnp.int32, r.code.shape, 0) * LAT
    slots = slots + lax.broadcasted_iota(jnp.int32, r.code.shape, 1)
    send = r.senders[...] - (me - 1) * own
    r.code[...] = encode_pairs(send, r.receivers[...] - me * own, slots < r.counts[...], own)

    def neighbours(at, up, up_target, down, down_target):
        def one(index, source, target, shift):
            return pltpu.make_async_remote_copy(
                src_ref=source,
                dst_ref=target,
                send_sem=r.halo_send.at[at + index],
                recv_sem=r.halo_recv.at[at + index],
                device_id={"edge": me + shift},
                device_id_type=MESH,
            )

        return one(0, up, up_target, 1), one(1, down, down_target, -1)

    def start(pair):
        @pl.when(has_right)
        def _():
            pair[0].start()

        @pl.when(has_left)
        def _():
            pair[1].start()

    def wait(pair):
        @pl.when(has_right)
        def _():
            pair[0].wait_send()
            pair[1].wait_recv()

        @pl.when(has_left)
        def _():
            pair[1].wait_send()
            pair[0].wait_recv()

    mine = r.feat_wide.at[1]
    feats = neighbours(0, mine, r.feat_wide.at[0], mine, r.feat_wide.at[2])

    def begin():
        pl.semaphore_wait(barrier, len(others))
        start(feats)

    turns = count // BLOCK

    def slot_of(group, index):
        def run():
            for at in range(index, group.steps if index == 4 else index + 1):
                group.step(at)

        return run

    def loop(body, hooks=None):
        def step(i, unused):
            for index, hook in (hooks or {}).items():
                pl.when(i == index)(hook)

            base = pl.multiple_of(i * (BLOCK // LAT), BLOCK // LAT)
            code = r.code[pl.ds(base, BLOCK // LAT), :]
            per = count // LAT
            planes = [r.x[pl.ds(base + p * per, BLOCK // LAT), :] for p in range(EFEAT)]
            parts = []
            for at in range(0, BLOCK, SUB):
                rows = pl.ds(pl.multiple_of(i * BLOCK + at, SUB), SUB)
                cut = slice(at // LAT, (at + SUB) // LAT)
                parts.append(body(rows, code[cut], [plane[cut] for plane in planes]))
            together(parts)
            return unused

        lax.fori_loop(0, count // BLOCK, step, 0)

    def features(planes):
        lines = [
            jnp.concatenate([plane[q : q + 1, :] for q in range(plane.shape[0])], 1)
            for plane in planes
        ]
        return jnp.concatenate(lines, 0)

    kept = [[r[f"{name}{i}"] for i in range(4)] for name in ("enc", "one", "two")]

    fetches[0].wait()
    r.w[0] = stacked(0.5 * mats[2])
    r.w[1] = stacked(center(mats[3]))
    vec = rows_of(1)

    def encode(rows, code, planes):
        half = mm3(features(planes), 0.5 * vecs[LEAD:ROWS0, :], TN) + 0.5 * vec[0]
        yield
        out = yield from edge_tail(rows, half, kept[0], r.w[0], r.w[1], vec)
        r.e0[rows, :] = out.astype(BF16)

    loop(encode, {turns // 2: begin})

    fetches[1].wait()
    fetches[2].wait()
    wait(feats)
    def particle_inputs():
        values = jnp.concatenate([r.feat_wide[i] for i in range(3)], 1)
        types = lax.broadcasted_iota(jnp.int32, (NTYPES, 3 * own), 0).astype(F32)
        return values[0:NFEAT], jnp.where(values[NFEAT : NFEAT + 1] == types, 1.0, 0.0)

    plain, onehot = particle_inputs()
    pre = mm3(plain, vecs[0:NFEAT, :], TN) + mm3(onehot, vecs[NFEAT:LEAD, :], TN)
    out, saved = node_tail(pre, mats[0], mats[1], rows_of(0))
    r.h0[...] = out
    for j, v in enumerate(saved):
        r.node_kept[j] = v
    latent = 0.5 * mm3(out, mats[7])
    half = own // 2

    def put_inner(v):
        r.senders_table[0:half, :] = jnp.concatenate([v[:half], v[half:]], 1).astype(BF16)

    def put_outer(left, right):
        r.senders_table[half:, :] = jnp.concatenate([left, right], 1).astype(BF16)

    put_inner(latent[own : 2 * own])
    put_outer(latent[:own], latent[2 * own :])
    shared = rows_of(2)[0]
    r.recv_table[...] = side_by_side(0.5 * (mm3(out[own : 2 * own], mats[8]) + shared))

    def put_weights(step):
        base = 6 + 9 * step
        r.w[0] = stacked(0.5 * mats[base])
        r.w[1] = stacked(0.5 * mats[base + 3])
        r.w[2] = stacked(center(mats[base + 4]))

    def near_part(column, e):
        wide = mm(pick_mask(recv_of(column), 0, own), r.recv_table[...])
        return joined(wide) + mm(twice(e), r.w[0])

    def sent_part(column, begin, end):
        wide = mm(pick_mask(send_of(column), begin, end - begin), r.senders_table[begin:end, :])
        return choose(wide, upper_of(column))

    def add_up(rows, half1, code, column, step, vec):
        out = yield from edge_tail(rows, half1, kept[1 + step], r.w[1], r.w[2], vec)
        r.agg_wide[...] += mm(
            add_mask(folded(recv_of(code), half), half), halves(out, recv_of(column) >= half)
        )
        return out

    put_weights(0)
    r.agg_wide[...] = jnp.zeros_like(r.agg_wide)
    vec0 = rows_of(2)

    def first_step(rows, code, planes):
        column = columns_of(code)
        e = r.e0[rows, :]
        half1 = near_part(column, e) + sent_part(column, 0, half + own)
        yield
        out = yield from add_up(rows, half1, code, column, 0, vec0)
        r.e1[rows, :] = (e.astype(F32) + out).astype(BF16)

    loop(first_step)
    h = r.h0[middle, :]
    agg = unfold(r.agg_wide[...])
    r.agg0[...] = agg
    delta, saved = node_tail(mm3(h, mats[11]) + mm3(agg, mats[12]), mats[13], mats[14], rows_of(3))
    for j, v in enumerate(saved):
        r.step_kept[j] = v
    h = h + delta
    r.h1[...] = h
    r.hb[middle, :] = 0.5 * mm3(h, mats[16])
    mine = r.hb.at[middle]
    latents = neighbours(2, mine, r.hb.at[pl.ds(0, own)], mine, r.hb.at[pl.ds(2 * own, own)])
    start(latents)
    r.recv_table[...] = side_by_side(0.5 * (mm3(h, mats[17]) + rows_of(4)[0]))
    put_inner(r.hb[middle, :])

    put_weights(1)
    r.agg_wide[...] = jnp.zeros_like(r.agg_wide)
    vec1 = rows_of(4)

    def near_step(rows, code, planes):
        column = columns_of(code)
        half1 = near_part(column, r.e1[rows, :]) + sent_part(column, 0, half)
        yield
        kept[2][2][rows, :], kept[2][3][rows, :] = split(half1)

    def second_step(rows, code, planes):
        column = columns_of(code)
        half1 = kept[2][2][rows, :].astype(F32) + kept[2][3][rows, :].astype(F32)
        half1 = half1 + sent_part(column, half, half + own)
        yield
        yield from add_up(rows, half1, code, column, 1, vec1)

    loop(near_step)
    wait(latents)
    put_outer(r.hb[0:own, :], r.hb[2 * own :, :])
    loop(second_step)

    def slot(group, places, which):
        at = places.index(which) * LAT
        return group.acc.at[pl.ds(at, LAT)]

    def put(group, places, which, value):
        slot(group, places, which)[...] = value

    def put_rows(group, places, at, rows):
        base = len(places) * LAT + at
        for v in rows:
            group.acc[base : base + v.shape[0], :] = v
            base += v.shape[0]
        return base

    def finish_step(group, at):
        for index in range(at, group.steps):
            group.step(index)

    put1, put2, put3, _ = (partial(put, group, places) for group, places in zip(groups, PLACES))
    agg = unfold(r.agg_wide[...])
    h = r.h1[...]
    vec = rows_of(5)
    delta, saved = node_tail(mm3(h, mats[20]) + mm3(agg, mats[21]), mats[22], mats[23], vec)
    out = h + delta
    base = ROWS0 + 30
    s1, d1 = silu_half(0.5 * (mm3(out, mats[4]) + vecs[base : base + 1, :]))
    s2, d2 = silu_half(0.5 * (mm3(s1, mats[5]) + vecs[base + 1 : base + 2, :]))
    ends = vecs[base + 2 : base + 4, :]
    keep = r.keep[...]
    goal = r.goal[...]
    diff = mm3(ends, s2, NT) - goal
    kept_diff = diff * keep
    dpred = 2.0 * kept_diff
    dz2 = mm3(dpred, 0.5 * ends, TN) * d2
    dz1 = mm3(dz2, 0.5 * mats[5], NT) * d1
    d = mm3(dz1, mats[4], NT)
    dz, g_second, g_third, rows = node_tail_back(d, saved, mats[22], mats[23], vec)
    r.dh[...] = d + mm3(dz, mats[20], NT)
    r.dagg[...] = fold_table(mm3(dz, mats[21], NT))
    put1(4, mm3(out, dz1, TN))
    put1(5, mm3(s1, dz2, TN))
    put1(20, mm3(h, dz, TN))
    put1(21, mm3(agg, dz, TN))
    put1(22, g_second)
    put1(23, g_third)
    rows = rows + [row_sum(dz1), row_sum(dz2), mm3(dpred, s2)]
    rows.append(jnp.zeros((7, LAT), F32))
    velocity = r.feat_wide[1, 8:10, :]
    for v in (
        kept_diff * diff,
        velocity * keep,
        velocity * velocity * keep,
        goal * keep,
        goal * goal * keep,
        jnp.broadcast_to(keep, velocity.shape),
    ):
        part = v[:, 0:LAT]
        for j in range(LAT, own, LAT):
            part = part + v[:, j : j + LAT]
        rows.append(part)
    end = put_rows(first, PLACES[0], 0, rows)
    first.acc[end:, :] = jnp.zeros((first.rows - end, LAT), F32)

    def zero(*targets):
        for target in targets:
            target[...] = jnp.zeros_like(target)

    def put_back(step):
        base = 6 + 9 * step
        for i, w in enumerate((mats[base], 0.5 * mats[base + 3], 0.5 * center(mats[base + 4]))):
            r.w[i] = stacked(jnp.transpose(w))

    def chain(rows, column, step, gain, residual):
        recv = recv_of(column)
        d = choose(mm(pick_mask(folded(recv, half), 0, half), r.dagg[...]), recv >= half)
        if residual is not None:
            d = d + residual
        yield
        return (
            yield from edge_tail_back(
                rows, d, kept[1 + step], r.w[1], r.w[2], gain, r.sums
            )
        )

    def add_sent(ref, code, begin, wide):
        ref[...] += mm(add_mask(send_of(code) - begin, ref.shape[0]), wide)

    def add_received(code, column, dz1):
        r.recv_total[...] += mm(
            add_mask(folded(recv_of(code), half), half), halves(dz1, recv_of(column) >= half)
        )

    def slots_of(group, places, step):
        base = 6 + 9 * step
        return [slot(group, places, which) for which in (base, base + 3, base + 4)]

    def add_grads(grads, e, dz1b, dz2b, dcb, s1, s2):
        grads[0][...] += mm(e, dz1b, TN)
        grads[1][...] += mm(s1, dz2b, TN)
        grads[2][...] += mm(s2, dcb, TN)

    put_back(1)
    grads1 = slots_of(second, PLACES[1], 1)
    zero(*grads1, r.sums, r.recv_total, r.inner_total, r.outer_total)
    gain1 = vec1[3]

    def chain_step(rows, code, planes):
        column = columns_of(code)
        dz1, *others = yield from chain(rows, column, 1, gain1, None)
        for ref, v in zip((kept[2][3], kept[2][2], kept[2][0], kept[2][1]), others):
            ref[rows, :] = v
        r.de[rows, :] = dz1.astype(BF16)
        add_sent(r.outer_total, code, half, halves(dz1, upper_of(column)))

    def grads_step(rows, code, planes):
        column = columns_of(code)
        dz1b = r.de[rows, :]
        s1, s2, dcb, dz2b = (ref[rows, :] for ref in kept[2])
        add_grads(grads1, r.e1[rows, :], dz1b, dz2b, dcb, s1, s2)
        dz1 = dz1b.astype(F32)
        add_received(code, column, dz1)
        add_sent(r.inner_total, code, 0, halves(dz1, upper_of(column)))
        r.de[rows, :] = mm(twice(dz1b), r.w[0]).astype(BF16)
        yield

    loop(chain_step, {0: slot_of(first, 0), 2: slot_of(first, 1), 3: slot_of(first, 2)})
    r.spread[0:own, :] = r.outer_total[:, :LAT]
    r.spread[2 * own :, :] = r.outer_total[:, LAT:]
    rims = neighbours(
        4, r.spread.at[pl.ds(2 * own, own)], r.rims.at[0], r.spread.at[pl.ds(0, own)], r.rims.at[1]
    )
    start(rims)
    loop(grads_step)
    grads1[2][...] = center(grads1[2][...])
    end = put_rows(second, PLACES[1], 0, finish_sums(r.sums))
    second.acc[end:, :] = jnp.zeros((second.rows - end, LAT), F32)
    got = unfold(r.recv_total[...])
    h = r.h1[...]
    put2(17, mm3(h, got, TN))
    d = r.dh[...] + mm3(got, mats[17], NT)
    sent = unfold(r.inner_total[...])
    wait(rims)
    first.step(3)
    sent = sent + r.rims[0] + r.rims[1]
    put2(16, mm3(h, sent, TN))
    d = d + mm3(sent, mats[16], NT)
    saved = [r.step_kept[j] for j in range(4)]
    dz, g_second, g_third, rows = node_tail_back(d, saved, mats[13], mats[14], rows_of(3))
    put2(11, mm3(r.h0[middle, :], dz, TN))
    put2(12, mm3(r.agg0[...], dz, TN))
    put2(13, g_second)
    put2(14, g_third)
    put_rows(third, PLACES[2], 0, rows)
    r.dh[...] = d + mm3(dz, mats[11], NT)
    r.dagg[...] = fold_table(mm3(dz, mats[12], NT))

    put_back(0)
    grads0 = slots_of(third, PLACES[2], 0)
    zero(*grads0, r.sums, r.recv_total, r.inner_total, r.outer_total)
    gain0 = vec0[3]

    def whole_step(rows, code, planes):
        column = columns_of(code)
        de = r.de[rows, :].astype(F32)
        dz1, *others = yield from chain(rows, column, 0, gain0, de)
        dz1b = dz1.astype(BF16)
        yield
        add_grads(grads0, r.e0[rows, :], dz1b, *others)
        wide = halves(dz1, upper_of(column))
        add_sent(r.inner_total, code, 0, wide)
        add_sent(r.outer_total, code, half, wide)
        add_received(code, column, dz1)
        r.de[rows, :] = (de + mm(twice(dz1b), r.w[0])).astype(BF16)

    hooks = [slot_of(second, 0), slot_of(first, 4), slot_of(second, 1), slot_of(second, 2)]
    loop(whole_step, dict(enumerate(hooks)))
    second.step(3)
    grads0[2][...] = center(grads0[2][...])
    sent = unfold(r.inner_total[...])
    sent = jnp.concatenate([r.outer_total[:, :LAT], sent, r.outer_total[:, LAT:]], 0)
    got = unfold(r.recv_total[...])
    h = r.h0[...]
    put3(7, mm3(h, sent, TN))
    put3(8, mm3(h[own : 2 * own], got, TN))
    d = mm3(sent, mats[7], NT)
    inner = d[own : 2 * own] + r.dh[...] + mm3(got, mats[8], NT)
    d = jnp.concatenate([d[:own], inner, d[2 * own :]], 0)
    saved = [r.node_kept[j] for j in range(4)]
    dz, g_second, g_third, more = node_tail_back(d, saved, mats[0], mats[1], rows_of(0))
    put3(0, g_second)
    put3(1, g_third)
    plain, onehot = particle_inputs()
    rows = finish_sums(r.sums) + more + [mm3(plain, dz), mm3(onehot, dz)]
    end = put_rows(third, PLACES[2], 5, rows)
    third.acc[end:, :] = jnp.zeros((third.rows - end, LAT), F32)
    third.step(0)

    enc_grads = [slot(fourth, PLACES[3], which) for which in PLACES[3]]
    zero(*enc_grads, r.sums, r.we)
    r.w[0] = stacked(jnp.transpose(0.5 * mats[2]))
    r.w[1] = stacked(jnp.transpose(0.5 * center(mats[3])))
    gain = rows_of(1)[3]

    def encoder_back(rows, code, planes):
        d = r.de[rows, :].astype(F32)
        dz1, dz2b, dcb, s1, s2 = yield from edge_tail_back(
            rows, d, kept[0], r.w[0], r.w[1], gain, r.sums
        )
        yield
        enc_grads[0][...] += mm(s1, dz2b, TN)
        enc_grads[1][...] += mm(s2, dcb, TN)
        r.we[...] += mm(features(planes).astype(BF16), dz1.astype(BF16))

    loop(encoder_back, {2: slot_of(second, 4), 3: slot_of(third, 1)})
    enc_grads[1][...] = center(enc_grads[1][...])
    end = put_rows(fourth, PLACES[3], 0, finish_sums(r.sums) + [r.we[...]])
    fourth.acc[end:, :] = jnp.zeros((fourth.rows - end, LAT), F32)

    def swap(at, source, target):
        return pltpu.make_async_remote_copy(
            src_ref=source,
            dst_ref=target,
            send_sem=r.pair_send.at[at],
            recv_sem=r.pair_recv.at[at],
            device_id=sibling,
            device_id_type=MESH,
        )

    def gradient(which):
        for group, places in zip(groups, PLACES):
            if which in places:
                return group.full[places.index(which) * LAT : (places.index(which) + 1) * LAT, :]
        return None

    def ranked(which):
        return slice(which * rank, (which + 1) * rank)

    fourth.step(0)
    for group, places, at, size in zip(groups[:2], PLACES, STARTS, ROWS):
        base = len(places) * LAT
        r.small_mine[at : at + size, :] = group.full[base : base + size, :]
    small = swap(0, r.small_mine, r.small_theirs)
    small.start()
    fetches[3].wait()
    for which in range(mats_count):
        r.projected[ranked(which), :] = mm3(r.factors[which], r.errors[which], NT)
    small.wait()
    small = r.small_mine[...] + r.small_theirs[...]
    r.small[0 : STARTS[2], :] = small
    at = 16 + 10
    scale = 1.0 / jnp.sum(small[at : at + 1, :], 1, keepdims=True)

    def take(chosen):
        for which in chosen:
            part = gradient(which)
            r.total[which] = part * scale + r.errors[which]
            r.projected[ranked(which), :] += scale * mm3(r.factors[which], part, NT)

    third.step(2)
    fourth.step(1)
    take(PLACES[0])
    for index in range(3, third.steps):
        third.step(index)
        fourth.step(index - 1)
        if index == 3:
            take(PLACES[1])
    take(PLACES[2])
    finish_step(fourth, third.steps - 1)
    take(PLACES[3])
    end = mats_count * rank
    for group, places, at, size in zip(groups[2:], PLACES[2:], STARTS[2:], ROWS[2:]):
        base = len(places) * LAT
        at = end + at - STARTS[2]
        r.projected[at : at + size, :] = group.full[base : base + size, :]
    both = swap(1, r.projected, r.projected_theirs)
    both.start()
    both.wait()
    r.small[STARTS[2] :, :] = r.projected[end:, :] + r.projected_theirs[end:, :]
    both = (r.projected[0:end, :] + r.projected_theirs[0:end, :]).reshape(mats_count, rank, LAT)
    columns = [both[:, i, :] for i in range(rank)]
    for i in range(rank):
        v = columns[i]
        v = v * lax.rsqrt(jnp.sum(v * v, 1, keepdims=True) + 1e-12)
        columns[i] = v
        for j in range(i + 1, rank):
            columns[j] = columns[j] - jnp.sum(v * columns[j], 1, keepdims=True) * v
    for i in range(rank):
        r.left[:, i, :] = columns[i]
    for which in range(mats_count):
        r.right_mine[ranked(which), :] = mm3(r.left[which], r.total[which])
    both = swap(2, r.right_mine, r.right_theirs)
    both.start()
    both.wait()
    r.right[...] = (r.right_mine[...] + r.right_theirs[...]).reshape(mats_count, rank, LAT)


def train(inputs, count_edge):
    own = inputs["goal"].shape[1]
    lines = inputs["senders"].shape
    count = lines[0] * LAT
    mats_count, rank, _ = inputs["factors"].shape
    reducers = [
        Reducer(count_edge, len(places) * LAT + rows)
        for places, rows in zip(PLACES, ROWS)
    ]
    flat = lambda *dims: pltpu.VMEM(dims, F32)
    half = lambda *dims: pltpu.VMEM(dims, BF16)
    small, late = STARTS[4], STARTS[4] - STARTS[2]
    outs = {
        "total": (mats_count, LAT, LAT),
        "left": (mats_count, rank, LAT),
        "right": (mats_count, rank, LAT),
        "small": (small, LAT),
    }
    scratch = {
        "code": pltpu.VMEM(lines, jnp.int32),
        "mats": flat(*inputs["mats_in"].shape),
        "errors": flat(*inputs["errors_in"].shape),
        "keep": flat(1, own),
        "feat_wide": flat(3, NFEAT + 2, own),
        "w": half(3, 2 * LAT, LAT),
        "h0": flat(3 * own, LAT),
        "node_kept": flat(4, 3 * own, LAT),
        "step_kept": flat(4, own, LAT),
        "senders_table": half(own // 2 + own, 2 * LAT),
        "recv_table": half(own, 2 * LAT),
        "dagg": half(own // 2, 2 * LAT),
        "agg0": flat(own, LAT),
        "h1": flat(own, LAT),
        "hb": flat(3 * own, LAT),
        "dh": flat(own, LAT),
        "rims": flat(2, own, LAT),
        "recv_total": flat(own // 2, 2 * LAT),
        "inner_total": flat(own // 2, 2 * LAT),
        "outer_total": flat(own, 2 * LAT),
        "sums": flat(5, 8, LAT),
        "we": flat(EFEAT, LAT),
        "e0": half(count, LAT),
        "e1": half(count, LAT),
        "de": half(count, LAT),
        "small_mine": flat(STARTS[2], LAT),
        "small_theirs": flat(STARTS[2], LAT),
        "projected": flat(mats_count * rank + late, LAT),
        "projected_theirs": flat(mats_count * rank + late, LAT),
        "right_mine": flat(mats_count * rank, LAT),
        "right_theirs": flat(mats_count * rank, LAT),
        "fetch_sem": pltpu.SemaphoreType.DMA((4,)),
        "halo_send": pltpu.SemaphoreType.DMA((6,)),
        "halo_recv": pltpu.SemaphoreType.DMA((6,)),
        "pair_send": pltpu.SemaphoreType.DMA((3,)),
        "pair_recv": pltpu.SemaphoreType.DMA((3,)),
    }
    for name in ("enc", "one", "two"):
        for i in range(4):
            scratch[f"{name}{i}"] = half(count, LAT)
    for i, reducer in enumerate(reducers):
        for name, shape in reducer.scratch().items():
            scratch[f"sum{i}_{name}"] = shape
    vmem = pl.BlockSpec(memory_space=pltpu.VMEM)
    names = list(inputs) + list(outs) + list(scratch)
    return pl.pallas_call(
        partial(train_kernel, reducers, names, mats_count, rank),
        in_specs=[pl.BlockSpec(memory_space=pl.ANY) if name.endswith("_in") else vmem for name in inputs],
        out_specs=[vmem] * len(outs),
        out_shape=[jax.ShapeDtypeStruct(shape, F32) for shape in outs.values()],
        scratch_shapes=list(scratch.values()),
        compiler_params=pltpu.CompilerParams(
            collective_id=0, has_side_effects=True, vmem_limit_bytes=VMEM_LIMIT
        ),
    )(*inputs.values())


VMEM_LIMIT = 62 << 20


def finish_kernel(total, left, right, small, mats, momentum, vecs, vecs_momentum, *outs):
    new_mats, new_momentum, new_errors, new_factors, *outs = outs
    new_vecs, new_vecs_momentum, loss, kept_count, stats = outs
    new_factors[...] = right[...]
    for k in range(total.shape[0]):
        approx = mm3(left[k], right[k], TN)
        moved = 0.9 * momentum[k] + approx
        new_momentum[k] = moved
        new_mats[k] = mats[k] - 4.0 * moved
        new_errors[k] = total[k] - approx

    @pl.when(pl.program_id(0) == 0)
    def _():
        sums = jnp.sum(small[16:28, :], 1, keepdims=True)
        kept = sums[10:11]
        scale = 1.0 / kept
        loss[...] = sums[0:1] + sums[1:2]
        kept_count[...] = kept
        lanes = lax.broadcasted_iota(jnp.int32, stats.shape, 1)
        table = jnp.zeros(stats.shape, F32)
        for i in range(4):
            table = jnp.where(lanes == i, sums[2 + 2 * i : 4 + 2 * i], table)
        stats[...] = table * scale
        n1, e1, n0, enc, _ = STARTS
        cuts = (
            (n0 + 15, 23), (enc + 5, 3), (n0 + 10, 5), (enc, 5), (n0 + 5, 5), (n0, 5), (e1, 5),
            (n1, 9),
        )
        grads = jnp.concatenate([small[at : at + length, :] for at, length in cuts], 0)
        moved = 0.9 * vecs_momentum[...] + grads * scale
        new_vecs_momentum[...] = moved
        new_vecs[...] = vecs[...] - 4.0 * moved


def finish(total, left, right, small, mats, momentum, vecs, vecs_momentum):
    group = 12
    big = pl.BlockSpec((group, LAT, LAT), lambda i: (i, 0, 0))
    thin = pl.BlockSpec((group,) + left.shape[1:], lambda i: (i, 0, 0))
    whole = lambda shape: pl.BlockSpec(shape, lambda i: (0,) * len(shape))
    shape = lambda *dims: jax.ShapeDtypeStruct(dims, F32)
    return pl.pallas_call(
        finish_kernel,
        grid=(total.shape[0] // group,),
        in_specs=[big, thin, thin, whole(small.shape), big, big]
        + [whole(vecs.shape), whole(vecs.shape)],
        out_specs=[big] * 3 + [thin] + [whole(vecs.shape)] * 2 + [whole((1, 1))] * 2 + [whole((2, 4))],
        out_shape=[shape(*total.shape)] * 3
        + [shape(*right.shape)]
        + [shape(*vecs.shape)] * 2
        + [shape(1, 1), shape(1, 1), shape(2, 4)],
    )(total, left, right, small, mats, momentum, vecs, vecs_momentum)


def shards(
    node_feat, node_types, boundary, target, edge_feat, senders, receivers, edge_counts, mats, vecs,
    mats_momentum, vecs_momentum, factors, errors,
):
    own = node_feat.shape[1]
    count = senders.shape[1]
    lines = (count // LAT, LAT)
    few = (own // LAT, LAT)
    inputs = {
        "senders": senders.reshape(lines),
        "receivers": receivers.reshape(lines),
        "counts": edge_counts,
        "x": jnp.transpose(edge_feat, (2, 0, 1)).reshape(EFEAT * lines[0], LAT),
        "node_lines": jnp.transpose(node_feat, (2, 0, 1)).reshape(NFEAT * few[0], LAT),
        "types": node_types.reshape(few),
        "boundary": boundary.reshape(few),
        "goal": target[0].T,
        "mats_in": mats,
        "vecs": vecs,
        "factors": jnp.swapaxes(factors, 1, 2),
        "errors_in": errors[0],
    }
    total, left, right, small = train(inputs, lax.axis_size("edge"))
    new_mats, mats_mom, new_errors, new_factors, new_vecs, vecs_mom, loss, kept, stats = finish(
        total, left, right, small, mats, mats_momentum, vecs, vecs_momentum
    )
    return (
        loss.reshape(()),
        kept.reshape(()),
        stats.T,
        new_mats,
        mats_mom,
        jnp.swapaxes(new_factors, 1, 2),
        new_errors[None],
        new_vecs,
        vecs_mom,
    )


def solution(mesh):
    placed = (
        P("rep", "edge", None),
        P("rep", "edge"),
        P("rep", "edge"),
        P("rep", "edge", None),
        P("rep", "edge", None),
        P("rep", "edge"),
        P("rep", "edge"),
        P("rep", "edge"),
        P(),
        P(),
        P(),
        P(),
        P(),
        P("rep", None, None, None),
    )
    return jax.shard_map(
        shards,
        mesh=mesh,
        in_specs=placed,
        out_specs=(P(), P(), P(), P(), P(), P(), P("rep", None, None, None), P(), P()),
        check_vma=False,
    )
```
